32 devices in a mesh: section: 2 (over core), fsdp: 4 (over z), ctx: 4 (over y, x).
Axes of the slice: x: 2, y: 2, z: 4, core: 2. Of those that a mesh axis runs over, the one named last changes fastest.
Arguments:
- inputs: bfloat16 [2, 4, 2048, 640], P(None, 'fsdp', 'ctx'), may hold values from -6 to 6
- grad_out: bfloat16 [2, 4, 2048, 640], P(None, 'fsdp', 'ctx'), may hold values from -6 to 6
- lengths: int32 [2, 4, 3], P(None, 'fsdp'), may hold values from 1 to 1537, 2048 in all within a row
- in_gain: bfloat16 [2, 640], P('section', 'fsdp'), may hold values from 0.099609375 to 1.8984375
- query_weight: bfloat16 [2, 640, 1024], P('section', 'fsdp'), may hold values from -0.25 to 0.25
- key_weight: bfloat16 [2, 640, 256], P('section', 'fsdp'), may hold values from -0.25 to 0.25
- value_weight: bfloat16 [2, 640, 256], P('section', 'fsdp'), may hold values from -0.25 to 0.25
- query_gain: bfloat16 [2, 256], P('section', 'fsdp'), may hold values from 0.099609375 to 1.8984375
- key_gain: bfloat16 [2, 256], P('section', 'fsdp'), may hold values from 0.099609375 to 1.8984375
- out_weight: bfloat16 [2, 1024, 640], P('section', 'fsdp'), may hold values from -0.1875 to 0.1875
- attn_gain: bfloat16 [2, 640], P('section', 'fsdp'), may hold values from 0.099609375 to 1.8984375
- ffn_gain: bfloat16 [2, 640], P('section', 'fsdp'), may hold values from 0.099609375 to 1.8984375
- gate_weight: bfloat16 [2, 640, 2048], P('section', 'fsdp'), may hold values from -0.25 to 0.25
- up_weight: bfloat16 [2, 640, 2048], P('section', 'fsdp'), may hold values from -0.25 to 0.25
- down_weight: bfloat16 [2, 2048, 640], P('section', 'fsdp'), may hold values from -0.125 to 0.125
- post_gain: bfloat16 [2, 640], P('section', 'fsdp'), may hold values from 0.099609375 to 1.8984375
Outputs:
- activations: bfloat16 [2, 2, 4, 2048, 640], P('section', None, 'fsdp', 'ctx')
- input_grads: bfloat16 [2, 2, 4, 2048, 640], P('section', None, 'fsdp', 'ctx')
- in_gain_grad: float32 [2, 640], P('section', 'fsdp')
- query_weight_grad: float32 [2, 640, 1024], P('section', 'fsdp')
- key_weight_grad: float32 [2, 640, 256], P('section', 'fsdp')
- value_weight_grad: float32 [2, 640, 256], P('section', 'fsdp')
- query_gain_grad: float32 [2, 256], P('section', 'fsdp')
- key_gain_grad: float32 [2, 256], P('section', 'fsdp')
- out_weight_grad: float32 [2, 1024, 640], P('section', 'fsdp')
- attn_gain_grad: float32 [2, 640], P('section', 'fsdp')
- ffn_gain_grad: float32 [2, 640], P('section', 'fsdp')
- gate_weight_grad: float32 [2, 640, 2048], P('section', 'fsdp')
- up_weight_grad: float32 [2, 640, 2048], P('section', 'fsdp')
- down_weight_grad: float32 [2, 2048, 640], P('section', 'fsdp')
- post_gain_grad: float32 [2, 640], P('section', 'fsdp')
The draws below stay inside these ranges and needn't reach their ends.
Inputs may be any that keep to these rules, and one draw needn't show every extreme that they name: The lengths of each row sum to 2048, and the longest sequence of every row has exactly 1537 tokens.
All inputs are finite; a program needn't handle non-finite values.
Results may differ from the reference program's by a relative error of at most 0.029.
Values may be sent and summed in bfloat16 or wider, within the bound.
No kernel may reach another device: no remote copies, remote signals or barrier semaphores. Data moves between devices by JAX's collectives and lax.ppermute only.
A program may use at most 256 MiB of HBM per device.

```python
import math
import jax
import jax.numpy as jnp
import numpy as np
from jax import lax

D = 640
HD = 256
FF = 2048
WINDOW = 512
MB = 2
SEQS = 3
QD = 1024
ROWS = 4
ROW = 2048
LONGEST = 1537


def shard_levels(rng, dims, shards, low, top_value):
    gain = 1.0
    for position, parts in shards:
        steps = jax.random.uniform(jax.random.fold_in(jax.random.fold_in(rng, 6), position), (parts,), jnp.float32, low / len(shards), top_value / len(shards))
        gain = gain * jnp.repeat(jnp.exp(steps), dims[position] // parts).reshape((-1,) + (1,) * (len(dims) - 1 - position))
    return gain


def profile(count, total, most, lean):
    loads = [(1 << 20) // math.isqrt(rank ** lean) + 1 for rank in range(2, count + 1)]
    rest, given = total - most - (count - 1), [1] * (count - 1)
    while rest > 0:
        free = [i for i in range(count - 1) if given[i] < most]
        whole, budget = sum([loads[i] for i in free]), rest
        for i in free:
            extra = min(most - given[i], max(1, budget * loads[i] // whole), rest)
            given[i] = given[i] + extra
            rest = rest - extra
    return np.array([most] + given)


def uneven(rng, amount, total, most, lean):
    if amount == 2:
        one = jax.random.randint(rng, (), max(1, total - most), min(most, total - 1) + 1)
        return jnp.stack([one, total - one])
    sizes = jnp.asarray(profile(amount, total, most, lean), jnp.int32)
    couples = (amount - 1) // 2
    donor, taker = sizes[1:1 + 2 * couples:2], sizes[2:2 + 2 * couples:2]
    margin = jnp.minimum(donor - 1, most - taker)
    moved = jax.random.randint(jax.random.fold_in(rng, 1), (couples,), 0, 1 << 20) % (margin + 1)
    sizes = sizes.at[1:1 + 2 * couples:2].set(donor - moved).at[2:2 + 2 * couples:2].set(taker + moved)
    return sizes[jax.random.permutation(jax.random.fold_in(rng, 2), amount)]


def scatter_about(key, shape, scale, bound, pieces=(), dtype=jnp.bfloat16):
    values = jax.random.normal(key, shape, jnp.float32) * scale
    if len(pieces) > 0:
        values = shard_levels(key, shape, pieces, -0.22, 0.18) * values
    return jnp.clip(values, min=-bound, max=bound).astype(dtype)


def setup_inputs(seed: int = 0) -> dict:
    streams_of = jax.random.split(jax.random.key(seed), 17)
    inputs = scatter_about(streams_of[0], (MB, ROWS, ROW, D), 1.0, 6.0, ((1, 4), (2, 4)))
    grad_out = scatter_about(streams_of[1], (MB, ROWS, ROW, D), 1.0, 6.0, ((1, 4), (2, 4)))
    lengths = jax.vmap(lambda own: uneven(own, SEQS, ROW, LONGEST, 2))(jax.random.split(streams_of[2], MB * ROWS)).reshape((MB, ROWS, SEQS)).astype(jnp.int32)
    in_gain = jnp.clip(1.0 + 0.18 * jax.random.normal(streams_of[3], (2, D), jnp.float32), 0.099609375, 1.8984375).astype(jnp.bfloat16)
    query_weight = scatter_about(streams_of[4], (2, D, QD), D ** -0.5, 0.25, ((0, 2), (1, 4)))
    key_weight = scatter_about(streams_of[5], (2, D, HD), D ** -0.5, 0.25, ((0, 2), (1, 4)))
    value_weight = scatter_about(streams_of[6], (2, D, HD), D ** -0.5, 0.25, ((0, 2), (1, 4)))
    query_gain = jnp.clip(1.0 + 0.18 * jax.random.normal(streams_of[7], (2, HD), jnp.float32), 0.099609375, 1.8984375).astype(jnp.bfloat16)
    key_gain = jnp.clip(1.0 + 0.18 * jax.random.normal(streams_of[8], (2, HD), jnp.float32), 0.099609375, 1.8984375).astype(jnp.bfloat16)
    out_weight = scatter_about(streams_of[9], (2, QD, D), QD ** -0.5, 0.1875, ((0, 2), (1, 4)))
    attn_gain = jnp.clip(1.0 + 0.18 * jax.random.normal(streams_of[10], (2, D), jnp.float32), 0.099609375, 1.8984375).astype(jnp.bfloat16)
    ffn_gain = jnp.clip(1.0 + 0.18 * jax.random.normal(streams_of[11], (2, D), jnp.float32), 0.099609375, 1.8984375).astype(jnp.bfloat16)
    gate_weight = scatter_about(streams_of[12], (2, D, FF), D ** -0.5, 0.25, ((0, 2), (1, 4)))
    up_weight = scatter_about(streams_of[13], (2, D, FF), D ** -0.5, 0.25, ((0, 2), (1, 4)))
    down_weight = scatter_about(streams_of[14], (2, FF, D), FF ** -0.5, 0.125, ((0, 2), (1, 4)))
    post_gain = jnp.clip(1.0 + 0.18 * jax.random.normal(streams_of[15], (2, D), jnp.float32), 0.099609375, 1.8984375).astype(jnp.bfloat16)
    return {"inputs": inputs, "grad_out": grad_out, "lengths": lengths, "in_gain": in_gain, "query_weight": query_weight, "key_weight": key_weight, "value_weight": value_weight, "query_gain": query_gain, "key_gain": key_gain, "out_weight": out_weight, "attn_gain": attn_gain, "ffn_gain": ffn_gain, "gate_weight": gate_weight, "up_weight": up_weight, "down_weight": down_weight, "post_gain": post_gain}


EPS = 1e-06

@jax.custom_vjp
def low(v):
    return lax.optimization_barrier(v.astype(jnp.bfloat16)).astype(jnp.float32)

@jax.custom_vjp
def low_back(v):
    return v

def low_keep(v):
    return (low(v), None)

def low_pass(kept, grad):
    return (grad,)

def back_keep(v):
    return (v, None)

def back_low(kept, grad):
    return (low(grad),)
low.defvjp(low_keep, low_pass)
low_back.defvjp(back_keep, back_low)

def matmul(left, right):
    return jnp.dot(left, right, precision=lax.Precision.HIGHEST)

def rms_norm(values, gain_vec):
    return values * lax.rsqrt(lax.optimization_barrier(jnp.mean(values * values, axis=-1, keepdims=True)) + EPS) * gain_vec

def rotary(values, cos_tab, sin_tab):
    half_dim = values.shape[-1] // 2
    lower_half = values[..., :half_dim]
    upper_half = values[..., half_dim:]
    return jnp.concatenate([lower_half * cos_tab - upper_half * sin_tab, upper_half * cos_tab + lower_half * sin_tab], axis=-1)

def rope_tables(offset):
    half_dim = HD // 2
    inv_freq = 10000.0 ** (-(jnp.arange(half_dim).astype(jnp.float32) * 2.0 / HD))
    angles = offset.astype(jnp.float32)[:, None] * inv_freq[None, :]
    return (jnp.cos(angles), jnp.sin(angles))

def row_layout(seq_lens, first_place, tok_count):
    seq_ends = jnp.cumsum(seq_lens).astype(jnp.int32)
    seq_starts = (seq_ends - seq_lens).astype(jnp.int32)
    places = (first_place + jnp.arange(tok_count)).astype(jnp.int32)
    segment = lax.optimization_barrier(jnp.sum((places[:, None] >= seq_ends[None, :]).astype(jnp.int32), axis=1)).astype(jnp.int32)
    labels = jnp.arange(seq_lens.shape[0]).astype(jnp.int32)
    seg_hit = segment[:, None] == labels[None, :]
    offset = places - lax.optimization_barrier(jnp.sum(jnp.where(seg_hit, seq_starts[None, :], 0), axis=1))
    return (places, segment, offset.astype(jnp.int32))

def attend(queries, all_keys, all_vals, places, segment):
    tok_count = queries.shape[0]
    q_block = min(512, tok_count)
    score_scale = HD ** (-0.5)
    pad_keys = jnp.concatenate([jnp.zeros((WINDOW, HD), jnp.float32), all_keys], axis=0)
    pad_vals = jnp.concatenate([jnp.zeros((WINDOW, HD), jnp.float32), all_vals], axis=0)
    pad_places = jnp.concatenate([jnp.arange(WINDOW).astype(jnp.int32) - WINDOW, places])
    pad_segment = jnp.concatenate([jnp.full((WINDOW,), -1, jnp.int32), segment])

    def one_block(start):
        q_part = lax.dynamic_slice_in_dim(queries, start, q_block, 0)
        k_part = lax.dynamic_slice_in_dim(pad_keys, start, q_block + WINDOW, 0)
        v_part = lax.dynamic_slice_in_dim(pad_vals, start, q_block + WINDOW, 0)
        q_places = lax.dynamic_slice_in_dim(places, start, q_block, 0)
        k_places = lax.dynamic_slice_in_dim(pad_places, start, q_block + WINDOW, 0)
        q_segment = lax.dynamic_slice_in_dim(segment, start, q_block, 0)
        k_segment = lax.dynamic_slice_in_dim(pad_segment, start, q_block + WINDOW, 0)
        scores = low_back(jnp.einsum('qhd,kd->hqk', q_part, k_part, precision=lax.Precision.HIGHEST) * score_scale)
        distance = q_places[:, None] - k_places[None, :]
        allowed = (q_segment[:, None] == k_segment[None, :]) & (distance >= 0) & (distance < WINDOW) & (k_places[None, :] >= 0)
        masked = jnp.where(allowed[None], scores, -1e+30)
        row_max = lax.optimization_barrier(jnp.max(masked, axis=-1, keepdims=True))
        exp_scores = jnp.exp(masked - row_max)
        soft_probs = exp_scores / lax.optimization_barrier(jnp.sum(exp_scores, axis=-1, keepdims=True))
        return jnp.einsum('hqk,kd->qhd', low(soft_probs), v_part, precision=lax.Precision.HIGHEST)
    starts = (jnp.arange(tok_count // q_block) * q_block).astype(jnp.int32)
    blocks = lax.map(jax.checkpoint(one_block), starts)
    return blocks.reshape(tok_count, -1)

def layer(params, hidden, places, segment, offset):
    in_gain, query_weight, key_weight, value_weight, query_gain, key_gain, out_weight, attn_gain, ffn_gain, gate_weight, up_weight, down_weight, post_gain = params
    tok_count = hidden.shape[0]
    normed = low(rms_norm(hidden, in_gain))
    cos_tab, sin_tab = rope_tables(offset)
    query_pre = low_back(matmul(normed, query_weight)).reshape(tok_count, -1, HD)
    key_pre = low_back(matmul(normed, key_weight))
    queries = low(rotary(rms_norm(query_pre, query_gain), cos_tab[:, None], sin_tab[:, None]))
    all_keys = low(rotary(rms_norm(key_pre, key_gain), cos_tab, sin_tab))
    all_vals = low(low_back(matmul(normed, value_weight)))
    mixed_heads = low_back(low(attend(queries, all_keys, all_vals, places, segment)))
    branch = low_back(matmul(mixed_heads, out_weight))
    middle = hidden + rms_norm(branch, attn_gain)
    ffn_in = low(rms_norm(middle, ffn_gain))
    gate_pre = low_back(matmul(ffn_in, gate_weight))
    up_pre = low_back(matmul(ffn_in, up_weight))
    product = low(jax.nn.gelu(gate_pre, approximate=True) * up_pre)
    down_out = low_back(matmul(product, down_weight))
    return middle + rms_norm(down_out, post_gain)

def reference(inputs, grad_out, lengths, in_gain, query_weight, key_weight, value_weight, query_gain, key_gain, out_weight, attn_gain, ffn_gain, gate_weight, up_weight, down_weight, post_gain):
    weights = tuple((item.astype(jnp.float32) for item in (in_gain, query_weight, key_weight, value_weight, query_gain, key_gain, out_weight, attn_gain, ffn_gain, gate_weight, up_weight, down_weight, post_gain)))
    section_zero = tuple((item[0] for item in weights))
    section_one = tuple((item[1] for item in weights))
    rows_in = inputs.reshape(MB * ROWS, ROW, D).astype(jnp.float32)
    rows_cot = grad_out.reshape(MB * ROWS, ROW, D).astype(jnp.float32)
    row_lens = lengths.reshape(MB * ROWS, SEQS)
    start_sums = (tuple((jnp.zeros_like(item) for item in section_zero)), tuple((jnp.zeros_like(item) for item in section_one)))

    def per_row(carry_sums, row_item):
        hidden, row_cot, seq_lens = row_item
        places, segment, offset = row_layout(seq_lens, 0, ROW)

        def one_layer(params, values):
            return low(layer(params, values, places, segment, offset))
        middle, pull_zero = jax.vjp(one_layer, section_zero, hidden)
        final, pull_one = jax.vjp(one_layer, section_one, middle)
        grads_one, back_mid = pull_one(row_cot)
        back_mid = low(back_mid)
        grads_zero, back_in = pull_zero(back_mid)
        new_sums = (jax.tree.map(jnp.add, carry_sums[0], grads_zero), jax.tree.map(jnp.add, carry_sums[1], grads_one))
        return (new_sums, (middle, final, back_in, back_mid))
    grad_sums, (middles, finals, backs_in, backs_mid) = lax.scan(per_row, start_sums, (rows_in, rows_cot, row_lens))
    activations = jnp.stack([middles, finals]).reshape(2, MB, ROWS, ROW, D).astype(jnp.bfloat16)
    input_grads = jnp.stack([backs_in, backs_mid]).reshape(2, MB, ROWS, ROW, D).astype(jnp.bfloat16)
    stacked = [jnp.stack([grad_sums[0][index], grad_sums[1][index]]) for index in range(13)]
    return (activations, input_grads, stacked[0], stacked[1], stacked[2], stacked[3], stacked[4], stacked[5], stacked[6], stacked[7], stacked[8], stacked[9], stacked[10], stacked[11], stacked[12])
```

```python
from functools import partial

import jax
import jax.numpy as jnp
from jax import lax
from jax.experimental import pallas as pl
from jax.experimental.pallas import tpu as pltpu
from jax.sharding import PartitionSpec as P

HD = 256
WINDOW = 512
EPS = 1e-06
LANES = 128
PARTS = 4
GAIN_ROWS = 16
QB = 128
F32 = jnp.float32
B16 = jnp.bfloat16
VMEM_LIMIT = 56 * 1024 * 1024
AXES = ("section", "fsdp", "ctx")


def rope_tables(offset):
    half_dim = HD // 2
    inv_freq = 10000.0 ** (-(jnp.arange(half_dim).astype(F32) * 2.0 / HD))
    angles = offset.astype(F32)[:, None] * inv_freq[None, :]
    return (jnp.cos(angles), jnp.sin(angles))


def layout_for(seq_lens, first_place, tok_count):
    seq_ends = jnp.cumsum(seq_lens)
    seq_starts = seq_ends - seq_lens
    places = first_place + jnp.arange(tok_count)
    segment = jnp.sum((places[:, None] >= seq_ends[None, :]).astype(jnp.int32), axis=1)
    labels = jnp.arange(seq_lens.shape[0])
    seg_hit = segment[:, None] == labels[None, :]
    start = jnp.sum(jnp.where(seg_hit, seq_starts[None, :], 0), axis=1)
    offset = places - start
    low = jnp.maximum(start, places - (WINDOW - 1)) - first_place + WINDOW
    return offset, low.astype(jnp.int32)


def dot(a, b):
    return lax.dot_general(a, b, (((1,), (0,)), ((), ())), preferred_element_type=F32)


def dot_nt(a, b):
    return lax.dot_general(a, b, (((1,), (1,)), ((), ())), preferred_element_type=F32)


def dot_tn(a, b):
    return lax.dot_general(a, b, (((0,), (0,)), ((), ())), preferred_element_type=F32)


def inv_rms(v):
    return lax.rsqrt(jnp.mean(v * v, axis=-1, keepdims=True) + EPS)


def rms_back(v, gain, grad):
    r = inv_rms(v)
    gg = grad * gain
    normed = v * r
    back = r * (gg - normed * jnp.mean(normed * gg, axis=-1, keepdims=True))
    return back, jnp.sum(grad * normed, axis=0, keepdims=True)


def rope(v, cos, sin):
    u, w = v[:, : HD // 2], v[:, HD // 2 :]
    return jnp.concatenate([u * cos - w * sin, w * cos + u * sin], axis=-1)


def rope_back(g, cos, sin):
    a, b = g[:, : HD // 2], g[:, HD // 2 :]
    return jnp.concatenate([a * cos + b * sin, b * cos - a * sin], axis=-1)


GELU_C = 0.7978845608028654
GELU_A = 0.044715


def gelu_parts(g):
    g2 = g * g
    t = jnp.tanh(GELU_C * g * (1.0 + GELU_A * g2))
    half = 0.5 * (1.0 + t)
    value = g * half
    slope = half + 0.5 * g * (1.0 - t * t) * (GELU_C * (1.0 + 3.0 * GELU_A * g2))
    return value, slope


def params(**kw):
    return pltpu.CompilerParams(vmem_limit_bytes=VMEM_LIMIT, **kw)


def cost(flops, nbytes):
    return pl.CostEstimate(flops=int(flops), bytes_accessed=int(nbytes), transcendentals=0)


def whole(shape):
    n = len(shape)
    return pl.BlockSpec(shape, lambda *i: (0,) * n)


def sds(shape, dtype):
    return jax.ShapeDtypeStruct(shape, dtype)


def kv_kernel(x_ref, gd_ref, gh_ref, cos_ref, sin_ref, w_ref, a_ref, pre_ref, kv_ref):
    x = x_ref[...].astype(F32)
    a = (x * inv_rms(x) * gd_ref[0:1, :]).astype(B16)
    a_ref[...] = a
    both = dot(a, w_ref[...])
    pre = both[:, :HD]
    pre_ref[...] = pre.astype(B16)
    keys = rope(pre * inv_rms(pre) * gh_ref[1:2, :], cos_ref[...], sin_ref[...])
    kv_ref[:, :HD] = keys.astype(B16)
    kv_ref[:, HD:] = both[:, HD:].astype(B16)


def kv_call(x, gd, gh, cos, sin, w_qkv):
    tok, width = x.shape
    q_width = w_qkv.shape[1] - 2 * HD
    return pl.pallas_call(
        kv_kernel,
        grid=(1,),
        in_specs=[
            whole(x.shape),
            whole(gd.shape),
            whole(gh.shape),
            whole(cos.shape),
            whole(sin.shape),
            pl.BlockSpec((width, 2 * HD), lambda j: (0, q_width // (2 * HD))),
        ],
        out_specs=[whole((tok, width)), whole((tok, HD)), whole((tok, 2 * HD))],
        out_shape=[sds((tok, width), B16), sds((tok, HD), B16), sds((tok, 2 * HD), B16)],
        compiler_params=params(),
        cost_estimate=cost(4 * tok * width * HD, 4e6),
        name="keys_values",
    )(x, gd, gh, cos, sin, w_qkv)


def q_kernel(a_ref, gh_ref, cos_ref, sin_ref, w_ref, pre_ref, q_ref):
    pre = dot(a_ref[...], w_ref[...])
    pre_ref[...] = pre.astype(B16)
    q_ref[...] = rope(pre * inv_rms(pre) * gh_ref[0:1, :], cos_ref[...], sin_ref[...]).astype(B16)


def q_call(a, gh, cos, sin, w_qkv):
    tok, width = a.shape
    q_width = w_qkv.shape[1] - 2 * HD
    block = pl.BlockSpec((tok, HD), lambda j: (0, j))
    return pl.pallas_call(
        q_kernel,
        grid=(q_width // HD,),
        in_specs=[
            whole(a.shape),
            whole(gh.shape),
            whole(cos.shape),
            whole(sin.shape),
            pl.BlockSpec((width, HD), lambda j: (0, j)),
        ],
        out_specs=[block, block],
        out_shape=[sds((tok, q_width), B16), sds((tok, q_width), B16)],
        compiler_params=params(),
        cost_estimate=cost(2 * tok * width * q_width, 5e6),
        name="queries",
    )(a, gh, cos, sin, w_qkv)


SCORE_SCALE = HD ** (-0.5)


def attn_kernel(q_ref, far_ref, near_ref, low_ref, o_ref, kv_scr):
    b = pl.program_id(0)

    @pl.when(b == 0)
    def _():
        kv_scr[:WINDOW, :] = far_ref[...]
        kv_scr[WINDOW:, :] = near_ref[...]

    span = WINDOW + QB
    first = pl.multiple_of(b * QB, QB)
    keys = kv_scr[pl.ds(first, span), :HD]
    vals = kv_scr[pl.ds(first, span), HD:]
    col = lax.broadcasted_iota(jnp.int32, (QB, span), 1)
    row = lax.broadcasted_iota(jnp.int32, (QB, span), 0)
    allowed = (col >= low_ref[...] - b * QB) & (col <= row + WINDOW)
    for h in range(q_ref.shape[1] // HD):
        scores = dot_nt(q_ref[:, h * HD : (h + 1) * HD], keys) * SCORE_SCALE
        e = jnp.where(allowed, jnp.exp(scores), 0.0)
        total = jnp.sum(e, axis=1, keepdims=True)
        o_ref[:, h * HD : (h + 1) * HD] = (dot(e.astype(B16), vals) / total).astype(B16)


def attn_call(q, far, near, low):
    tok, q_width = q.shape
    return pl.pallas_call(
        attn_kernel,
        grid=(tok // QB,),
        in_specs=[
            pl.BlockSpec((QB, q_width), lambda b: (b, 0)),
            whole(far.shape),
            whole(near.shape),
            pl.BlockSpec((QB, 1), lambda b: (b, 0)),
        ],
        out_specs=pl.BlockSpec((QB, q_width), lambda b: (b, 0)),
        out_shape=sds((tok, q_width), B16),
        scratch_shapes=[pltpu.VMEM((WINDOW + tok, 2 * HD), B16)],
        compiler_params=params(),
        cost_estimate=cost(4 * tok * q_width * (WINDOW + QB), 3e6),
        name="attend",
    )(q, far, near, low)


FC = 512


def ffn_kernel(
    o_ref, x_ref, gd_ref, wo_ref, wg_ref, wu_ref, wd_ref,
    y_ref, h_ref, g_ref, u_ref, z_ref, out_ref, b_scr,
):
    j = pl.program_id(0)

    @pl.when(j == 0)
    def _():
        y = dot(o_ref[...], wo_ref[...])
        y_ref[...] = y
        h = x_ref[...].astype(F32) + y * inv_rms(y) * gd_ref[1:2, :]
        h_ref[...] = h
        b_scr[...] = (h * inv_rms(h) * gd_ref[2:3, :]).astype(B16)

    b = b_scr[...]
    g = dot(b, wg_ref[...])
    u = dot(b, wu_ref[...])
    g_ref[...] = g.astype(B16)
    u_ref[...] = u.astype(B16)
    value = g * 0.5 * (1.0 + jnp.tanh(GELU_C * g * (1.0 + GELU_A * g * g)))
    z = dot((value * u).astype(B16), wd_ref[...])

    @pl.when(j == 0)
    def _():
        z_ref[...] = z

    @pl.when(j > 0)
    def _():
        z_ref[...] += z

    @pl.when(j == pl.num_programs(0) - 1)
    def _():
        zz = z_ref[...]
        out_ref[...] = (h_ref[...] + zz * inv_rms(zz) * gd_ref[3:4, :]).astype(B16)


def ffn_call(o, x, gd, w_out, w_gate, w_up, w_down):
    tok, width = x.shape
    ff = w_gate.shape[1]
    cols = pl.BlockSpec((tok, FC), lambda j: (0, j))
    tw = whole((tok, width))
    return pl.pallas_call(
        ffn_kernel,
        grid=(ff // FC,),
        in_specs=[
            whole(o.shape),
            tw,
            whole(gd.shape),
            whole(w_out.shape),
            pl.BlockSpec((width, FC), lambda j: (0, j)),
            pl.BlockSpec((width, FC), lambda j: (0, j)),
            pl.BlockSpec((FC, width), lambda j: (j, 0)),
        ],
        out_specs=[tw, tw, cols, cols, tw, tw],
        out_shape=[
            sds((tok, width), F32),
            sds((tok, width), F32),
            sds((tok, ff), B16),
            sds((tok, ff), B16),
            sds((tok, width), F32),
            sds((tok, width), B16),
        ],
        scratch_shapes=[pltpu.VMEM((tok, width), B16)],
        compiler_params=params(),
        cost_estimate=cost(2 * tok * width * (o.shape[1] + 3 * ff), 22e6),
        name="feed_forward",
    )(o, x, gd, w_out, w_gate, w_up, w_down)


def ffn_back_kernel(
    c_ref, z_ref, h_ref, y_ref, o_ref, gd_ref, g_ref, u_ref, wo_ref, wg_ref, wu_ref, wd_ref,
    pack_ref, dh_ref, do_ref, gg_ref, dz_scr, bt_scr, db_scr,
):
    j = pl.program_id(0)
    tok, width = c_ref.shape
    part = width // PARTS
    n_gate = PARTS * part
    n_down = (width // LANES) * (FC // PARTS)
    out_rows = o_ref.shape[1] // (PARTS * PARTS)

    @pl.when(j == 0)
    def _():
        dz, post_grad = rms_back(z_ref[...], gd_ref[3:4, :], c_ref[...].astype(F32))
        dz_scr[...] = dz.astype(B16)
        gg_ref[...] = jnp.zeros(gg_ref.shape, F32)
        gg_ref[3:4, :] = post_grad
        h = h_ref[...]
        bt_scr[...] = (h * inv_rms(h) * gd_ref[2:3, :]).T.astype(B16)
        db_scr[...] = jnp.zeros(db_scr.shape, F32)

    dz = dz_scr[...]
    df = dot_nt(dz, wd_ref[...])
    value, slope = gelu_parts(g_ref[...].astype(F32))
    u = u_ref[...].astype(F32)
    f = (value * u).astype(B16)
    du = (df * value).astype(B16)
    dg = (df * u * slope).astype(B16)
    db_scr[...] += dot_nt(dg, wg_ref[...]) + dot_nt(du, wu_ref[...])
    bt = bt_scr[...]
    for first, term in ((0, dg), (n_gate, du)):
        grad = dot(bt, term).astype(B16)
        for p in range(PARTS):
            for t in range(FC // LANES):
                pack_ref[j, p, pl.ds(first + t * part, part), :] = grad[
                    p * part : (p + 1) * part, t * LANES : (t + 1) * LANES
                ]
    grad = dot_tn(f, dz).astype(B16)
    rows = FC // PARTS
    for p in range(PARTS):
        for t in range(width // LANES):
            pack_ref[p, j, pl.ds(2 * n_gate + t * rows, rows), :] = grad[
                p * rows : (p + 1) * rows, t * LANES : (t + 1) * LANES
            ]

    @pl.when(j == pl.num_programs(0) - 1)
    def _():
        add, ffn_grad = rms_back(h_ref[...], gd_ref[2:3, :], db_scr[...])
        dh = c_ref[...].astype(F32) + add
        dh_ref[...] = dh
        dy32, attn_grad = rms_back(y_ref[...], gd_ref[1:2, :], dh)
        dy = dy32.astype(B16)
        gg_ref[1:2, :] = attn_grad
        gg_ref[2:3, :] = ffn_grad
        do_ref[...] = dot_nt(dy, wo_ref[...]).astype(B16)
        og = dot_tn(o_ref[...], dy).astype(B16)
        for f_part in range(PARTS):
            for p in range(PARTS):
                at = (f_part * PARTS + p) * out_rows
                for t in range(width // LANES):
                    pack_ref[p, f_part, pl.ds(2 * n_gate + n_down + t * out_rows, out_rows), :] = (
                        og[at : at + out_rows, t * LANES : (t + 1) * LANES]
                    )


def pack_rows(width, ff, q_width):
    gate = width // PARTS * (ff // PARTS // LANES)
    down = ff // (PARTS * PARTS) * (width // LANES)
    out = q_width // (PARTS * PARTS) * (width // LANES)
    return gate, down, out


def ffn_back_call(c, z, h, y, o, gd, g, u, w_out, w_gate, w_up, w_down):
    tok, width = c.shape
    ff = w_gate.shape[1]
    q_width = o.shape[1]
    gate, down, out = pack_rows(width, ff, q_width)
    pack_shape = (PARTS, PARTS, 2 * gate + down + out, LANES)
    cols = pl.BlockSpec((tok, FC), lambda j: (0, j))
    tw = whole((tok, width))
    return pl.pallas_call(
        ffn_back_kernel,
        grid=(ff // FC,),
        in_specs=[
            tw,
            tw,
            tw,
            tw,
            whole(o.shape),
            whole(gd.shape),
            cols,
            cols,
            whole(w_out.shape),
            pl.BlockSpec((width, FC), lambda j: (0, j)),
            pl.BlockSpec((width, FC), lambda j: (0, j)),
            pl.BlockSpec((FC, width), lambda j: (j, 0)),
        ],
        out_specs=[whole(pack_shape), tw, whole(o.shape), whole(gd.shape)],
        out_shape=[
            sds(pack_shape, B16),
            sds((tok, width), F32),
            sds(o.shape, B16),
            sds(gd.shape, F32),
        ],
        scratch_shapes=[
            pltpu.VMEM((tok, width), B16),
            pltpu.VMEM((width, tok), B16),
            pltpu.VMEM((tok, width), F32),
        ],
        compiler_params=params(),
        cost_estimate=cost(4 * tok * width * (q_width + 3 * ff), 35e6),
        name="feed_forward_back",
    )(c, z, h, y, o, gd, g, u, w_out, w_gate, w_up, w_down)


def attn_back_kernel(
    q_ref, do_ref, qpre_ref, far_ref, near_ref, low_ref, gh_ref, cos_ref, sin_ref,
    dq_ref, dfar_ref, dnear_ref, gg_ref, kv_scr, dkv_scr,
):
    b = pl.program_id(0)

    @pl.when(b == 0)
    def _():
        kv_scr[:WINDOW, :] = far_ref[...]
        kv_scr[WINDOW:, :] = near_ref[...]
        dkv_scr[...] = jnp.zeros(dkv_scr.shape, F32)
        gg_ref[...] = jnp.zeros(gg_ref.shape, F32)

    span = WINDOW + QB
    first = pl.multiple_of(b * QB, QB)
    keys = kv_scr[pl.ds(first, span), :HD]
    vals = kv_scr[pl.ds(first, span), HD:]
    col = lax.broadcasted_iota(jnp.int32, (span, QB), 0)
    row = lax.broadcasted_iota(jnp.int32, (span, QB), 1)
    allowed = (col >= low_ref[...] - b * QB) & (col <= row + WINDOW)
    cos, sin = cos_ref[...], sin_ref[...]
    dkeys = jnp.zeros((span, HD), F32)
    dvals = jnp.zeros((span, HD), F32)
    gain_grad = jnp.zeros((1, HD), F32)
    for h in range(q_ref.shape[1] // HD):
        at = slice(h * HD, (h + 1) * HD)
        q = q_ref[:, at]
        do = do_ref[:, at]
        scores = dot_nt(keys, q) * SCORE_SCALE
        e = jnp.where(allowed, jnp.exp(scores), 0.0)
        p = e * (1.0 / jnp.sum(e, axis=0, keepdims=True))
        dp = dot_nt(vals, do)
        inner = jnp.sum(p * dp, axis=0, keepdims=True)
        ds = (p * (dp - inner)).astype(B16)
        dvals += dot(p.astype(B16), do)
        dkeys += dot(ds, q)
        dq = dot_tn(ds, keys) * SCORE_SCALE
        dq0, gain = rms_back(qpre_ref[:, at].astype(F32), gh_ref[0:1, :], rope_back(dq, cos, sin))
        gain_grad += gain
        dq_ref[:, at] = dq0.astype(B16)
    dkv_scr[pl.ds(first, span), :HD] += dkeys * SCORE_SCALE
    dkv_scr[pl.ds(first, span), HD:] += dvals
    gg_ref[0:1, :] += gain_grad

    @pl.when(b == pl.num_programs(0) - 1)
    def _():
        dfar_ref[...] = dkv_scr[:WINDOW, :].astype(B16)
        dnear_ref[...] = dkv_scr[WINDOW:, :]


def attn_back_call(q, do, qpre, far, near, low_row, gh, cos, sin):
    tok, q_width = q.shape
    block = pl.BlockSpec((QB, q_width), lambda b: (b, 0))
    table = pl.BlockSpec((QB, HD // 2), lambda b: (b, 0))
    return pl.pallas_call(
        attn_back_kernel,
        grid=(tok // QB,),
        in_specs=[
            block,
            block,
            block,
            whole(far.shape),
            whole(near.shape),
            pl.BlockSpec((1, QB), lambda b: (0, b)),
            whole(gh.shape),
            table,
            table,
        ],
        out_specs=[block, whole(far.shape), whole(near.shape), whole(gh.shape)],
        out_shape=[
            sds(q.shape, B16),
            sds(far.shape, B16),
            sds(near.shape, F32),
            sds(gh.shape, F32),
        ],
        scratch_shapes=[
            pltpu.VMEM((WINDOW + tok, 2 * HD), B16),
            pltpu.VMEM((WINDOW + tok, 2 * HD), F32),
        ],
        compiler_params=params(),
        cost_estimate=cost(10 * tok * q_width * (WINDOW + QB), 8e6),
        name="attend_back",
    )(q, do, qpre, far, near, low_row, gh, cos, sin)


def q_back_kernel(a_ref, dq_ref, w_ref, wq_grad_ref, da_ref):
    dq = dq_ref[...]
    wq_grad_ref[...] = dot_tn(a_ref[...], dq).astype(B16)
    da_ref[...] = dot_nt(dq, w_ref[...])


def q_back_call(a, dq, w_qkv):
    tok, width = a.shape
    q_width = dq.shape[1]
    return pl.pallas_call(
        q_back_kernel,
        grid=(1,),
        in_specs=[whole(a.shape), whole(dq.shape), whole((width, q_width))],
        out_specs=[whole((width, q_width)), whole((tok, width))],
        out_shape=[sds((width, q_width), B16), sds((tok, width), F32)],
        compiler_params=params(),
        cost_estimate=cost(4 * tok * width * q_width, 6e6),
        name="queries_back",
    )(a, dq, w_qkv)


def kv_back_kernel(
    a_ref, x_ref, dh_ref, da_ref, dnear_ref, dback_ref, kpre_ref, gd_ref, gh_ref,
    cos_ref, sin_ref, w_ref, wq_ref, pack_ref, dx_ref, gd_grad_ref, gh_grad_ref,
):
    width = x_ref.shape[1]
    part = width // PARTS
    dkv = dnear_ref[...]
    tail = dback_ref[...].astype(F32)
    dkv = dkv + tail
    dk0, k_grad = rms_back(
        kpre_ref[...].astype(F32),
        gh_ref[1:2, :],
        rope_back(dkv[:, :HD], cos_ref[...], sin_ref[...]),
    )
    both = jnp.concatenate([dk0.astype(B16), dkv[:, HD:].astype(B16)], axis=1)
    kv_grad = dot_tn(a_ref[...], both).astype(B16)
    da = da_ref[...] + dot_nt(both, w_ref[...])
    add, in_grad = rms_back(x_ref[...].astype(F32), gd_ref[0:1, :], da)
    dx_ref[...] = (dh_ref[...] + add).astype(B16)
    gd_grad_ref[...] = jnp.zeros(gd_grad_ref.shape, F32)
    gd_grad_ref[0:1, :] = in_grad
    gh_grad_ref[...] = jnp.zeros(gh_grad_ref.shape, F32)
    gh_grad_ref[1:2, :] = k_grad
    q_tiles = wq_ref.shape[1] // LANES
    tiles = q_tiles + 2 * HD // LANES
    each = tiles // PARTS
    for t in range(tiles):
        c_part, slot = t // each, t % each
        for p in range(PARTS):
            rows = slice(p * part, (p + 1) * part)
            if t < q_tiles:
                piece = wq_ref[rows, t * LANES : (t + 1) * LANES]
            else:
                piece = kv_grad[rows, (t - q_tiles) * LANES : (t - q_tiles + 1) * LANES]
            pack_ref[c_part, p, slot * part : (slot + 1) * part, :] = piece


def kv_back_call(a, x, dh, da, dnear, dback, kpre, gd, gh, cos, sin, w_qkv, wq_grad):
    tok, width = a.shape
    q_width = wq_grad.shape[1]
    part = width // PARTS
    pack_shape = (PARTS, PARTS, part * ((q_width + 2 * HD) // LANES // PARTS), LANES)
    tw = whole((tok, width))
    return pl.pallas_call(
        kv_back_kernel,
        grid=(1,),
        in_specs=[
            tw,
            tw,
            tw,
            tw,
            whole(dnear.shape),
            whole(dback.shape),
            whole(kpre.shape),
            whole(gd.shape),
            whole(gh.shape),
            whole(cos.shape),
            whole(sin.shape),
            pl.BlockSpec((width, 2 * HD), lambda j: (0, q_width // (2 * HD))),
            whole(wq_grad.shape),
        ],
        out_specs=[whole(pack_shape), tw, whole(gd.shape), whole(gh.shape)],
        out_shape=[
            sds(pack_shape, B16),
            sds((tok, width), B16),
            sds(gd.shape, F32),
            sds(gh.shape, F32),
        ],
        compiler_params=params(),
        cost_estimate=cost(8 * tok * width * HD, 10e6),
        name="keys_values_back",
    )(a, x, dh, da, dnear, dback, kpre, gd, gh, cos, sin, w_qkv, wq_grad)


def pack_own(qkv, gains, gate, up, down, out):
    def by_cols(w):
        rows, cols = w.shape
        tiles = cols // (PARTS * LANES)
        return (
            w.reshape(rows, PARTS, tiles, LANES)
            .transpose(1, 2, 0, 3)
            .reshape(PARTS, tiles * rows, LANES)
        )

    def by_rows(w):
        rows, cols = w.shape
        n = rows // PARTS
        return (
            w.reshape(PARTS, n, cols // LANES, LANES)
            .transpose(0, 2, 1, 3)
            .reshape(PARTS, cols // LANES * n, LANES)
        )

    gain_rows = jnp.broadcast_to(gains[None], (PARTS,) + gains.shape)
    return (
        jnp.concatenate([by_cols(qkv), gain_rows], axis=1),
        jnp.concatenate([by_cols(gate), by_cols(up), by_rows(down), by_rows(out)], axis=1),
    )


def pick(spot_ref, j):
    return lax.rem(spot_ref[0] - j + PARTS, PARTS)


def piece_specs(rows):
    def own_map(j, spot):
        return (jnp.where(spot[2] == 1, pick(spot, j), 0), 0, 0, 0)

    def other_map(j, spot):
        return (jnp.where(spot[2] == 1, 0, pick(spot, j)), 0, 0, 0)

    shape = (1, PARTS, rows, LANES)
    return [pl.BlockSpec(shape, own_map), pl.BlockSpec(shape, other_map)]


def unpack_qkv_kernel(spot, own_ref, other_ref, w_ref, gain_ref):
    part = w_ref.shape[0] // PARTS

    def take(ref):
        for p in range(PARTS):
            d = lax.rem(spot[1] - p + PARTS, PARTS)
            for t in range(w_ref.shape[1] // LANES):
                w_ref[p * part : (p + 1) * part, t * LANES : (t + 1) * LANES] = ref[
                    0, d, t * part : (t + 1) * part, :
                ]
            gain_ref[p] = ref[0, d, ref.shape[2] - GAIN_ROWS :, :]

    pl.when(spot[2] == 1)(lambda: take(own_ref))
    pl.when(spot[2] == 0)(lambda: take(other_ref))


def unpack_qkv(spot, own, other, width, cols):
    return pl.pallas_call(
        unpack_qkv_kernel,
        grid_spec=pltpu.PrefetchScalarGridSpec(
            num_scalar_prefetch=1,
            grid=(PARTS,),
            in_specs=piece_specs(own.shape[2]),
            out_specs=[
                pl.BlockSpec((width, cols // PARTS), lambda j, spot: (0, j)),
                pl.BlockSpec((PARTS, GAIN_ROWS, LANES), lambda j, spot: (0, 0, 0)),
            ],
        ),
        out_shape=[sds((width, cols), B16), sds((PARTS, GAIN_ROWS, LANES), B16)],
        compiler_params=params(),
        cost_estimate=cost(0, 6e6),
        name="place_qkv",
    )(spot, own, other)


def unpack_ffn_kernel(spot, own_ref, other_ref, gate_ref, up_ref, down_ref, out_ref):
    width, cols = gate_ref.shape
    part = width // PARTS
    tiles = cols // LANES
    n_gate = tiles * part

    def take(ref):
        for p in range(PARTS):
            d = lax.rem(spot[1] - p + PARTS, PARTS)
            for n, w_ref in enumerate((gate_ref, up_ref)):
                for t in range(tiles):
                    at = n * n_gate + t * part
                    w_ref[p * part : (p + 1) * part, t * LANES : (t + 1) * LANES] = ref[
                        0, d, at : at + part, :
                    ]
            at = 2 * n_gate
            for w_ref in (down_ref, out_ref):
                rows = w_ref.shape[2]
                for t in range(width // LANES):
                    w_ref[p, 0, :, t * LANES : (t + 1) * LANES] = ref[0, d, at : at + rows, :]
                    at += rows

    pl.when(spot[2] == 1)(lambda: take(own_ref))
    pl.when(spot[2] == 0)(lambda: take(other_ref))


def unpack_ffn(spot, own, other, width, ff, q_width):
    cols = pl.BlockSpec((width, ff // PARTS), lambda j, spot: (0, j))

    def rows(n):
        return pl.BlockSpec((PARTS, 1, n // PARTS**2, width), lambda j, spot: (0, j, 0, 0))

    gate, up, down, out = pl.pallas_call(
        unpack_ffn_kernel,
        grid_spec=pltpu.PrefetchScalarGridSpec(
            num_scalar_prefetch=1,
            grid=(PARTS,),
            in_specs=piece_specs(own.shape[2]),
            out_specs=[cols, cols, rows(ff), rows(q_width)],
        ),
        out_shape=[
            sds((width, ff), B16),
            sds((width, ff), B16),
            sds((PARTS, PARTS, ff // PARTS**2, width), B16),
            sds((PARTS, PARTS, q_width // PARTS**2, width), B16),
        ],
        compiler_params=params(),
        cost_estimate=cost(0, 22e6),
        name="place_ffn",
    )(spot, own, other)
    return gate, up, down.reshape(ff, width), out.reshape(q_width, width)


def split_pack(pack, width, ff, q_width):
    gate, down, out = pack_rows(width, ff, q_width)
    part = width // PARTS

    def cols(p):
        tiles = p.shape[2] // part
        return (
            p.reshape(PARTS, PARTS, tiles, part, LANES)
            .transpose(1, 3, 0, 2, 4)
            .reshape(width, PARTS * tiles * LANES)
        )

    def rows(p):
        n = p.shape[2] // (width // LANES)
        return (
            p.reshape(PARTS, PARTS, width // LANES, n, LANES)
            .transpose(1, 0, 3, 2, 4)
            .reshape(PARTS * PARTS * n, width)
        )

    return (
        cols(pack[:, :, :gate]),
        cols(pack[:, :, gate : 2 * gate]),
        rows(pack[:, :, 2 * gate : 2 * gate + down]),
        rows(pack[:, :, 2 * gate + down :]),
    )


def moved(array, axis, by, layer):
    sizes = [lax.axis_size(name) for name in AXES]
    pairs = []
    for f in range(sizes[1]):
        for c in range(sizes[2]):
            f2 = (f + by) % sizes[1] if axis == "fsdp" else f
            c2 = (c + by) % sizes[2] if axis == "ctx" else c
            pairs.append(
                ((layer * sizes[1] + f) * sizes[2] + c, (layer * sizes[1] + f2) * sizes[2] + c2)
            )
    return lax.ppermute(array, AXES, pairs)


def handed(array, to):
    return lax.ppermute(array, "section", [(1 - to, to)])


def passed_along(array, by):
    devices = lax.axis_size("ctx")
    pairs = [(i, i + by) for i in range(devices) if 0 <= i + by < devices]
    return lax.ppermute(array, "ctx", pairs)


def gathered_pieces(own, layer):
    shards = [own[0]] + [moved(own[0], "fsdp", d, layer) for d in range(1, PARTS)]
    travelling = jnp.stack(shards[1:])
    quarters = [jnp.stack(shards)]
    for e in range(1, PARTS):
        quarters.append(jnp.concatenate([own[e][None], moved(travelling, "ctx", e, layer)]))
    return jnp.stack(quarters)


def at(array, index):
    return lax.dynamic_index_in_dim(array, lax.rem(index, PARTS), 0, keepdims=False)


def reduced_pieces(pack, layer, fsdp_index, ctx_index):
    other = handed(pack, layer)

    def both(index):
        return at(pack, index).astype(F32) + at(other, index).astype(F32)

    total = both(ctx_index)
    for e in range(1, PARTS):
        total += moved(both(ctx_index + e).astype(B16), "ctx", e, layer).astype(F32)
    rounded = total.astype(B16)
    piece = at(total, fsdp_index)
    for d in range(1, PARTS):
        piece += moved(at(rounded, fsdp_index + d), "fsdp", d, layer).astype(F32)
    piece = piece.astype(B16)
    ring = jnp.stack([piece] + [moved(piece, "ctx", e, layer) for e in range(1, PARTS)])
    return jnp.stack([at(ring, ctx_index - p + PARTS) for p in range(PARTS)])


def per_device(
    inputs,
    grad_out,
    lengths,
    in_gain,
    query_weight,
    key_weight,
    value_weight,
    query_gain,
    key_gain,
    out_weight,
    attn_gain,
    ffn_gain,
    gate_weight,
    up_weight,
    down_weight,
    post_gain,
):
    section = lax.axis_index("section")
    fsdp_index = lax.axis_index("fsdp")
    ctx_index = lax.axis_index("ctx")
    shards = lax.axis_size("fsdp")
    in_pieces = shards == PARTS and lax.axis_size("ctx") == PARTS
    tok = inputs.shape[2]
    width = inputs.shape[3]
    q_width = query_weight.shape[2]
    ff = gate_weight.shape[2]
    first_layer = section == 0

    qkv_own = jnp.concatenate([query_weight[0], key_weight[0], value_weight[0]], axis=1)
    gain_own = jnp.concatenate(
        [in_gain[0], attn_gain[0], ffn_gain[0], post_gain[0], query_gain[0], key_gain[0]]
    )

    def as_gains(raw):
        n, m = width // shards, HD // shards
        gd = [raw[:, i * n : (i + 1) * n].reshape(1, width) for i in range(4)]
        gh = [raw[:, 4 * n + i * m : 4 * n + (i + 1) * m].reshape(1, HD) for i in range(2)]
        gd = jnp.concatenate(gd + [jnp.zeros((4, width), raw.dtype)]).astype(F32)
        gh = jnp.concatenate(gh + [jnp.zeros((6, HD), raw.dtype)]).astype(F32)
        return gd, gh

    layers = []
    if in_pieces:
        gain_rows = jnp.pad(gain_own, (0, GAIN_ROWS * LANES - gain_own.shape[0]))
        packs = pack_own(
            qkv_own,
            gain_rows.reshape(GAIN_ROWS, LANES),
            gate_weight[0],
            up_weight[0],
            down_weight[0],
            out_weight[0],
        )

        def own_first(pack):
            back = pack[::-1]
            return lax.dynamic_slice_in_dim(
                jnp.concatenate([back, back]), PARTS - 1 - ctx_index, PARTS, 0
            )

        packs = [own_first(pack) for pack in packs]
        for layer in range(2):
            spot = jnp.stack([ctx_index, fsdp_index, (section == layer).astype(jnp.int32)])
            spot = spot.astype(jnp.int32)
            pieces = gathered_pieces(packs[0], layer)
            other = handed(pieces, 1 - layer)
            w_qkv, raw = unpack_qkv(spot, pieces, other, width, qkv_own.shape[1])
            gains = as_gains(raw.reshape(PARTS, GAIN_ROWS * LANES))
            pieces = gathered_pieces(packs[1], layer)
            other = handed(pieces, 1 - layer)
            gate, up, down, out = unpack_ffn(spot, pieces, other, width, ff, q_width)
            layers.append((w_qkv, out, gate, up, down) + gains)
    else:

        def whole_weight(own):
            full = lax.all_gather(own, "fsdp", axis=0, tiled=True)
            return lax.all_gather(full, "section", axis=0)

        full = [
            whole_weight(w)
            for w in (qkv_own, out_weight[0], gate_weight[0], up_weight[0], down_weight[0])
        ]
        raw = whole_weight(gain_own[None])
        for layer in range(2):
            layers.append(tuple(w[layer] for w in full) + as_gains(raw[layer]))

    def own_row(array):
        return lax.dynamic_index_in_dim(array[:, 0], section, 0, keepdims=False)

    offset, low = layout_for(own_row(lengths), ctx_index * tok, tok)
    cos, sin = rope_tables(offset)
    low_col, low_row = low[:, None], low[None, :]

    x = own_row(inputs)
    kept = []
    for w_qkv, w_out, w_gate, w_up, w_down, gd, gh in layers:
        a, kpre, near = kv_call(x, gd, gh, cos, sin, w_qkv)
        far = passed_along(near, 1)
        qpre, q = q_call(a, gh, cos, sin, w_qkv)
        o = attn_call(q, far, near, low_col)
        y, h, g, u, z, result = ffn_call(o, x, gd, w_out, w_gate, w_up, w_down)
        kept.append((x, a, kpre, near, far, qpre, q, o, y, h, g, u, z, result))
        x = result

    cot = own_row(grad_out)
    packs, in_grads, gain_grads = [None] * 2, [None] * 2, [None] * 2
    for layer in (1, 0):
        w_qkv, w_out, w_gate, w_up, w_down, gd, gh = layers[layer]
        x, a, kpre, near, far, qpre, q, o, y, h, g, u, z, result = kept[layer]
        ffn_pack, dh, do, gd_one = ffn_back_call(
            cot, z, h, y, o, gd, g, u, w_out, w_gate, w_up, w_down
        )
        dq, dfar, dnear, gh_one = attn_back_call(q, do, qpre, far, near, low_row, gh, cos, sin)
        dback = passed_along(dfar, -1)
        if tok > WINDOW:
            dback = jnp.pad(dback, ((tok - WINDOW, 0), (0, 0)))
        wq_grad, da = q_back_call(a, dq, w_qkv)
        qkv_pack, cot, gd_two, gh_two = kv_back_call(
            a, x, dh, da, dnear, dback, kpre, gd, gh, cos, sin, w_qkv, wq_grad
        )
        in_grads[layer] = cot
        packs[layer] = (ffn_pack, qkv_pack)
        gain_grads[layer] = jnp.concatenate(
            [(gd_one + gd_two)[:4].reshape(-1), (gh_one + gh_two)[:2].reshape(-1)]
        )

    def by_layer(first, second):
        own = jnp.where(first_layer, first, second)
        got = lax.ppermute(jnp.where(first_layer, second, first), "section", [(0, 1), (1, 0)])
        return jnp.stack([jnp.where(first_layer, own, got), jnp.where(first_layer, got, own)])

    activations = by_layer(kept[0][-1], kept[1][-1])
    input_grads = by_layer(in_grads[0], in_grads[1])

    gain_sums = lax.psum(jnp.stack(gain_grads), AXES)
    gain_sums = lax.dynamic_index_in_dim(gain_sums, section, 0, keepdims=False)

    def gain_shard(first, n):
        return lax.dynamic_slice_in_dim(gain_sums, first + fsdp_index * n, n, 0)[None]

    dn, hn = width // shards, HD // shards
    d_gains = [gain_shard(i * width, dn) for i in range(4)]
    h_gains = [gain_shard(4 * width + i * HD, hn) for i in range(2)]

    if in_pieces:
        done = [None] * 2
        for layer in (1, 0):
            done[layer] = tuple(
                reduced_pieces(p, layer, fsdp_index, ctx_index) for p in packs[layer]
            )
        ffn_own, qkv_own = (jnp.where(first_layer, p, r) for p, r in zip(*done))
        n_gate, n_down, n_out = pack_rows(width, ff, q_width)
        part = width // PARTS

        def cols(p):
            tiles = p.shape[1] // part
            return p.reshape(PARTS, tiles, part, LANES).transpose(2, 0, 1, 3).reshape(part, -1)

        def rows(p):
            n = p.shape[1] // (width // LANES)
            return (
                p.reshape(PARTS, width // LANES, n, LANES).transpose(0, 2, 1, 3).reshape(-1, width)
            )

        gate_g = cols(ffn_own[:, :n_gate])
        up_g = cols(ffn_own[:, n_gate : 2 * n_gate])
        down_g = rows(ffn_own[:, 2 * n_gate : 2 * n_gate + n_down])
        out_g = rows(ffn_own[:, 2 * n_gate + n_down :])
        qkv_g = cols(qkv_own)
    else:
        sums = []
        for ffn_pack, qkv_pack in packs:
            gate, up, down, out = split_pack(ffn_pack, width, ff, q_width)
            part = width // PARTS
            tiles = qkv_pack.shape[2] // part
            qkv = (
                qkv_pack.reshape(PARTS, PARTS, tiles, part, LANES)
                .transpose(1, 3, 0, 2, 4)
                .reshape(width, -1)
            )
            sums.append((gate, up, down, out, qkv))
        shard = [
            lax.psum_scatter(
                lax.psum_scatter(jnp.stack(pair), "section", scatter_dimension=0, tiled=True)[0],
                "fsdp",
                scatter_dimension=0,
                tiled=True,
            )
            for pair in zip(*sums)
        ]
        gate_g, up_g, down_g, out_g, qkv_g = lax.psum(tuple(shard), "ctx")

    gate_g, up_g, down_g, out_g, qkv_g = (
        w.astype(F32)[None] for w in (gate_g, up_g, down_g, out_g, qkv_g)
    )
    return (
        activations[None, :, None],
        input_grads[None, :, None],
        d_gains[0],
        qkv_g[:, :, :q_width],
        qkv_g[:, :, q_width : q_width + HD],
        qkv_g[:, :, q_width + HD :],
        h_gains[0],
        h_gains[1],
        out_g,
        d_gains[1],
        d_gains[2],
        gate_g,
        up_g,
        down_g,
        d_gains[3],
    )


def solution(mesh):
    return jax.shard_map(
        per_device,
        mesh=mesh,
        in_specs=(
            P(None, "fsdp", "ctx", None),
            P(None, "fsdp", "ctx", None),
            P(None, "fsdp", None),
            P("section", "fsdp"),
            P("section", "fsdp", None),
            P("section", "fsdp", None),
            P("section", "fsdp", None),
            P("section", "fsdp"),
            P("section", "fsdp"),
            P("section", "fsdp", None),
            P("section", "fsdp"),
            P("section", "fsdp"),
            P("section", "fsdp", None),
            P("section", "fsdp", None),
            P("section", "fsdp", None),
            P("section", "fsdp"),
        ),
        out_specs=(
            P("section", None, "fsdp", "ctx", None),
            P("section", None, "fsdp", "ctx", None),
            P("section", "fsdp"),
            P("section", "fsdp", None),
            P("section", "fsdp", None),
            P("section", "fsdp", None),
            P("section", "fsdp"),
            P("section", "fsdp"),
            P("section", "fsdp", None),
            P("section", "fsdp"),
            P("section", "fsdp"),
            P("section", "fsdp", None),
            P("section", "fsdp", None),
            P("section", "fsdp", None),
            P("section", "fsdp"),
        ),
        check_vma=False,
    )
```

```python
from functools import partial

import jax
import jax.numpy as jnp
from jax import lax
from jax.experimental import pallas as pl
from jax.experimental.pallas import tpu as pltpu
from jax.sharding import PartitionSpec as P

HD = 256
WINDOW = 512
EPS = 1e-06
LANES = 128
PARTS = 4
GAIN_ROWS = 32
QB = 128
F32 = jnp.float32
B16 = jnp.bfloat16
VMEM_LIMIT = 56 * 1024 * 1024
AXES = ("section", "fsdp", "ctx")


def rope_tables(offset):
    half_dim = HD // 2
    inv_freq = 10000.0 ** (-(jnp.arange(half_dim).astype(F32) * 2.0 / HD))
    angles = offset.astype(F32)[:, None] * inv_freq[None, :]
    return (jnp.cos(angles), jnp.sin(angles))


def layout_for(seq_lens, first_place, tok_count):
    seq_ends = jnp.cumsum(seq_lens)
    seq_starts = seq_ends - seq_lens
    places = first_place + jnp.arange(tok_count)
    segment = jnp.sum((places[:, None] >= seq_ends[None, :]).astype(jnp.int32), axis=1)
    labels = jnp.arange(seq_lens.shape[0])
    seg_hit = segment[:, None] == labels[None, :]
    start = jnp.sum(jnp.where(seg_hit, seq_starts[None, :], 0), axis=1)
    offset = places - start
    low = jnp.maximum(start, places - (WINDOW - 1)) - first_place + WINDOW
    return offset, low.astype(jnp.int32)


def dot(a, b):
    return lax.dot_general(a, b, (((1,), (0,)), ((), ())), preferred_element_type=F32)


def dot_nt(a, b):
    return lax.dot_general(a, b, (((1,), (1,)), ((), ())), preferred_element_type=F32)


def dot_tn(a, b):
    return lax.dot_general(a, b, (((0,), (0,)), ((), ())), preferred_element_type=F32)


def inv_rms(v):
    return lax.rsqrt(jnp.mean(v * v, axis=-1, keepdims=True) + EPS)


def rms_back(v, gain, grad):
    r = inv_rms(v)
    gg = grad * gain
    normed = v * r
    back = r * (gg - normed * jnp.mean(normed * gg, axis=-1, keepdims=True))
    return back, jnp.sum(grad * normed, axis=0, keepdims=True)


def rope(v, cos, sin):
    u, w = v[:, : HD // 2], v[:, HD // 2 :]
    return jnp.concatenate([u * cos - w * sin, w * cos + u * sin], axis=-1)


def rope_back(g, cos, sin):
    a, b = g[:, : HD // 2], g[:, HD // 2 :]
    return jnp.concatenate([a * cos + b * sin, b * cos - a * sin], axis=-1)


GELU_C = 0.7978845608028654
GELU_A = 0.044715


def gelu_parts(g):
    g2 = g * g
    t = jnp.tanh(GELU_C * g * (1.0 + GELU_A * g2))
    half = 0.5 * (1.0 + t)
    value = g * half
    slope = half + 0.5 * g * (1.0 - t * t) * (GELU_C * (1.0 + 3.0 * GELU_A * g2))
    return value, slope


def params(**kw):
    return pltpu.CompilerParams(vmem_limit_bytes=VMEM_LIMIT, **kw)


def cost(flops, nbytes):
    return pl.CostEstimate(flops=int(flops) * 30, bytes_accessed=int(nbytes), transcendentals=0)


def whole(shape):
    n = len(shape)
    return pl.BlockSpec(shape, lambda *i: (0,) * n)


def held_back(kernel, first, n):
    def body(*refs):
        kernel(*refs[:first], *refs[first + n :])

    return body


def sds(shape, dtype):
    return jax.ShapeDtypeStruct(shape, dtype)


def kv_kernel(x_ref, gd_ref, gh_ref, cos_ref, sin_ref, w_ref, a_ref, pre_ref, kv_ref):
    x = x_ref[...].astype(F32)
    a = (x * inv_rms(x) * gd_ref[0:1, :]).astype(B16)
    a_ref[...] = a
    both = dot(a, w_ref[...])
    pre = both[:, :HD]
    pre_ref[...] = pre.astype(B16)
    keys = rope(pre * inv_rms(pre) * gh_ref[1:2, :], cos_ref[...], sin_ref[...])
    kv_ref[:, :HD] = keys.astype(B16)
    kv_ref[:, HD:] = both[:, HD:].astype(B16)


def kv_call(layer, x, gd, gh, cos, sin, w_qkv):
    tok, width = x.shape
    q_width = w_qkv.shape[2] - 2 * HD
    return pl.pallas_call(
        kv_kernel,
        grid=(1,),
        in_specs=[
            whole(x.shape),
            whole(gd.shape),
            whole(gh.shape),
            whole(cos.shape),
            whole(sin.shape),
            pl.BlockSpec((None, width, 2 * HD), lambda j: (layer, 0, q_width // (2 * HD))),
        ],
        out_specs=[whole((tok, width)), whole((tok, HD)), whole((tok, 2 * HD))],
        out_shape=[sds((tok, width), B16), sds((tok, HD), B16), sds((tok, 2 * HD), B16)],
        compiler_params=params(),
        cost_estimate=cost(4 * tok * width * HD, 4e6),
        name="keys_values",
    )(x, gd, gh, cos, sin, w_qkv)


def q_kernel(a_ref, gh_ref, cos_ref, sin_ref, w_ref, pre_ref, q_ref):
    pre = dot(a_ref[...], w_ref[...])
    pre_ref[...] = pre.astype(B16)
    q_ref[...] = rope(pre * inv_rms(pre) * gh_ref[0:1, :], cos_ref[...], sin_ref[...]).astype(B16)


def q_call(layer, a, gh, cos, sin, w_qkv):
    tok, width = a.shape
    q_width = w_qkv.shape[2] - 2 * HD
    block = pl.BlockSpec((tok, HD), lambda j: (0, j))
    return pl.pallas_call(
        q_kernel,
        grid=(q_width // HD,),
        in_specs=[
            whole(a.shape),
            whole(gh.shape),
            whole(cos.shape),
            whole(sin.shape),
            pl.BlockSpec((None, width, HD), lambda j: (layer, 0, j)),
        ],
        out_specs=[block, block],
        out_shape=[sds((tok, q_width), B16), sds((tok, q_width), B16)],
        compiler_params=params(),
        cost_estimate=cost(2 * tok * width * q_width, 5e6),
        name="queries",
    )(a, gh, cos, sin, w_qkv)


SCORE_SCALE = HD ** (-0.5)


def attn_kernel(q_ref, far_ref, near_ref, low_ref, o_ref, kv_scr):
    b = pl.program_id(0)

    @pl.when(b == 0)
    def _():
        kv_scr[:WINDOW, :] = far_ref[...]
        kv_scr[WINDOW:, :] = near_ref[...]

    span = WINDOW + QB
    first = pl.multiple_of(b * QB, QB)
    keys = kv_scr[pl.ds(first, span), :HD]
    vals = kv_scr[pl.ds(first, span), HD:]
    col = lax.broadcasted_iota(jnp.int32, (QB, span), 1)
    row = lax.broadcasted_iota(jnp.int32, (QB, span), 0)
    allowed = (col >= low_ref[...] - b * QB) & (col <= row + WINDOW)
    for h in range(q_ref.shape[1] // HD):
        scores = dot_nt(q_ref[:, h * HD : (h + 1) * HD], keys) * SCORE_SCALE
        e = jnp.where(allowed, jnp.exp(scores), 0.0)
        total = jnp.sum(e, axis=1, keepdims=True)
        o_ref[:, h * HD : (h + 1) * HD] = (dot(e.astype(B16), vals) / total).astype(B16)


def attn_call(q, far, near, low):
    tok, q_width = q.shape
    return pl.pallas_call(
        attn_kernel,
        grid=(tok // QB,),
        in_specs=[
            pl.BlockSpec((QB, q_width), lambda b: (b, 0)),
            whole(far.shape),
            whole(near.shape),
            pl.BlockSpec((QB, 1), lambda b: (b, 0)),
        ],
        out_specs=pl.BlockSpec((QB, q_width), lambda b: (b, 0)),
        out_shape=sds((tok, q_width), B16),
        scratch_shapes=[pltpu.VMEM((WINDOW + tok, 2 * HD), B16)],
        compiler_params=params(),
        cost_estimate=cost(4 * tok * q_width * (WINDOW + QB), 3e6),
        name="attend",
    )(q, far, near, low)


FC = 512


def ffn_kernel(
    o_ref, x_ref, gd_ref, wo_ref, wg_ref, wu_ref, wd_ref,
    y_ref, h_ref, g_ref, u_ref, z_ref, out_ref, b_scr,
):
    j = pl.program_id(0)

    @pl.when(j == 0)
    def _():
        y = dot(o_ref[...], wo_ref[...])
        y_ref[...] = y
        h = x_ref[...].astype(F32) + y * inv_rms(y) * gd_ref[1:2, :]
        h_ref[...] = h
        b_scr[...] = (h * inv_rms(h) * gd_ref[2:3, :]).astype(B16)

    b = b_scr[...]
    g = dot(b, wg_ref[...])
    u = dot(b, wu_ref[...])
    g_ref[...] = g.astype(B16)
    u_ref[...] = u.astype(B16)
    value = g * 0.5 * (1.0 + jnp.tanh(GELU_C * g * (1.0 + GELU_A * g * g)))
    z = dot((value * u).astype(B16), wd_ref[...])

    @pl.when(j == 0)
    def _():
        z_ref[...] = z

    @pl.when(j > 0)
    def _():
        z_ref[...] += z

    @pl.when(j == pl.num_programs(0) - 1)
    def _():
        zz = z_ref[...]
        out_ref[...] = (h_ref[...] + zz * inv_rms(zz) * gd_ref[3:4, :]).astype(B16)


def ffn_call(o, x, gd, w_out, w_gate, w_up, w_down):
    tok, width = x.shape
    ff = w_gate.shape[1]
    cols = pl.BlockSpec((tok, FC), lambda j: (0, j))
    tw = whole((tok, width))
    return pl.pallas_call(
        ffn_kernel,
        grid=(ff // FC,),
        in_specs=[
            whole(o.shape),
            tw,
            whole(gd.shape),
            whole(w_out.shape),
            pl.BlockSpec((width, FC), lambda j: (0, j)),
            pl.BlockSpec((width, FC), lambda j: (0, j)),
            pl.BlockSpec((FC, width), lambda j: (j, 0)),
        ],
        out_specs=[tw, tw, cols, cols, tw, tw],
        out_shape=[
            sds((tok, width), F32),
            sds((tok, width), F32),
            sds((tok, ff), B16),
            sds((tok, ff), B16),
            sds((tok, width), F32),
            sds((tok, width), B16),
        ],
        scratch_shapes=[pltpu.VMEM((tok, width), B16)],
        compiler_params=params(),
        cost_estimate=cost(2 * tok * width * (o.shape[1] + 3 * ff), 22e6),
        name="feed_forward",
    )(o, x, gd, w_out, w_gate, w_up, w_down)


def ffn_back_kernel(
    spot, c_ref, z_ref, h_ref, y_ref, o_ref, gd_ref, g_ref, u_ref, wo_ref, wg_ref, wu_ref, wd_ref,
    keep_ref, send_ref, dh_ref, do_ref, gg_ref, dz_scr, bt_scr, db_scr,
):
    j = pl.program_id(0)
    half = keep_ref.shape[2]

    def put(blocks):
        for section in range(2):

            @pl.when(spot[2] == section)
            def _():
                for c_part, p, row, block in blocks:
                    ref = keep_ref if row // half == section else send_ref
                    ref[c_part, p, pl.ds(row % half, block.shape[0]), :] = block

    tok, width = c_ref.shape
    part = width // PARTS
    n_gate = PARTS * part
    n_down = (width // LANES) * (FC // PARTS)
    out_rows = o_ref.shape[1] // (PARTS * PARTS)

    @pl.when(j == 0)
    def _():
        dz, post_grad = rms_back(z_ref[...], gd_ref[3:4, :], c_ref[...].astype(F32))
        dz_scr[...] = dz.astype(B16)
        gg_ref[...] = jnp.zeros(gg_ref.shape, F32)
        gg_ref[3:4, :] = post_grad
        h = h_ref[...]
        bt_scr[...] = (h * inv_rms(h) * gd_ref[2:3, :]).T.astype(B16)
        db_scr[...] = jnp.zeros(db_scr.shape, F32)

    dz = dz_scr[...]
    df = dot_nt(dz, wd_ref[...])
    value, slope = gelu_parts(g_ref[...].astype(F32))
    u = u_ref[...].astype(F32)
    f = (value * u).astype(B16)
    du = (df * value).astype(B16)
    dg = (df * u * slope).astype(B16)
    db_scr[...] += dot_nt(dg, wg_ref[...]) + dot_nt(du, wu_ref[...])
    bt = bt_scr[...]
    blocks = []
    for first, term in ((0, dg), (n_gate, du)):
        grad = dot(bt, term).astype(B16)
        for p in range(PARTS):
            for t in range(FC // LANES):
                block = grad[p * part : (p + 1) * part, t * LANES : (t + 1) * LANES]
                blocks.append((j, p, first + t * part, block))
    grad = dot_tn(f, dz).astype(B16)
    rows = FC // PARTS
    for p in range(PARTS):
        for t in range(width // LANES):
            block = grad[p * rows : (p + 1) * rows, t * LANES : (t + 1) * LANES]
            blocks.append((p, j, 2 * n_gate + t * rows, block))
    put(blocks)

    @pl.when(j == pl.num_programs(0) - 1)
    def _():
        add, ffn_grad = rms_back(h_ref[...], gd_ref[2:3, :], db_scr[...])
        dh = c_ref[...].astype(F32) + add
        dh_ref[...] = dh
        dy32, attn_grad = rms_back(y_ref[...], gd_ref[1:2, :], dh)
        dy = dy32.astype(B16)
        gg_ref[1:2, :] = attn_grad
        gg_ref[2:3, :] = ffn_grad
        do_ref[...] = dot_nt(dy, wo_ref[...]).astype(B16)
        og = dot_tn(o_ref[...], dy).astype(B16)
        out_blocks = []
        for f_part in range(PARTS):
            for p in range(PARTS):
                at = (f_part * PARTS + p) * out_rows
                for t in range(width // LANES):
                    block = og[at : at + out_rows, t * LANES : (t + 1) * LANES]
                    out_blocks.append((p, f_part, 2 * n_gate + n_down + t * out_rows, block))
        put(out_blocks)


def pack_rows(width, ff, q_width):
    gate = width // PARTS * (ff // PARTS // LANES)
    down = ff // (PARTS * PARTS) * (width // LANES)
    out = q_width // (PARTS * PARTS) * (width // LANES)
    return gate, down, out


def ffn_back_call(spot, c, z, h, y, o, gd, g, u, w_out, w_gate, w_up, w_down):
    tok, width = c.shape
    ff = w_gate.shape[1]
    q_width = o.shape[1]
    gate, down, out = pack_rows(width, ff, q_width)
    pack_shape = (PARTS, PARTS, (2 * gate + down + out) // 2, LANES)
    cols = pl.BlockSpec((tok, FC), lambda j, *_: (0, j))
    tw = whole((tok, width))
    return pl.pallas_call(
        ffn_back_kernel,
        grid_spec=pltpu.PrefetchScalarGridSpec(
            num_scalar_prefetch=1,
            grid=(ff // FC,),
            in_specs=[
                tw,
                tw,
                tw,
                tw,
                whole(o.shape),
                whole(gd.shape),
                cols,
                cols,
                whole(w_out.shape),
                pl.BlockSpec((width, FC), lambda j, *_: (0, j)),
                pl.BlockSpec((width, FC), lambda j, *_: (0, j)),
                pl.BlockSpec((FC, width), lambda j, *_: (j, 0)),
            ],
            out_specs=[whole(pack_shape), whole(pack_shape), tw, whole(o.shape), whole(gd.shape)],
            scratch_shapes=[
                pltpu.VMEM((tok, width), B16),
                pltpu.VMEM((width, tok), B16),
                pltpu.VMEM((tok, width), F32),
            ],
        ),
        out_shape=[
            sds(pack_shape, B16),
            sds(pack_shape, B16),
            sds((tok, width), F32),
            sds(o.shape, B16),
            sds(gd.shape, F32),
        ],
        compiler_params=params(),
        cost_estimate=cost(4 * tok * width * (q_width + 3 * ff), 35e6),
        name="feed_forward_back",
    )(spot, c, z, h, y, o, gd, g, u, w_out, w_gate, w_up, w_down)


def attn_back_kernel(
    q_ref, do_ref, qpre_ref, far_ref, near_ref, low_ref, gh_ref, cos_ref, sin_ref,
    dq_ref, dfar_ref, dnear_ref, gg_ref, kv_scr, dkv_scr,
):
    b = pl.program_id(0)

    @pl.when(b == 0)
    def _():
        kv_scr[:WINDOW, :] = far_ref[...]
        kv_scr[WINDOW:, :] = near_ref[...]
        dkv_scr[...] = jnp.zeros(dkv_scr.shape, F32)
        gg_ref[...] = jnp.zeros(gg_ref.shape, F32)

    span = WINDOW + QB
    first = pl.multiple_of(b * QB, QB)
    keys = kv_scr[pl.ds(first, span), :HD]
    vals = kv_scr[pl.ds(first, span), HD:]
    col = lax.broadcasted_iota(jnp.int32, (span, QB), 0)
    row = lax.broadcasted_iota(jnp.int32, (span, QB), 1)
    allowed = (col >= low_ref[...] - b * QB) & (col <= row + WINDOW)
    cos, sin = cos_ref[...], sin_ref[...]
    dkeys = jnp.zeros((span, HD), F32)
    dvals = jnp.zeros((span, HD), F32)
    gain_grad = jnp.zeros((1, HD), F32)
    for h in range(q_ref.shape[1] // HD):
        at = slice(h * HD, (h + 1) * HD)
        q = q_ref[:, at]
        do = do_ref[:, at]
        scores = dot_nt(keys, q) * SCORE_SCALE
        e = jnp.where(allowed, jnp.exp(scores), 0.0)
        p = e * (1.0 / jnp.sum(e, axis=0, keepdims=True))
        dp = dot_nt(vals, do)
        inner = jnp.sum(p * dp, axis=0, keepdims=True)
        ds = (p * (dp - inner)).astype(B16)
        dvals += dot(p.astype(B16), do)
        dkeys += dot(ds, q)
        dq = dot_tn(ds, keys) * SCORE_SCALE
        dq0, gain = rms_back(qpre_ref[:, at].astype(F32), gh_ref[0:1, :], rope_back(dq, cos, sin))
        gain_grad += gain
        dq_ref[:, at] = dq0.astype(B16)
    dkv_scr[pl.ds(first, span), :HD] += dkeys * SCORE_SCALE
    dkv_scr[pl.ds(first, span), HD:] += dvals
    gg_ref[0:1, :] += gain_grad

    @pl.when(b == pl.num_programs(0) - 1)
    def _():
        dfar_ref[...] = dkv_scr[:WINDOW, :].astype(B16)
        dnear_ref[...] = dkv_scr[WINDOW:, :]


def attn_back_call(q, do, qpre, far, near, low_row, gh, cos, sin, *deps):
    tok, q_width = q.shape
    block = pl.BlockSpec((QB, q_width), lambda b: (b, 0))
    table = pl.BlockSpec((QB, HD // 2), lambda b: (b, 0))
    return pl.pallas_call(
        held_back(attn_back_kernel, 9, len(deps)),
        grid=(tok // QB,),
        in_specs=[
            block,
            block,
            block,
            whole(far.shape),
            whole(near.shape),
            pl.BlockSpec((1, QB), lambda b: (0, b)),
            whole(gh.shape),
            table,
            table,
        ]
        + [pl.BlockSpec(memory_space=pl.ANY)] * len(deps),
        out_specs=[block, whole(far.shape), whole(near.shape), whole(gh.shape)],
        out_shape=[
            sds(q.shape, B16),
            sds(far.shape, B16),
            sds(near.shape, F32),
            sds(gh.shape, F32),
        ],
        scratch_shapes=[
            pltpu.VMEM((WINDOW + tok, 2 * HD), B16),
            pltpu.VMEM((WINDOW + tok, 2 * HD), F32),
        ],
        compiler_params=params(),
        cost_estimate=cost(10 * tok * q_width * (WINDOW + QB), 8e6),
        name="attend_back",
    )(q, do, qpre, far, near, low_row, gh, cos, sin, *deps)


def q_back_kernel(a_ref, dq_ref, w_ref, wq_grad_ref, da_ref):
    dq = dq_ref[...]
    wq_grad_ref[...] = dot_tn(a_ref[...], dq).astype(B16)
    da_ref[...] = dot_nt(dq, w_ref[...])


def q_back_call(layer, a, dq, w_qkv, *deps):
    tok, width = a.shape
    q_width = dq.shape[1]
    return pl.pallas_call(
        held_back(q_back_kernel, 3, len(deps)),
        grid=(1,),
        in_specs=[
            whole(a.shape),
            whole(dq.shape),
            pl.BlockSpec((None, width, q_width), lambda j: (layer, 0, 0)),
        ]
        + [pl.BlockSpec(memory_space=pl.ANY)] * len(deps),
        out_specs=[whole((width, q_width)), whole((tok, width))],
        out_shape=[sds((width, q_width), B16), sds((tok, width), F32)],
        compiler_params=params(),
        cost_estimate=cost(4 * tok * width * q_width, 6e6),
        name="queries_back",
    )(a, dq, w_qkv, *deps)


def kv_back_kernel(
    a_ref, x_ref, dh_ref, da_ref, dnear_ref, dback_ref, kpre_ref, gd_ref, gh_ref,
    cos_ref, sin_ref, w_ref, wq_ref, gd_part_ref, gh_part_ref, pack_ref, dx_ref,
):
    width = x_ref.shape[1]
    part = width // PARTS
    dkv = dnear_ref[...]
    tail = dback_ref[...].astype(F32)
    dkv = dkv + tail
    dk0, k_grad = rms_back(
        kpre_ref[...].astype(F32),
        gh_ref[1:2, :],
        rope_back(dkv[:, :HD], cos_ref[...], sin_ref[...]),
    )
    both = jnp.concatenate([dk0.astype(B16), dkv[:, HD:].astype(B16)], axis=1)
    kv_grad = dot_tn(a_ref[...], both).astype(B16)
    da = da_ref[...] + dot_nt(both, w_ref[...])
    add, in_grad = rms_back(x_ref[...].astype(F32), gd_ref[0:1, :], da)
    dx_ref[...] = (dh_ref[...] + add).astype(B16)
    gains = [in_grad] + [gd_part_ref[i : i + 1, :] for i in range(1, 4)]
    gains += [gh_part_ref[0:1, :], k_grad]
    lines = [g[:, t : t + LANES] for g in gains for t in range(0, g.shape[1], LANES)]
    n = len(lines) // PARTS
    blank = jnp.zeros((GAIN_ROWS - n, LANES), F32)
    for c_part in range(PARTS):
        block = jnp.concatenate(lines[c_part * n : (c_part + 1) * n] + [blank]).astype(B16)
        for p in range(PARTS):
            pack_ref[c_part, p, pack_ref.shape[2] - GAIN_ROWS :, :] = block
    q_tiles = wq_ref.shape[1] // LANES
    tiles = q_tiles + 2 * HD // LANES
    each = tiles // PARTS
    for t in range(tiles):
        c_part, slot = t // each, t % each
        for p in range(PARTS):
            rows = slice(p * part, (p + 1) * part)
            if t < q_tiles:
                piece = wq_ref[rows, t * LANES : (t + 1) * LANES]
            else:
                piece = kv_grad[rows, (t - q_tiles) * LANES : (t - q_tiles + 1) * LANES]
            pack_ref[c_part, p, slot * part : (slot + 1) * part, :] = piece


def kv_back_call(
    layer, a, x, dh, da, dnear, dback, kpre, gd, gh, cos, sin, w_qkv, wq_grad, gd_part, gh_part
):
    tok, width = a.shape
    q_width = wq_grad.shape[1]
    part = width // PARTS
    rows = part * ((q_width + 2 * HD) // LANES // PARTS) + GAIN_ROWS
    pack_shape = (PARTS, PARTS, rows, LANES)
    tw = whole((tok, width))
    return pl.pallas_call(
        kv_back_kernel,
        grid=(1,),
        in_specs=[
            tw,
            tw,
            tw,
            tw,
            whole(dnear.shape),
            whole(dback.shape),
            whole(kpre.shape),
            whole(gd.shape),
            whole(gh.shape),
            whole(cos.shape),
            whole(sin.shape),
            pl.BlockSpec((None, width, 2 * HD), lambda j: (layer, 0, q_width // (2 * HD))),
            whole(wq_grad.shape),
            whole(gd.shape),
            whole(gh.shape),
        ],
        out_specs=[whole(pack_shape), tw],
        out_shape=[sds(pack_shape, B16), sds((tok, width), B16)],
        compiler_params=params(),
        cost_estimate=cost(8 * tok * width * HD, 10e6),
        name="keys_values_back",
    )(a, x, dh, da, dnear, dback, kpre, gd, gh, cos, sin, w_qkv, wq_grad, gd_part, gh_part)


def pack_qkv_kernel(spot, q_ref, k_ref, v_ref, gain_ref, dep_ref, all_ref, own_ref):
    part = q_ref.shape[0]
    refs = [(r, t) for r in (q_ref, k_ref, v_ref) for t in range(r.shape[1] // LANES)]
    each = len(refs) // PARTS
    for n, (ref, t) in enumerate(refs):
        rows = slice(n % each * part, (n % each + 1) * part)
        all_ref[n // each, rows, :] = ref[:, t * LANES : (t + 1) * LANES]
    for c_part in range(PARTS):
        all_ref[c_part, each * part :, :] = gain_ref[...]
    own_ref[0] = all_ref[spot[0]]


def pack_qkv(spot, query, key, value, gains, dep):
    weights = (query, key, value)
    rows = sum(w.shape[2] for w in weights) // PARTS // LANES * query.shape[1] + GAIN_ROWS
    return pl.pallas_call(
        pack_qkv_kernel,
        grid_spec=pltpu.PrefetchScalarGridSpec(
            num_scalar_prefetch=1,
            grid=(1,),
            in_specs=[
                pl.BlockSpec((None,) + w.shape[1:], lambda i, spot: (0, 0, 0)) for w in weights
            ]
            + [whole(gains.shape), pl.BlockSpec(memory_space=pl.ANY)],
            out_specs=[whole((PARTS, rows, LANES)), whole((1, rows, LANES))],
        ),
        out_shape=[sds((PARTS, rows, LANES), B16), sds((1, rows, LANES), B16)],
        compiler_params=params(),
        cost_estimate=cost(0, 2e6),
        name="pack_qkv",
    )(spot, *weights, gains, dep)


def pack_ffn_kernel(gate_ref, up_ref, down_ref, out_ref, all_ref):
    at = 0
    for ref in (gate_ref, up_ref, down_ref, out_ref):
        rows = ref.shape[0]
        for t in range(ref.shape[1] // LANES):
            all_ref[at : at + rows, :] = ref[:, t * LANES : (t + 1) * LANES]
            at += rows


def pack_ffn(gate, up, down, out):
    by_cols = pl.BlockSpec(
        (None, gate.shape[1], gate.shape[2] // PARTS), lambda i: (0, 0, i)
    )

    def by_rows(w):
        return pl.BlockSpec((None, w.shape[1] // PARTS, w.shape[2]), lambda i: (0, i, 0))

    rows = sum(w.size for w in (gate, up, down, out)) // PARTS // LANES
    return pl.pallas_call(
        pack_ffn_kernel,
        grid=(PARTS,),
        in_specs=[by_cols, by_cols, by_rows(down), by_rows(out)],
        out_specs=pl.BlockSpec((None, rows, LANES), lambda i: (i, 0, 0)),
        out_shape=sds((PARTS, rows, LANES), B16),
        compiler_params=params(),
        cost_estimate=cost(0, 5e6),
        name="pack_ffn",
    )(gate, up, down, out)


def half_quarter_kernel(layer, spot, own_ref, other_ref, *refs):
    mine = spot[2] == layer

    @pl.when(mine)
    def _():
        refs[-1][...] = own_ref[...]

    @pl.when(jnp.logical_not(mine))
    def _():
        refs[-1][...] = other_ref[...]


def half_quarter(layer, spot, own, other, *deps):
    shape = (1, own.shape[1] // 2, LANES)
    block = pl.BlockSpec(shape, lambda i, spot: (spot[0], spot[2], 0))
    return pl.pallas_call(
        partial(half_quarter_kernel, layer),
        grid_spec=pltpu.PrefetchScalarGridSpec(
            num_scalar_prefetch=1,
            grid=(1,),
            in_specs=[block, block] + [pl.BlockSpec(memory_space=pl.ANY)] * len(deps),
            out_specs=pl.BlockSpec(shape, lambda i, spot: (0, 0, 0)),
        ),
        out_shape=sds(shape, B16),
        compiler_params=params(),
        cost_estimate=cost(0, 1e6),
        name="half_quarter",
    )(spot, own, other, *deps)


def joined(parts, *deps):
    parts = [p if isinstance(p, tuple) else (p, 0, p.shape[1]) for p in parts]
    counts = [p[0].shape[0] for p in parts]

    def body(*refs):
        at = 0
        for (array, low, high), ref in zip(parts, refs):
            refs[-1][at : at + array.shape[0]] = ref[:, low:high, :]
            at += array.shape[0]

    shape = (sum(counts), parts[0][2] - parts[0][1], LANES)
    return pl.pallas_call(
        body,
        in_specs=[pl.BlockSpec(memory_space=pltpu.VMEM)] * len(parts)
        + [pl.BlockSpec(memory_space=pl.ANY)] * len(deps),
        out_specs=pl.BlockSpec(memory_space=pltpu.VMEM),
        out_shape=sds(shape, B16),
        compiler_params=params(),
        cost_estimate=cost(0, 4 * shape[0] * shape[1] * LANES),
        name="joined",
    )(*[p[0] for p in parts], *deps)


def place_qkv_kernel(spot, own_ref, other_ref, w_ref, gain_ref):
    part = w_ref.shape[0] // PARTS
    each = w_ref.shape[1] // LANES // PARTS

    def take(ref):
        for c_part in range(PARTS):
            e = spot[0] ^ c_part
            for p in range(PARTS):
                d = spot[1] ^ p
                at = jnp.where(d == 0, c_part, PARTS + (PARTS - 1) * e + d - 1)
                for t in range(each):
                    lane = (c_part * each + t) * LANES
                    w_ref[p * part : (p + 1) * part, lane : lane + LANES] = ref[
                        at, t * part : (t + 1) * part, :
                    ]
                if c_part == 0:
                    gain_ref[p] = ref[at, ref.shape[1] - GAIN_ROWS :, :]

    pl.when(pl.program_id(0) == 0)(lambda: take(own_ref))
    pl.when(pl.program_id(0) == 1)(lambda: take(other_ref))


def place_qkv(spot, own, other, width, cols):
    everything = pl.BlockSpec(own.shape, lambda i, spot: (0, 0, 0))
    return pl.pallas_call(
        place_qkv_kernel,
        grid_spec=pltpu.PrefetchScalarGridSpec(
            num_scalar_prefetch=1,
            grid=(2,),
            in_specs=[everything, everything],
            out_specs=[
                pl.BlockSpec((None, width, cols), lambda i, spot: (spot[2] ^ i, 0, 0)),
                pl.BlockSpec(
                    (None, PARTS, GAIN_ROWS, LANES), lambda i, spot: (spot[2] ^ i, 0, 0, 0)
                ),
            ],
        ),
        out_shape=[sds((2, width, cols), B16), sds((2, PARTS, GAIN_ROWS, LANES), B16)],
        compiler_params=params(),
        cost_estimate=cost(0, 8e6),
        name="place_qkv",
    )(spot, own, other)


def place_ffn_kernel(
    layer, spot, own_ref, other_ref, near_ref, far_ref, got_near_ref, got_far_ref,
    gate_ref, up_ref, down_ref, out_ref, pieces, sems,
):
    step = pl.program_id(0)
    section = spot[2]
    last = PARTS * PARTS - PARTS + 1
    shard = pieces.at[:PARTS]
    copies = [
        pltpu.make_async_copy(near_ref, pieces.at[PARTS:last, section], sems.at[1]),
        pltpu.make_async_copy(got_near_ref, pieces.at[PARTS:last, 1 - section], sems.at[2]),
        pltpu.make_async_copy(far_ref, pieces.at[last:, section], sems.at[3]),
        pltpu.make_async_copy(got_far_ref, pieces.at[last:, 1 - section], sems.at[4]),
    ]

    def shard_copy(do):
        pl.when(section == layer)(lambda: do(pltpu.make_async_copy(own_ref, shard, sems.at[0])))
        pl.when(section != layer)(lambda: do(pltpu.make_async_copy(other_ref, shard, sems.at[0])))

    @pl.when(step == 0)
    def _():
        shard_copy(lambda copy: copy.start())
        for copy in copies:
            copy.start()
        shard_copy(lambda copy: copy.wait())
        copies[0].wait()
        copies[1].wait()

    @pl.when(step == PARTS - 1)
    def _():
        copies[2].wait()
        copies[3].wait()

    width, cols = gate_ref.shape
    part = width // PARTS
    half = pieces.shape[2]
    c_part = spot[0] ^ step
    for p in range(PARTS):
        d = spot[1] ^ p
        index = jnp.where(d == 0, c_part, PARTS + (PARTS - 1) * step + d - 1)

        def piece(at, n):
            return pieces[index, at // half, at % half : at % half + n, :]

        at = 0
        for w_ref in (gate_ref, up_ref):
            for t in range(cols // LANES):
                w_ref[p * part : (p + 1) * part, t * LANES : (t + 1) * LANES] = piece(at, part)
                at += part
        for w_ref in (down_ref, out_ref):
            rows = w_ref.shape[2]
            for t in range(width // LANES):
                w_ref[p, 0, :, t * LANES : (t + 1) * LANES] = piece(at, rows)
                at += rows


def place_ffn(layer, spot, own, other, pieces, width, ff, q_width):
    cols = pl.BlockSpec((width, ff // PARTS), lambda i, spot: (0, spot[0] ^ i))

    def rows(n):
        return pl.BlockSpec(
            (PARTS, 1, n // PARTS**2, width), lambda i, spot: (0, spot[0] ^ i, 0, 0)
        )

    half = own.shape[1] // 2
    shard = (PARTS, 2, half, LANES)
    gate, up, down, out = pl.pallas_call(
        partial(place_ffn_kernel, layer),
        grid_spec=pltpu.PrefetchScalarGridSpec(
            num_scalar_prefetch=1,
            grid=(PARTS,),
            in_specs=[pl.BlockSpec(memory_space=pl.ANY)] * 6,
            out_specs=[cols, cols, rows(ff), rows(q_width)],
            scratch_shapes=[
                pltpu.VMEM((PARTS * PARTS, 2, half, LANES), B16),
                pltpu.SemaphoreType.DMA((5,)),
            ],
        ),
        out_shape=[
            sds((width, ff), B16),
            sds((width, ff), B16),
            sds((PARTS, PARTS, ff // PARTS**2, width), B16),
            sds((PARTS, PARTS, q_width // PARTS**2, width), B16),
        ],
        compiler_params=params(),
        cost_estimate=cost(0, 18e6),
        name="place_ffn",
    )(spot, own.reshape(shard), other.reshape(shard), *pieces)
    return gate, up, down.reshape(ff, width), out.reshape(q_width, width)


def add_split_kernel(spot, first_ref, second_ref, *refs):
    keep_a, send_a, keep_b, send_b = refs[-PARTS:]
    half = first_ref.shape[1] // 2
    a, b = slice(0, half), slice(half, 2 * half)
    for rows, far, out, n in (
        (a, 0, keep_a, 0), (a, 2, keep_a, 1), (a, 1, send_a, 0), (a, 3, send_a, 1),
        (b, 0, keep_b, 0), (b, 1, keep_b, 1), (b, 2, send_b, 0), (b, 3, send_b, 1),
    ):
        c_part = spot[0] ^ far
        total = first_ref[c_part, rows, :].astype(F32) + second_ref[c_part, rows, :].astype(F32)
        out[n] = total.astype(B16)


def add_split(spot, first, second, *deps):
    n = first.shape[2]
    block = pl.BlockSpec((PARTS, None, n, LANES), lambda i, spot: (0, i, 0, 0))
    out = pl.BlockSpec((2, None, n // 2, LANES), lambda i, spot: (0, i, 0, 0))
    return pl.pallas_call(
        add_split_kernel,
        grid_spec=pltpu.PrefetchScalarGridSpec(
            num_scalar_prefetch=1,
            grid=(PARTS,),
            in_specs=[block, block] + [pl.BlockSpec(memory_space=pl.ANY)] * len(deps),
            out_specs=[out] * PARTS,
        ),
        out_shape=[sds((2, PARTS, n // 2, LANES), B16)] * PARTS,
        compiler_params=params(),
        cost_estimate=cost(0, 3 * 2 * first.size),
        name="add_split",
    )(spot, first, second, *deps)


def add_pairs_kernel(a_ref, b_ref, c_ref, d_ref, *refs):
    refs[-2][...] = (a_ref[...].astype(F32) + b_ref[...].astype(F32)).astype(B16)
    refs[-1][...] = (c_ref[...].astype(F32) + d_ref[...].astype(F32)).astype(B16)


def add_pairs(a, b, c, d, *deps):
    shape = a.shape[1:]
    return pl.pallas_call(
        add_pairs_kernel,
        grid=(1,),
        in_specs=[pl.BlockSpec((None,) + shape, lambda i: (1, 0, 0, 0))] * 4
        + [pl.BlockSpec(memory_space=pl.ANY)] * len(deps),
        out_specs=[whole(shape)] * 2,
        out_shape=[sds(shape, B16)] * 2,
        compiler_params=params(),
        cost_estimate=cost(0, 6 * a.size),
        name="add_pairs",
    )(a, b, c, d, *deps)


def sum_parts_kernel(spot, a0, a1, a2, b0, b1, b2, *refs):
    outs = refs[-PARTS:]
    half = a0.shape[1]
    for d in range(PARTS):
        f = spot[1] ^ d
        for rows, terms in ((slice(0, half), (a0, a1, a2)), (slice(half, 2 * half), (b0, b1, b2))):
            total = sum(term[f].astype(F32) for term in terms)
            outs[d][rows, :] = total.astype(B16)


def sum_parts(spot, split, got, last, *deps):
    keep_a, _, keep_b, _ = split
    shape = keep_a.shape[1:]
    first = pl.BlockSpec((None,) + shape, lambda i, spot: (0, 0, 0, 0))
    one = whole(shape)
    out = (2 * shape[1], LANES)
    return pl.pallas_call(
        sum_parts_kernel,
        grid_spec=pltpu.PrefetchScalarGridSpec(
            num_scalar_prefetch=1,
            grid=(1,),
            in_specs=[first, first, one] * 2 + [pl.BlockSpec(memory_space=pl.ANY)] * len(deps),
            out_specs=[whole(out)] * PARTS,
        ),
        out_shape=[sds(out, B16)] * PARTS,
        compiler_params=params(),
        cost_estimate=cost(0, 10 * keep_a.size),
        name="sum_parts",
    )(spot, keep_a, got[0], last[0], keep_b, got[1], last[1], *deps)


def choose_ring_kernel(spot, *refs):
    firsts, seconds, out_ref = refs[:PARTS], refs[PARTS : 2 * PARTS], refs[-1]
    rows = out_ref.shape[1]
    for e in range(PARTS):

        @pl.when(spot[2] == 0)
        def _():
            out_ref[e] = seconds[e][...]

        @pl.when(spot[2] == 1)
        def _():
            out_ref[e] = firsts[e][:rows, :]


def choose_ring(spot, firsts, seconds):
    shape = (PARTS,) + seconds[0].shape
    return pl.pallas_call(
        choose_ring_kernel,
        grid_spec=pltpu.PrefetchScalarGridSpec(
            num_scalar_prefetch=1,
            grid=(1,),
            in_specs=[whole(p.shape) for p in (*firsts, *seconds)],
            out_specs=whole(shape),
        ),
        out_shape=sds(shape, B16),
        compiler_params=params(),
        cost_estimate=cost(0, 4e6),
        name="choose_ring",
    )(spot, *firsts, *seconds)


def finish_kernel(spot, *refs):
    firsts, seconds, got_ref = refs[:PARTS], refs[PARTS : 2 * PARTS], refs[2 * PARTS]
    gate_ref, up_ref, down_ref, out_ref, qkv_ref, gain_ref, mine_ref = refs[2 * PARTS + 1 :]
    half = got_ref.shape[1]
    part = gate_ref.shape[0]
    for e in range(PARTS):

        @pl.when(pl.program_id(0) == e)
        def _():
            mine_ref[1 - spot[2]] = got_ref[e]
            n = qkv_ref.shape[1] // LANES
            for t in range(n):
                at = half + t * part
                qkv_ref[:, t * LANES : (t + 1) * LANES] = firsts[e][at : at + part, :].astype(F32)
            gain_ref[...] = firsts[e][half + n * part :, :].astype(F32)

            @pl.when(spot[2] == 0)
            def _():
                mine_ref[0] = firsts[e][:half, :]

            @pl.when(spot[2] == 1)
            def _():
                mine_ref[1] = seconds[e][...]

    at = 0
    for ref in (gate_ref, up_ref, down_ref, out_ref):
        rows = ref.shape[0]
        for t in range(ref.shape[1] // LANES):
            block = mine_ref[at // half, at % half : at % half + rows, :]
            ref[:, t * LANES : (t + 1) * LANES] = block.astype(F32)
            at += rows


def finish(spot, firsts, seconds, got, width, ff, q_width):
    part, cols, qkv_cols = width // PARTS, ff // PARTS, (q_width + 2 * HD) // PARTS

    def by_cols(n):
        return pl.BlockSpec((None, part, n), lambda i, spot: (0, 0, spot[0] ^ i))

    def by_rows(n):
        return pl.BlockSpec((None, n, width), lambda i, spot: (0, spot[0] ^ i, 0))

    return pl.pallas_call(
        finish_kernel,
        grid_spec=pltpu.PrefetchScalarGridSpec(
            num_scalar_prefetch=1,
            grid=(PARTS,),
            in_specs=[whole(p.shape) for p in (*firsts, *seconds, got)],
            out_specs=[
                by_cols(cols),
                by_cols(cols),
                by_rows(ff // PARTS**2),
                by_rows(q_width // PARTS**2),
                by_cols(qkv_cols),
                pl.BlockSpec((None, GAIN_ROWS, LANES), lambda i, spot: (spot[0] ^ i, 0, 0)),
            ],
            scratch_shapes=[pltpu.VMEM((2,) + seconds[0].shape, B16)],
        ),
        out_shape=[
            sds((1, part, ff), F32),
            sds((1, part, ff), F32),
            sds((1, ff // PARTS, width), F32),
            sds((1, q_width // PARTS, width), F32),
            sds((1, part, q_width + 2 * HD), F32),
            sds((PARTS, GAIN_ROWS, LANES), F32),
        ],
        compiler_params=params(),
        cost_estimate=cost(0, 12e6),
        name="finish",
    )(spot, *firsts, *seconds, got)


def split_pack(pack, width, ff, q_width):
    gate, down, out = pack_rows(width, ff, q_width)
    part = width // PARTS

    def cols(p):
        tiles = p.shape[2] // part
        return (
            p.reshape(PARTS, PARTS, tiles, part, LANES)
            .transpose(1, 3, 0, 2, 4)
            .reshape(width, PARTS * tiles * LANES)
        )

    def rows(p):
        n = p.shape[2] // (width // LANES)
        return (
            p.reshape(PARTS, PARTS, width // LANES, n, LANES)
            .transpose(1, 0, 3, 2, 4)
            .reshape(PARTS * PARTS * n, width)
        )

    return (
        cols(pack[:, :, :gate]),
        cols(pack[:, :, gate : 2 * gate]),
        rows(pack[:, :, 2 * gate : 2 * gate + down]),
        rows(pack[:, :, 2 * gate + down :]),
    )


def moved(array, axis, far, layer=None):
    sizes = [lax.axis_size(name) for name in AXES]
    pairs = []
    for s in range(sizes[0]) if layer is None else [layer]:
        for f in range(sizes[1]):
            for c in range(sizes[2]):
                f2 = f ^ far if axis == "fsdp" else f
                c2 = c ^ far if axis == "ctx" else c
                pairs.append(
                    ((s * sizes[1] + f) * sizes[2] + c, (s * sizes[1] + f2) * sizes[2] + c2)
                )
    return lax.ppermute(array, AXES, pairs)


def swapped(array):
    return lax.ppermute(array, "section", [(0, 1), (1, 0)])


def passed_along(array, by):
    devices = lax.axis_size("ctx")
    pairs = [(i, i + by) for i in range(devices) if 0 <= i + by < devices]
    return lax.ppermute(array, "ctx", pairs)


FAR = range(1, PARTS)


def other_shards(quarter, layer=None):
    return [moved(quarter, "fsdp", d, layer) for d in FAR]


def at(array, index):
    return lax.dynamic_index_in_dim(array, index, 0, keepdims=False)


def near_quarters(shards, layer=None):
    return moved(shards, "ctx", 1, layer), moved(shards, "ctx", 2, layer)


def far_quarter(near, deps=(), layer=None):
    one, two = near
    rows = one.shape[1]
    by_one = moved(joined([(one, 0, rows // 2)], *deps), "ctx", 2, layer)
    by_two = moved(joined([(two, rows // 2, rows)], *deps), "ctx", 1, layer)
    return jnp.concatenate([by_one, by_two], axis=1)


def ctx_near(split):
    return moved(split[1], "ctx", 1), moved(split[3], "ctx", 2)


def ctx_far(split, got, *deps):
    keep_a, _, keep_b, _ = split
    send_a, send_b = add_pairs(keep_a, got[0], keep_b, got[1], *deps)
    return moved(send_a, "ctx", 2), moved(send_b, "ctx", 1)


def fsdp_summed(parts, layer=None):
    total = parts[0].astype(F32)
    for d in FAR:
        total += moved(parts[d], "fsdp", d, layer).astype(F32)
    return total.astype(B16)


def ctx_ring(piece):
    return [piece] + [moved(piece, "ctx", e) for e in FAR]


def per_device(
    inputs,
    grad_out,
    lengths,
    in_gain,
    query_weight,
    key_weight,
    value_weight,
    query_gain,
    key_gain,
    out_weight,
    attn_gain,
    ffn_gain,
    gate_weight,
    up_weight,
    down_weight,
    post_gain,
):
    section = lax.axis_index("section")
    fsdp_index = lax.axis_index("fsdp")
    ctx_index = lax.axis_index("ctx")
    shards = lax.axis_size("fsdp")
    in_pieces = shards == PARTS and lax.axis_size("ctx") == PARTS
    tok = inputs.shape[2]
    width = inputs.shape[3]
    q_width = query_weight.shape[2]
    ff = gate_weight.shape[2]
    first_layer = section == 0

    qkv_own = jnp.concatenate([query_weight[0], key_weight[0], value_weight[0]], axis=1)
    gain_own = jnp.concatenate(
        [in_gain[0], attn_gain[0], ffn_gain[0], post_gain[0], query_gain[0], key_gain[0]]
    )

    def as_gains(raw):
        n, m = width // shards, HD // shards
        gd = [raw[:, i * n : (i + 1) * n].reshape(1, width) for i in range(4)]
        gh = [raw[:, 4 * n + i * m : 4 * n + (i + 1) * m].reshape(1, HD) for i in range(2)]
        gd = jnp.concatenate(gd + [jnp.zeros((4, width), raw.dtype)]).astype(F32)
        gh = jnp.concatenate(gh + [jnp.zeros((6, HD), raw.dtype)]).astype(F32)
        return gd, gh

    spot = jnp.stack([ctx_index, fsdp_index, section]).astype(jnp.int32)
    if in_pieces:
        gain_rows = jnp.pad(gain_own, (0, GAIN_ROWS * LANES - gain_own.shape[0]))
        gain_rows = gain_rows.reshape(GAIN_ROWS, LANES)
        ffn_parts = pack_ffn(gate_weight, up_weight, down_weight, out_weight)
        ffn_other = swapped(ffn_parts)
        qkv_parts, quarter = pack_qkv(
            spot, query_weight, key_weight, value_weight, gain_rows, ffn_parts
        )

        def arriving(layer, *deps):
            own = half_quarter(layer, spot, ffn_parts, ffn_other, *deps)
            return own, other_shards(own)

        first_own, first_arriving = arriving(0)
        shards_in = joined(other_shards(quarter), first_own)
        near = near_quarters(shards_in)
        pieces = joined([qkv_parts, shards_in, *near, far_quarter(near)])
        w_qkv, raw = place_qkv(spot, pieces, swapped(pieces), width, q_width + 2 * HD)
        raw = raw.reshape(2, PARTS, GAIN_ROWS * LANES)
        first_shards = joined(first_arriving, w_qkv)
        first_near = near_quarters(first_shards)
        _, second_arriving = arriving(1, first_shards)

        def place(layer, shards, near, *deps):
            far = far_quarter(near, deps)
            near = joined([shards, *near])
            pieces = [near, far, swapped(near), swapped(far)]
            gate, up, down, out = place_ffn(
                layer, spot, ffn_parts, ffn_other, pieces, width, ff, q_width
            )
            return out, gate, up, down

        def place_first(q, o):
            return place(0, first_shards, first_near, q)

        def place_second(q, o):
            shards = joined(second_arriving, kept[0][7])
            return place(1, shards, near_quarters(shards), kept[0][13])

        ffn_layers = [place_first, place_second]
    else:

        def whole_weight(own):
            full = lax.all_gather(own, "fsdp", axis=0, tiled=True)
            return lax.all_gather(full, "section", axis=0)

        full = [
            whole_weight(w)
            for w in (qkv_own, out_weight[0], gate_weight[0], up_weight[0], down_weight[0])
        ]
        w_qkv = full[0]
        raw = whole_weight(gain_own[None])
        ffn_layers = [lambda *deps, n=n: tuple(w[n] for w in full[1:]) for n in range(2)]

    def own_row(array):
        return lax.dynamic_index_in_dim(array[:, 0], section, 0, keepdims=False)

    offset, low = layout_for(own_row(lengths), ctx_index * tok, tok)
    cos, sin = rope_tables(offset)
    low_col, low_row = low[:, None], low[None, :]

    x = own_row(inputs)
    kept = []
    for layer in range(2):
        gd, gh = as_gains(raw[layer])
        a, kpre, near = kv_call(layer, x, gd, gh, cos, sin, w_qkv)
        far = passed_along(near, 1)
        qpre, q = q_call(layer, a, gh, cos, sin, w_qkv)
        o = attn_call(q, far, near, low_col)
        weights = ffn_layers[layer](q, o)
        y, h, g, u, z, result = ffn_call(o, x, gd, *weights)
        kept.append((x, a, kpre, near, far, qpre, q, o, y, h, g, u, z, result, gd, gh, weights))
        x = result

    spot_back = spot if in_pieces else jnp.zeros_like(spot)

    def layer_back(layer, cot, attn_deps, q_deps):
        x, a, kpre, near, far, qpre, q, o, y, h, g, u, z, result, gd, gh, weights = kept[layer]
        keep, send, dh, do, gd_part = ffn_back_call(spot_back, cot, z, h, y, o, gd, g, u, *weights)
        dq, dfar, dnear, gh_part = attn_back_call(
            q, do, qpre, far, near, low_row, gh, cos, sin, *attn_deps(keep, send)
        )
        dback = passed_along(dfar, -1)
        if tok > WINDOW:
            dback = jnp.pad(dback, ((tok - WINDOW, 0), (0, 0)))
        wq_grad, da = q_back_call(layer, a, dq, w_qkv, *q_deps(keep, send, dq))
        qkv_pack, dx = kv_back_call(
            layer, a, x, dh, da, dnear, dback, kpre, gd, gh, cos, sin, w_qkv, wq_grad,
            gd_part, gh_part,
        )
        return (keep, send), qkv_pack, dx

    cot = own_row(grad_out)
    if in_pieces:
        state = {}

        def split_second(keep, send, dq):
            state["split1"] = add_split(spot, keep, swapped(send))
            state["near1"] = ctx_near(state["split1"])
            return (state["split1"][0],)

        ffn_pack, qkv_pack, mid = layer_back(1, cot, lambda *_: (), split_second)

        def far_second(keep, send):
            state["far1"] = ctx_far(state["split1"], state["near1"], keep)
            return ()

        def split_first(keep, send, dq):
            parts = sum_parts(spot, state["split1"], state["near1"], state["far1"], dq)
            state["split0"] = add_split(spot, keep, swapped(send), dq)
            state["near0"] = ctx_near(state["split0"])
            state["ffn1"] = fsdp_summed(parts)
            return (state["split0"][0], parts[0])

        first_ffn_pack, first_qkv_pack, grad_in = layer_back(0, mid, far_second, split_first)
    else:
        ffn_pack, qkv_pack, mid = layer_back(1, cot, lambda *_: (), lambda *_: ())
        first_ffn_pack, first_qkv_pack, grad_in = layer_back(0, mid, lambda *_: (), lambda *_: ())
    packs = [(first_ffn_pack, first_qkv_pack), (ffn_pack, qkv_pack)]
    in_grads = [grad_in, mid]

    mine = jnp.stack([kept[0][13], in_grads[0]])
    others = jnp.stack([kept[1][13], in_grads[1]])
    got = swapped(jnp.where(first_layer, others, mine))
    mine = jnp.where(first_layer, mine, others)
    activations, input_grads = [
        jnp.stack([jnp.where(first_layer, mine[n], got[n]), jnp.where(first_layer, got[n], mine[n])])
        for n in range(2)
    ]

    if in_pieces:
        keep = jnp.where(first_layer, first_qkv_pack, qkv_pack)
        qkv_split = add_split(spot, keep, swapped(jnp.where(first_layer, qkv_pack, first_qkv_pack)))
        seconds = ctx_ring(state["ffn1"])
        far0 = ctx_far(state["split0"], state["near0"])
        ffn0 = fsdp_summed(sum_parts(spot, state["split0"], state["near0"], far0))
        qkv_near = ctx_near(qkv_split)
        qkv_far = ctx_far(qkv_split, qkv_near)
        qkv_own = fsdp_summed(sum_parts(spot, qkv_split, qkv_near, qkv_far))
        firsts = ctx_ring(jnp.concatenate([ffn0, qkv_own]))
        got = swapped(choose_ring(spot, firsts, seconds))
        gate_g, up_g, down_g, out_g, qkv_g, gain_sums = finish(
            spot, firsts, seconds, got, width, ff, q_width
        )
        gain_sums = gain_sums[:, : (4 * width + 2 * HD) // LANES // PARTS].reshape(-1)
    else:
        sums = []
        gain_sums = []
        for halves, qkv_pack in packs:
            ffn_pack = jnp.concatenate(halves, axis=2)
            gate, up, down, out = split_pack(ffn_pack, width, ff, q_width)
            part = width // PARTS
            n = (4 * width + 2 * HD) // LANES // PARTS
            gain_sums.append(qkv_pack[:, 0, -GAIN_ROWS:][:, :n].reshape(-1))
            qkv_pack = qkv_pack[:, :, :-GAIN_ROWS]
            tiles = qkv_pack.shape[2] // part
            qkv = (
                qkv_pack.reshape(PARTS, PARTS, tiles, part, LANES)
                .transpose(1, 3, 0, 2, 4)
                .reshape(width, -1)
            )
            sums.append((gate, up, down, out, qkv))
        shard = [
            lax.psum_scatter(
                lax.psum_scatter(jnp.stack(pair), "section", scatter_dimension=0, tiled=True)[0],
                "fsdp",
                scatter_dimension=0,
                tiled=True,
            )
            for pair in zip(*sums)
        ]
        gate_g, up_g, down_g, out_g, qkv_g = (
            w.astype(F32)[None] for w in lax.psum(tuple(shard), "ctx")
        )
        gain_sums = at(lax.psum(jnp.stack(gain_sums), AXES), section).astype(F32)

    def gain_shard(first, n):
        return lax.dynamic_slice_in_dim(gain_sums, first + fsdp_index * n, n, 0)[None]

    dn, hn = width // shards, HD // shards
    d_gains = [gain_shard(i * width, dn) for i in range(4)]
    h_gains = [gain_shard(4 * width + i * HD, hn) for i in range(2)]

    return (
        activations[None, :, None],
        input_grads[None, :, None],
        d_gains[0],
        qkv_g[:, :, :q_width],
        qkv_g[:, :, q_width : q_width + HD],
        qkv_g[:, :, q_width + HD :],
        h_gains[0],
        h_gains[1],
        out_g,
        d_gains[1],
        d_gains[2],
        gate_g,
        up_g,
        down_g,
        d_gains[3],
    )


def solution(mesh):
    return jax.shard_map(
        per_device,
        mesh=mesh,
        in_specs=(
            P(None, "fsdp", "ctx", None),
            P(None, "fsdp", "ctx", None),
            P(None, "fsdp", None),
            P("section", "fsdp"),
            P("section", "fsdp", None),
            P("section", "fsdp", None),
            P("section", "fsdp", None),
            P("section", "fsdp"),
            P("section", "fsdp"),
            P("section", "fsdp", None),
            P("section", "fsdp"),
            P("section", "fsdp"),
            P("section", "fsdp", None),
            P("section", "fsdp", None),
            P("section", "fsdp", None),
            P("section", "fsdp"),
        ),
        out_specs=(
            P("section", None, "fsdp", "ctx", None),
            P("section", None, "fsdp", "ctx", None),
            P("section", "fsdp"),
            P("section", "fsdp", None),
            P("section", "fsdp", None),
            P("section", "fsdp", None),
            P("section", "fsdp"),
            P("section", "fsdp"),
            P("section", "fsdp", None),
            P("section", "fsdp"),
            P("section", "fsdp"),
            P("section", "fsdp", None),
            P("section", "fsdp", None),
            P("section", "fsdp", None),
            P("section", "fsdp"),
        ),
        check_vma=False,
    )
```

```python
from functools import partial

import jax
import jax.numpy as jnp
from jax import lax
from jax.experimental import pallas as pl
from jax.experimental.pallas import tpu as pltpu
from jax.sharding import PartitionSpec as P

HD = 256
WINDOW = 512
EPS = 1e-06
LANES = 128
PARTS = 4
GAIN_ROWS = 32
QB = 128
F32 = jnp.float32
B16 = jnp.bfloat16
VMEM_LIMIT = 56 * 1024 * 1024
AXES = ("section", "fsdp", "ctx")


def rope_tables(offset):
    half_dim = HD // 2
    inv_freq = 10000.0 ** (-(jnp.arange(half_dim).astype(F32) * 2.0 / HD))
    angles = offset.astype(F32)[:, None] * inv_freq[None, :]
    return (jnp.cos(angles), jnp.sin(angles))


def layout_for(seq_lens, first_place, tok_count):
    seq_ends = jnp.cumsum(seq_lens)
    seq_starts = seq_ends - seq_lens
    places = first_place + jnp.arange(tok_count)
    segment = jnp.sum((places[:, None] >= seq_ends[None, :]).astype(jnp.int32), axis=1)
    labels = jnp.arange(seq_lens.shape[0])
    seg_hit = segment[:, None] == labels[None, :]
    start = jnp.sum(jnp.where(seg_hit, seq_starts[None, :], 0), axis=1)
    offset = places - start
    low = jnp.maximum(start, places - (WINDOW - 1)) - first_place + WINDOW
    return offset, low.astype(jnp.int32)


def dot(a, b):
    return lax.dot_general(a, b, (((1,), (0,)), ((), ())), preferred_element_type=F32)


def dot_nt(a, b):
    return lax.dot_general(a, b, (((1,), (1,)), ((), ())), preferred_element_type=F32)


def dot_tn(a, b):
    return lax.dot_general(a, b, (((0,), (0,)), ((), ())), preferred_element_type=F32)


def inv_rms(v):
    return lax.rsqrt(jnp.mean(v * v, axis=-1, keepdims=True) + EPS)


def rms_back(v, gain, grad):
    r = inv_rms(v)
    gg = grad * gain
    normed = v * r
    back = r * (gg - normed * jnp.mean(normed * gg, axis=-1, keepdims=True))
    return back, jnp.sum(grad * normed, axis=0, keepdims=True)


def rope(v, cos, sin):
    u, w = v[:, : HD // 2], v[:, HD // 2 :]
    return jnp.concatenate([u * cos - w * sin, w * cos + u * sin], axis=-1)


def rope_back(g, cos, sin):
    a, b = g[:, : HD // 2], g[:, HD // 2 :]
    return jnp.concatenate([a * cos + b * sin, b * cos - a * sin], axis=-1)


GELU_C = 0.7978845608028654
GELU_A = 0.044715


def gelu_parts(g):
    g2 = g * g
    t = jnp.tanh(GELU_C * g * (1.0 + GELU_A * g2))
    half = 0.5 * (1.0 + t)
    value = g * half
    slope = half + 0.5 * g * (1.0 - t * t) * (GELU_C * (1.0 + 3.0 * GELU_A * g2))
    return value, slope


def params(**kw):
    return pltpu.CompilerParams(vmem_limit_bytes=VMEM_LIMIT, **kw)


def cost(flops, nbytes):
    return pl.CostEstimate(flops=int(flops) * 30, bytes_accessed=int(nbytes), transcendentals=0)


def whole(shape):
    n = len(shape)
    return pl.BlockSpec(shape, lambda *i: (0,) * n)


def held_back(kernel, first, n):
    def body(*refs):
        kernel(*refs[:first], *refs[first + n :])

    return body


def sds(shape, dtype):
    return jax.ShapeDtypeStruct(shape, dtype)


def kv_kernel(x_ref, gd_ref, gh_ref, cos_ref, sin_ref, w_ref, a_ref, pre_ref, kv_ref):
    x = x_ref[...].astype(F32)
    a = (x * inv_rms(x) * gd_ref[0:1, :]).astype(B16)
    a_ref[...] = a
    both = dot(a, w_ref[...])
    pre = both[:, :HD]
    pre_ref[...] = pre.astype(B16)
    keys = rope(pre * inv_rms(pre) * gh_ref[1:2, :], cos_ref[...], sin_ref[...])
    kv_ref[:, :HD] = keys.astype(B16)
    kv_ref[:, HD:] = both[:, HD:].astype(B16)


def kv_call(layer, x, gd, gh, cos, sin, w_qkv):
    tok, width = x.shape
    q_width = w_qkv.shape[2] - 2 * HD
    return pl.pallas_call(
        kv_kernel,
        grid=(1,),
        in_specs=[
            whole(x.shape),
            whole(gd.shape),
            whole(gh.shape),
            whole(cos.shape),
            whole(sin.shape),
            pl.BlockSpec((None, width, 2 * HD), lambda j: (layer, 0, q_width // (2 * HD))),
        ],
        out_specs=[whole((tok, width)), whole((tok, HD)), whole((tok, 2 * HD))],
        out_shape=[sds((tok, width), B16), sds((tok, HD), B16), sds((tok, 2 * HD), B16)],
        compiler_params=params(),
        cost_estimate=cost(4 * tok * width * HD, 4e6),
        name="keys_values",
    )(x, gd, gh, cos, sin, w_qkv)


def q_kernel(a_ref, gh_ref, cos_ref, sin_ref, w_ref, pre_ref, q_ref):
    pre = dot(a_ref[...], w_ref[...])
    pre_ref[...] = pre.astype(B16)
    q_ref[...] = rope(pre * inv_rms(pre) * gh_ref[0:1, :], cos_ref[...], sin_ref[...]).astype(B16)


def q_call(layer, a, gh, cos, sin, w_qkv):
    tok, width = a.shape
    q_width = w_qkv.shape[2] - 2 * HD
    block = pl.BlockSpec((tok, HD), lambda j: (0, j))
    return pl.pallas_call(
        q_kernel,
        grid=(q_width // HD,),
        in_specs=[
            whole(a.shape),
            whole(gh.shape),
            whole(cos.shape),
            whole(sin.shape),
            pl.BlockSpec((None, width, HD), lambda j: (layer, 0, j)),
        ],
        out_specs=[block, block],
        out_shape=[sds((tok, q_width), B16), sds((tok, q_width), B16)],
        compiler_params=params(),
        cost_estimate=cost(2 * tok * width * q_width, 5e6),
        name="queries",
    )(a, gh, cos, sin, w_qkv)


SCORE_SCALE = HD ** (-0.5)


def attn_kernel(q_ref, far_ref, near_ref, low_ref, o_ref, kv_scr):
    b = pl.program_id(0)

    @pl.when(b == 0)
    def _():
        kv_scr[:WINDOW, :] = far_ref[...]
        kv_scr[WINDOW:, :] = near_ref[...]

    span = WINDOW + QB
    first = pl.multiple_of(b * QB, QB)
    keys = kv_scr[pl.ds(first, span), :HD]
    vals = kv_scr[pl.ds(first, span), HD:]
    col = lax.broadcasted_iota(jnp.int32, (QB, span), 1)
    row = lax.broadcasted_iota(jnp.int32, (QB, span), 0)
    allowed = (col >= low_ref[...] - b * QB) & (col <= row + WINDOW)
    for h in range(q_ref.shape[1] // HD):
        scores = dot_nt(q_ref[:, h * HD : (h + 1) * HD], keys) * SCORE_SCALE
        e = jnp.where(allowed, jnp.exp(scores), 0.0)
        total = jnp.sum(e, axis=1, keepdims=True)
        o_ref[:, h * HD : (h + 1) * HD] = (dot(e.astype(B16), vals) / total).astype(B16)


def attn_call(q, far, near, low, *deps):
    tok, q_width = q.shape
    return pl.pallas_call(
        held_back(attn_kernel, 4, len(deps)),
        grid=(tok // QB,),
        in_specs=[
            pl.BlockSpec((QB, q_width), lambda b: (b, 0)),
            whole(far.shape),
            whole(near.shape),
            pl.BlockSpec((QB, 1), lambda b: (b, 0)),
        ]
        + [pl.BlockSpec(memory_space=pl.ANY)] * len(deps),
        out_specs=pl.BlockSpec((QB, q_width), lambda b: (b, 0)),
        out_shape=sds((tok, q_width), B16),
        scratch_shapes=[pltpu.VMEM((WINDOW + tok, 2 * HD), B16)],
        compiler_params=params(),
        cost_estimate=cost(4 * tok * q_width * (WINDOW + QB), 3e6),
        name="attend",
    )(q, far, near, low, *deps)


FC = 512


def ffn_kernel(
    o_ref, x_ref, gd_ref, wo_ref, wg_ref, wu_ref, wd_ref,
    y_ref, h_ref, g_ref, u_ref, z_ref, out_ref, b_scr,
):
    j = pl.program_id(0)

    @pl.when(j == 0)
    def _():
        y = dot(o_ref[...], wo_ref[...])
        y_ref[...] = y
        h = x_ref[...].astype(F32) + y * inv_rms(y) * gd_ref[1:2, :]
        h_ref[...] = h
        b_scr[...] = (h * inv_rms(h) * gd_ref[2:3, :]).astype(B16)

    b = b_scr[...]
    g = dot(b, wg_ref[...])
    u = dot(b, wu_ref[...])
    g_ref[...] = g.astype(B16)
    u_ref[...] = u.astype(B16)
    value = g * 0.5 * (1.0 + jnp.tanh(GELU_C * g * (1.0 + GELU_A * g * g)))
    z = dot((value * u).astype(B16), wd_ref[...])

    @pl.when(j == 0)
    def _():
        z_ref[...] = z

    @pl.when(j > 0)
    def _():
        z_ref[...] += z

    @pl.when(j == pl.num_programs(0) - 1)
    def _():
        zz = z_ref[...]
        out_ref[...] = (h_ref[...] + zz * inv_rms(zz) * gd_ref[3:4, :]).astype(B16)


def ffn_call(o, x, gd, w_out, w_gate, w_up, w_down, *deps):
    tok, width = x.shape
    ff = w_gate.shape[1]
    cols = pl.BlockSpec((tok, FC), lambda j: (0, j))
    tw = whole((tok, width))
    return pl.pallas_call(
        held_back(ffn_kernel, 7, len(deps)),
        grid=(ff // FC,),
        in_specs=[
            whole(o.shape),
            tw,
            whole(gd.shape),
            whole(w_out.shape),
            pl.BlockSpec((width, FC), lambda j: (0, j)),
            pl.BlockSpec((width, FC), lambda j: (0, j)),
            pl.BlockSpec((FC, width), lambda j: (j, 0)),
        ]
        + [pl.BlockSpec(memory_space=pl.ANY)] * len(deps),
        out_specs=[tw, tw, cols, cols, tw, tw],
        out_shape=[
            sds((tok, width), F32),
            sds((tok, width), F32),
            sds((tok, ff), B16),
            sds((tok, ff), B16),
            sds((tok, width), F32),
            sds((tok, width), B16),
        ],
        scratch_shapes=[pltpu.VMEM((tok, width), B16)],
        compiler_params=params(),
        cost_estimate=cost(2 * tok * width * (o.shape[1] + 3 * ff), 22e6),
        name="feed_forward",
    )(o, x, gd, w_out, w_gate, w_up, w_down, *deps)


def ffn_back_kernel(
    spot, c_ref, z_ref, h_ref, y_ref, o_ref, gd_ref, g_ref, u_ref, wo_ref, wg_ref, wu_ref, wd_ref,
    keep_ref, send_ref, dh_ref, do_ref, gg_ref, dz_scr, bt_scr, db_scr,
):
    j = pl.program_id(0)
    half = keep_ref.shape[2]

    def put(blocks):
        for section in range(2):

            @pl.when(spot[2] == section)
            def _():
                for c_part, p, row, block in blocks:
                    ref = keep_ref if row // half == section else send_ref
                    ref[c_part, p, pl.ds(row % half, block.shape[0]), :] = block

    tok, width = c_ref.shape
    part = width // PARTS
    n_gate = PARTS * part
    n_down = (width // LANES) * (FC // PARTS)
    out_rows = o_ref.shape[1] // (PARTS * PARTS)

    @pl.when(j == 0)
    def _():
        dz, post_grad = rms_back(z_ref[...], gd_ref[3:4, :], c_ref[...].astype(F32))
        dz_scr[...] = dz.astype(B16)
        gg_ref[...] = jnp.zeros(gg_ref.shape, F32)
        gg_ref[3:4, :] = post_grad
        h = h_ref[...]
        bt_scr[...] = (h * inv_rms(h) * gd_ref[2:3, :]).T.astype(B16)
        db_scr[...] = jnp.zeros(db_scr.shape, F32)

    dz = dz_scr[...]
    df = dot_nt(dz, wd_ref[...])
    value, slope = gelu_parts(g_ref[...].astype(F32))
    u = u_ref[...].astype(F32)
    f = (value * u).astype(B16)
    du = (df * value).astype(B16)
    dg = (df * u * slope).astype(B16)
    db_scr[...] += dot_nt(dg, wg_ref[...]) + dot_nt(du, wu_ref[...])
    bt = bt_scr[...]
    blocks = []
    for first, term in ((0, dg), (n_gate, du)):
        grad = dot(bt, term).astype(B16)
        for p in range(PARTS):
            for t in range(FC // LANES):
                block = grad[p * part : (p + 1) * part, t * LANES : (t + 1) * LANES]
                blocks.append((j, p, first + t * part, block))
    grad = dot_tn(f, dz).astype(B16)
    rows = FC // PARTS
    for p in range(PARTS):
        for t in range(width // LANES):
            block = grad[p * rows : (p + 1) * rows, t * LANES : (t + 1) * LANES]
            blocks.append((p, j, 2 * n_gate + t * rows, block))
    put(blocks)

    @pl.when(j == pl.num_programs(0) - 1)
    def _():
        add, ffn_grad = rms_back(h_ref[...], gd_ref[2:3, :], db_scr[...])
        dh = c_ref[...].astype(F32) + add
        dh_ref[...] = dh
        dy32, attn_grad = rms_back(y_ref[...], gd_ref[1:2, :], dh)
        dy = dy32.astype(B16)
        gg_ref[1:2, :] = attn_grad
        gg_ref[2:3, :] = ffn_grad
        do_ref[...] = dot_nt(dy, wo_ref[...]).astype(B16)
        og = dot_tn(o_ref[...], dy).astype(B16)
        out_blocks = []
        for f_part in range(PARTS):
            for p in range(PARTS):
                at = (f_part * PARTS + p) * out_rows
                for t in range(width // LANES):
                    block = og[at : at + out_rows, t * LANES : (t + 1) * LANES]
                    out_blocks.append((p, f_part, 2 * n_gate + n_down + t * out_rows, block))
        put(out_blocks)


def pack_rows(width, ff, q_width):
    gate = width // PARTS * (ff // PARTS // LANES)
    down = ff // (PARTS * PARTS) * (width // LANES)
    out = q_width // (PARTS * PARTS) * (width // LANES)
    return gate, down, out


def ffn_back_call(spot, c, z, h, y, o, gd, g, u, w_out, w_gate, w_up, w_down):
    tok, width = c.shape
    ff = w_gate.shape[1]
    q_width = o.shape[1]
    gate, down, out = pack_rows(width, ff, q_width)
    pack_shape = (PARTS, PARTS, (2 * gate + down + out) // 2, LANES)
    cols = pl.BlockSpec((tok, FC), lambda j, *_: (0, j))
    tw = whole((tok, width))
    return pl.pallas_call(
        ffn_back_kernel,
        grid_spec=pltpu.PrefetchScalarGridSpec(
            num_scalar_prefetch=1,
            grid=(ff // FC,),
            in_specs=[
                tw,
                tw,
                tw,
                tw,
                whole(o.shape),
                whole(gd.shape),
                cols,
                cols,
                whole(w_out.shape),
                pl.BlockSpec((width, FC), lambda j, *_: (0, j)),
                pl.BlockSpec((width, FC), lambda j, *_: (0, j)),
                pl.BlockSpec((FC, width), lambda j, *_: (j, 0)),
            ],
            out_specs=[whole(pack_shape), whole(pack_shape), tw, whole(o.shape), whole(gd.shape)],
            scratch_shapes=[
                pltpu.VMEM((tok, width), B16),
                pltpu.VMEM((width, tok), B16),
                pltpu.VMEM((tok, width), F32),
            ],
        ),
        out_shape=[
            sds(pack_shape, B16),
            sds(pack_shape, B16),
            sds((tok, width), F32),
            sds(o.shape, B16),
            sds(gd.shape, F32),
        ],
        compiler_params=params(),
        cost_estimate=cost(4 * tok * width * (q_width + 3 * ff), 35e6),
        name="feed_forward_back",
    )(spot, c, z, h, y, o, gd, g, u, w_out, w_gate, w_up, w_down)


def attn_back_kernel(
    q_ref, do_ref, qpre_ref, far_ref, near_ref, low_ref, gh_ref, cos_ref, sin_ref,
    dq_ref, dfar_ref, dnear_ref, gg_ref, kv_scr, dkv_scr,
):
    b = pl.program_id(0)

    @pl.when(b == 0)
    def _():
        kv_scr[:WINDOW, :] = far_ref[...]
        kv_scr[WINDOW:, :] = near_ref[...]
        dkv_scr[...] = jnp.zeros(dkv_scr.shape, F32)
        gg_ref[...] = jnp.zeros(gg_ref.shape, F32)

    span = WINDOW + QB
    first = pl.multiple_of(b * QB, QB)
    keys = kv_scr[pl.ds(first, span), :HD]
    vals = kv_scr[pl.ds(first, span), HD:]
    col = lax.broadcasted_iota(jnp.int32, (span, QB), 0)
    row = lax.broadcasted_iota(jnp.int32, (span, QB), 1)
    allowed = (col >= low_ref[...] - b * QB) & (col <= row + WINDOW)
    cos, sin = cos_ref[...], sin_ref[...]
    dkeys = jnp.zeros((span, HD), F32)
    dvals = jnp.zeros((span, HD), F32)
    gain_grad = jnp.zeros((1, HD), F32)
    for h in range(q_ref.shape[1] // HD):
        at = slice(h * HD, (h + 1) * HD)
        q = q_ref[:, at]
        do = do_ref[:, at]
        scores = dot_nt(keys, q) * SCORE_SCALE
        e = jnp.where(allowed, jnp.exp(scores), 0.0)
        p = e * (1.0 / jnp.sum(e, axis=0, keepdims=True))
        dp = dot_nt(vals, do)
        inner = jnp.sum(p * dp, axis=0, keepdims=True)
        ds = (p * (dp - inner)).astype(B16)
        dvals += dot(p.astype(B16), do)
        dkeys += dot(ds, q)
        dq = dot_tn(ds, keys) * SCORE_SCALE
        dq0, gain = rms_back(qpre_ref[:, at].astype(F32), gh_ref[0:1, :], rope_back(dq, cos, sin))
        gain_grad += gain
        dq_ref[:, at] = dq0.astype(B16)
    dkv_scr[pl.ds(first, span), :HD] += dkeys * SCORE_SCALE
    dkv_scr[pl.ds(first, span), HD:] += dvals
    gg_ref[0:1, :] += gain_grad

    @pl.when(b == pl.num_programs(0) - 1)
    def _():
        dfar_ref[...] = dkv_scr[:WINDOW, :].astype(B16)
        dnear_ref[...] = dkv_scr[WINDOW:, :]


def attn_back_call(q, do, qpre, far, near, low_row, gh, cos, sin, *deps):
    tok, q_width = q.shape
    block = pl.BlockSpec((QB, q_width), lambda b: (b, 0))
    table = pl.BlockSpec((QB, HD // 2), lambda b: (b, 0))
    return pl.pallas_call(
        held_back(attn_back_kernel, 9, len(deps)),
        grid=(tok // QB,),
        in_specs=[
            block,
            block,
            block,
            whole(far.shape),
            whole(near.shape),
            pl.BlockSpec((1, QB), lambda b: (0, b)),
            whole(gh.shape),
            table,
            table,
        ]
        + [pl.BlockSpec(memory_space=pl.ANY)] * len(deps),
        out_specs=[block, whole(far.shape), whole(near.shape), whole(gh.shape)],
        out_shape=[
            sds(q.shape, B16),
            sds(far.shape, B16),
            sds(near.shape, F32),
            sds(gh.shape, F32),
        ],
        scratch_shapes=[
            pltpu.VMEM((WINDOW + tok, 2 * HD), B16),
            pltpu.VMEM((WINDOW + tok, 2 * HD), F32),
        ],
        compiler_params=params(),
        cost_estimate=cost(10 * tok * q_width * (WINDOW + QB), 8e6),
        name="attend_back",
    )(q, do, qpre, far, near, low_row, gh, cos, sin, *deps)


def q_back_kernel(a_ref, dq_ref, w_ref, wq_grad_ref, da_ref):
    dq = dq_ref[...]
    wq_grad_ref[...] = dot_tn(a_ref[...], dq).astype(B16)
    da_ref[...] = dot_nt(dq, w_ref[...])


def q_back_call(layer, a, dq, w_qkv, *deps):
    tok, width = a.shape
    q_width = dq.shape[1]
    return pl.pallas_call(
        held_back(q_back_kernel, 3, len(deps)),
        grid=(1,),
        in_specs=[
            whole(a.shape),
            whole(dq.shape),
            pl.BlockSpec((None, width, q_width), lambda j: (layer, 0, 0)),
        ]
        + [pl.BlockSpec(memory_space=pl.ANY)] * len(deps),
        out_specs=[whole((width, q_width)), whole((tok, width))],
        out_shape=[sds((width, q_width), B16), sds((tok, width), F32)],
        compiler_params=params(),
        cost_estimate=cost(4 * tok * width * q_width, 6e6),
        name="queries_back",
    )(a, dq, w_qkv, *deps)


def kv_back_kernel(
    a_ref, x_ref, dh_ref, da_ref, dnear_ref, dback_ref, kpre_ref, gd_ref, gh_ref,
    cos_ref, sin_ref, w_ref, wq_ref, gd_part_ref, gh_part_ref, pack_ref, dx_ref,
):
    width = x_ref.shape[1]
    part = width // PARTS
    dkv = dnear_ref[...]
    tail = dback_ref[...].astype(F32)
    dkv = dkv + tail
    dk0, k_grad = rms_back(
        kpre_ref[...].astype(F32),
        gh_ref[1:2, :],
        rope_back(dkv[:, :HD], cos_ref[...], sin_ref[...]),
    )
    both = jnp.concatenate([dk0.astype(B16), dkv[:, HD:].astype(B16)], axis=1)
    kv_grad = dot_tn(a_ref[...], both).astype(B16)
    da = da_ref[...] + dot_nt(both, w_ref[...])
    add, in_grad = rms_back(x_ref[...].astype(F32), gd_ref[0:1, :], da)
    dx_ref[...] = (dh_ref[...] + add).astype(B16)
    gains = [in_grad] + [gd_part_ref[i : i + 1, :] for i in range(1, 4)]
    gains += [gh_part_ref[0:1, :], k_grad]
    lines = [g[:, t : t + LANES] for g in gains for t in range(0, g.shape[1], LANES)]
    n = len(lines) // PARTS
    blank = jnp.zeros((GAIN_ROWS - n, LANES), F32)
    for c_part in range(PARTS):
        block = jnp.concatenate(lines[c_part * n : (c_part + 1) * n] + [blank]).astype(B16)
        for p in range(PARTS):
            pack_ref[c_part, p, pack_ref.shape[2] - GAIN_ROWS :, :] = block
    q_tiles = wq_ref.shape[1] // LANES
    tiles = q_tiles + 2 * HD // LANES
    each = tiles // PARTS
    for t in range(tiles):
        c_part, slot = t // each, t % each
        for p in range(PARTS):
            rows = slice(p * part, (p + 1) * part)
            if t < q_tiles:
                piece = wq_ref[rows, t * LANES : (t + 1) * LANES]
            else:
                piece = kv_grad[rows, (t - q_tiles) * LANES : (t - q_tiles + 1) * LANES]
            pack_ref[c_part, p, slot * part : (slot + 1) * part, :] = piece


def kv_back_call(
    layer, a, x, dh, da, dnear, dback, kpre, gd, gh, cos, sin, w_qkv, wq_grad, gd_part, gh_part,
    *deps,
):
    tok, width = a.shape
    q_width = wq_grad.shape[1]
    part = width // PARTS
    rows = part * ((q_width + 2 * HD) // LANES // PARTS) + GAIN_ROWS
    pack_shape = (PARTS, PARTS, rows, LANES)
    tw = whole((tok, width))
    return pl.pallas_call(
        held_back(kv_back_kernel, 15, len(deps)),
        grid=(1,),
        in_specs=[
            tw,
            tw,
            tw,
            tw,
            whole(dnear.shape),
            whole(dback.shape),
            whole(kpre.shape),
            whole(gd.shape),
            whole(gh.shape),
            whole(cos.shape),
            whole(sin.shape),
            pl.BlockSpec((None, width, 2 * HD), lambda j: (layer, 0, q_width // (2 * HD))),
            whole(wq_grad.shape),
            whole(gd.shape),
            whole(gh.shape),
        ]
        + [pl.BlockSpec(memory_space=pl.ANY)] * len(deps),
        out_specs=[whole(pack_shape), tw],
        out_shape=[sds(pack_shape, B16), sds((tok, width), B16)],
        compiler_params=params(),
        cost_estimate=cost(8 * tok * width * HD, 10e6),
        name="keys_values_back",
    )(a, x, dh, da, dnear, dback, kpre, gd, gh, cos, sin, w_qkv, wq_grad, gd_part, gh_part, *deps)


def pack_qkv_kernel(spot, q_ref, k_ref, v_ref, gain_ref, dep_ref, all_ref, own_ref):
    part = q_ref.shape[0]
    refs = [(r, t) for r in (q_ref, k_ref, v_ref) for t in range(r.shape[1] // LANES)]
    each = len(refs) // PARTS
    for n, (ref, t) in enumerate(refs):
        rows = slice(n % each * part, (n % each + 1) * part)
        all_ref[n // each, rows, :] = ref[:, t * LANES : (t + 1) * LANES]
    for c_part in range(PARTS):
        all_ref[c_part, each * part :, :] = gain_ref[...]
    own_ref[0] = all_ref[spot[0]]


def pack_qkv(spot, query, key, value, gains, dep):
    weights = (query, key, value)
    rows = sum(w.shape[2] for w in weights) // PARTS // LANES * query.shape[1] + GAIN_ROWS
    return pl.pallas_call(
        pack_qkv_kernel,
        grid_spec=pltpu.PrefetchScalarGridSpec(
            num_scalar_prefetch=1,
            grid=(1,),
            in_specs=[
                pl.BlockSpec((None,) + w.shape[1:], lambda i, spot: (0, 0, 0)) for w in weights
            ]
            + [whole(gains.shape), pl.BlockSpec(memory_space=pl.ANY)],
            out_specs=[whole((PARTS, rows, LANES)), whole((1, rows, LANES))],
        ),
        out_shape=[sds((PARTS, rows, LANES), B16), sds((1, rows, LANES), B16)],
        compiler_params=params(),
        cost_estimate=cost(0, 2e6),
        name="pack_qkv",
    )(spot, *weights, gains, dep)


def pack_ffn_kernel(gate_ref, up_ref, down_ref, out_ref, all_ref):
    at = 0
    for ref in (gate_ref, up_ref, down_ref, out_ref):
        rows = ref.shape[0]
        for t in range(ref.shape[1] // LANES):
            all_ref[at : at + rows, :] = ref[:, t * LANES : (t + 1) * LANES]
            at += rows


def pack_ffn(gate, up, down, out):
    by_cols = pl.BlockSpec(
        (None, gate.shape[1], gate.shape[2] // PARTS), lambda i: (0, 0, i)
    )

    def by_rows(w):
        return pl.BlockSpec((None, w.shape[1] // PARTS, w.shape[2]), lambda i: (0, i, 0))

    rows = sum(w.size for w in (gate, up, down, out)) // PARTS // LANES
    return pl.pallas_call(
        pack_ffn_kernel,
        grid=(PARTS,),
        in_specs=[by_cols, by_cols, by_rows(down), by_rows(out)],
        out_specs=pl.BlockSpec((None, rows, LANES), lambda i: (i, 0, 0)),
        out_shape=sds((PARTS, rows, LANES), B16),
        compiler_params=params(),
        cost_estimate=cost(0, 5e6),
        name="pack_ffn",
    )(gate, up, down, out)


def half_quarter_kernel(layer, spot, own_ref, other_ref, *refs):
    mine = spot[2] == layer

    @pl.when(mine)
    def _():
        refs[-1][...] = own_ref[...]

    @pl.when(jnp.logical_not(mine))
    def _():
        refs[-1][...] = other_ref[...]


def half_quarter(layer, spot, own, other, *deps):
    shape = (1, own.shape[1] // 2, LANES)
    block = pl.BlockSpec(shape, lambda i, spot: (spot[0], spot[2], 0))
    return pl.pallas_call(
        partial(half_quarter_kernel, layer),
        grid_spec=pltpu.PrefetchScalarGridSpec(
            num_scalar_prefetch=1,
            grid=(1,),
            in_specs=[block, block] + [pl.BlockSpec(memory_space=pl.ANY)] * len(deps),
            out_specs=pl.BlockSpec(shape, lambda i, spot: (0, 0, 0)),
        ),
        out_shape=sds(shape, B16),
        compiler_params=params(),
        cost_estimate=cost(0, 1e6),
        name="half_quarter",
    )(spot, own, other, *deps)


def joined(parts, *deps):
    parts = [p if isinstance(p, tuple) else (p, 0, p.shape[1]) for p in parts]
    counts = [p[0].shape[0] for p in parts]

    def body(*refs):
        at = 0
        for (array, low, high), ref in zip(parts, refs):
            refs[-1][at : at + array.shape[0]] = ref[:, low:high, :]
            at += array.shape[0]

    shape = (sum(counts), parts[0][2] - parts[0][1], LANES)
    return pl.pallas_call(
        body,
        in_specs=[pl.BlockSpec(memory_space=pltpu.VMEM)] * len(parts)
        + [pl.BlockSpec(memory_space=pl.ANY)] * len(deps),
        out_specs=pl.BlockSpec(memory_space=pltpu.VMEM),
        out_shape=sds(shape, B16),
        compiler_params=params(),
        cost_estimate=cost(0, 4 * shape[0] * shape[1] * LANES),
        name="joined",
    )(*[p[0] for p in parts], *deps)


def place_qkv_kernel(spot, own_ref, other_ref, w_ref, gain_ref):
    part = w_ref.shape[0] // PARTS
    each = w_ref.shape[1] // LANES // PARTS

    def take(ref):
        for c_part in range(PARTS):
            e = spot[0] ^ c_part
            for p in range(PARTS):
                d = spot[1] ^ p
                at = jnp.where(d == 0, c_part, PARTS + (PARTS - 1) * e + d - 1)
                for t in range(each):
                    lane = (c_part * each + t) * LANES
                    w_ref[p * part : (p + 1) * part, lane : lane + LANES] = ref[
                        at, t * part : (t + 1) * part, :
                    ]
                if c_part == 0:
                    gain_ref[p] = ref[at, ref.shape[1] - GAIN_ROWS :, :]

    pl.when(pl.program_id(0) == 0)(lambda: take(own_ref))
    pl.when(pl.program_id(0) == 1)(lambda: take(other_ref))


def place_qkv(spot, own, other, width, cols):
    everything = pl.BlockSpec(own.shape, lambda i, spot: (0, 0, 0))
    return pl.pallas_call(
        place_qkv_kernel,
        grid_spec=pltpu.PrefetchScalarGridSpec(
            num_scalar_prefetch=1,
            grid=(2,),
            in_specs=[everything, everything],
            out_specs=[
                pl.BlockSpec((None, width, cols), lambda i, spot: (spot[2] ^ i, 0, 0)),
                pl.BlockSpec(
                    (None, PARTS, GAIN_ROWS, LANES), lambda i, spot: (spot[2] ^ i, 0, 0, 0)
                ),
            ],
        ),
        out_shape=[sds((2, width, cols), B16), sds((2, PARTS, GAIN_ROWS, LANES), B16)],
        compiler_params=params(),
        cost_estimate=cost(0, 8e6),
        name="place_qkv",
    )(spot, own, other)


def place_ffn_kernel(
    layer, spot, own_ref, other_ref, near_ref, far_ref, got_near_ref, got_far_ref,
    gate_ref, up_ref, down_ref, out_ref, pieces, sems,
):
    step = pl.program_id(0)
    section = spot[2]
    last = PARTS * PARTS - PARTS + 1
    shard = pieces.at[:PARTS]
    copies = [
        pltpu.make_async_copy(near_ref, pieces.at[PARTS:last, section], sems.at[1]),
        pltpu.make_async_copy(got_near_ref, pieces.at[PARTS:last, 1 - section], sems.at[2]),
        pltpu.make_async_copy(far_ref, pieces.at[last:, section], sems.at[3]),
        pltpu.make_async_copy(got_far_ref, pieces.at[last:, 1 - section], sems.at[4]),
    ]

    def shard_copy(do):
        pl.when(section == layer)(lambda: do(pltpu.make_async_copy(own_ref, shard, sems.at[0])))
        pl.when(section != layer)(lambda: do(pltpu.make_async_copy(other_ref, shard, sems.at[0])))

    @pl.when(step == 0)
    def _():
        shard_copy(lambda copy: copy.start())
        for copy in copies:
            copy.start()
        shard_copy(lambda copy: copy.wait())
        copies[0].wait()
        copies[1].wait()

    @pl.when(step == PARTS - 1)
    def _():
        copies[2].wait()
        copies[3].wait()

    width, cols = gate_ref.shape
    part = width // PARTS
    half = pieces.shape[2]
    c_part = spot[0] ^ step
    for p in range(PARTS):
        d = spot[1] ^ p
        index = jnp.where(d == 0, c_part, PARTS + (PARTS - 1) * step + d - 1)

        def piece(at, n):
            return pieces[index, at // half, at % half : at % half + n, :]

        at = 0
        for w_ref in (gate_ref, up_ref):
            for t in range(cols // LANES):
                w_ref[p * part : (p + 1) * part, t * LANES : (t + 1) * LANES] = piece(at, part)
                at += part
        for w_ref in (down_ref, out_ref):
            rows = w_ref.shape[2]
            for t in range(width // LANES):
                w_ref[p, 0, :, t * LANES : (t + 1) * LANES] = piece(at, rows)
                at += rows


def place_ffn(layer, spot, own, other, pieces, width, ff, q_width):
    cols = pl.BlockSpec((width, ff // PARTS), lambda i, spot: (0, spot[0] ^ i))

    def rows(n):
        return pl.BlockSpec(
            (PARTS, 1, n // PARTS**2, width), lambda i, spot: (0, spot[0] ^ i, 0, 0)
        )

    half = own.shape[1] // 2
    shard = (PARTS, 2, half, LANES)
    gate, up, down, out = pl.pallas_call(
        partial(place_ffn_kernel, layer),
        grid_spec=pltpu.PrefetchScalarGridSpec(
            num_scalar_prefetch=1,
            grid=(PARTS,),
            in_specs=[pl.BlockSpec(memory_space=pl.ANY)] * 6,
            out_specs=[cols, cols, rows(ff), rows(q_width)],
            scratch_shapes=[
                pltpu.VMEM((PARTS * PARTS, 2, half, LANES), B16),
                pltpu.SemaphoreType.DMA((5,)),
            ],
        ),
        out_shape=[
            sds((width, ff), B16),
            sds((width, ff), B16),
            sds((PARTS, PARTS, ff // PARTS**2, width), B16),
            sds((PARTS, PARTS, q_width // PARTS**2, width), B16),
        ],
        compiler_params=params(),
        cost_estimate=cost(0, 18e6),
        name="place_ffn",
    )(spot, own.reshape(shard), other.reshape(shard), *pieces)
    return gate, up, down.reshape(ff, width), out.reshape(q_width, width)


def add_split_kernel(spot, first_ref, second_ref, *refs):
    keep_a, send_a, keep_b, send_b = refs[-PARTS:]
    half = first_ref.shape[1] // 2
    a, b = slice(0, half), slice(half, 2 * half)
    for rows, far, out, n in (
        (a, 0, keep_a, 0), (a, 2, keep_a, 1), (a, 1, send_a, 0), (a, 3, send_a, 1),
        (b, 0, keep_b, 0), (b, 1, keep_b, 1), (b, 2, send_b, 0), (b, 3, send_b, 1),
    ):
        c_part = spot[0] ^ far
        total = first_ref[c_part, rows, :].astype(F32) + second_ref[c_part, rows, :].astype(F32)
        out[n] = total.astype(B16)


def add_split(spot, first, second, *deps):
    n = first.shape[2]
    block = pl.BlockSpec((PARTS, None, n, LANES), lambda i, spot: (0, i, 0, 0))
    out = pl.BlockSpec((2, None, n // 2, LANES), lambda i, spot: (0, i, 0, 0))
    return pl.pallas_call(
        add_split_kernel,
        grid_spec=pltpu.PrefetchScalarGridSpec(
            num_scalar_prefetch=1,
            grid=(PARTS,),
            in_specs=[block, block] + [pl.BlockSpec(memory_space=pl.ANY)] * len(deps),
            out_specs=[out] * PARTS,
        ),
        out_shape=[sds((2, PARTS, n // 2, LANES), B16)] * PARTS,
        compiler_params=params(),
        cost_estimate=cost(0, 3 * 2 * first.size),
        name="add_split",
    )(spot, first, second, *deps)


def add_pairs_kernel(a_ref, b_ref, c_ref, d_ref, *refs):
    refs[-2][...] = (a_ref[...].astype(F32) + b_ref[...].astype(F32)).astype(B16)
    refs[-1][...] = (c_ref[...].astype(F32) + d_ref[...].astype(F32)).astype(B16)


def add_pairs(a, b, c, d, *deps):
    shape = a.shape[1:]
    return pl.pallas_call(
        add_pairs_kernel,
        grid=(1,),
        in_specs=[pl.BlockSpec((None,) + shape, lambda i: (1, 0, 0, 0))] * 4
        + [pl.BlockSpec(memory_space=pl.ANY)] * len(deps),
        out_specs=[whole(shape)] * 2,
        out_shape=[sds(shape, B16)] * 2,
        compiler_params=params(),
        cost_estimate=cost(0, 6 * a.size),
        name="add_pairs",
    )(a, b, c, d, *deps)


def sum_pairs_kernel(spot, a0, a1, a2, b0, b1, b2, *refs):
    sum_parts_kernel(
        spot, a0, a1, a2, b0, b1, b2,
        refs[-2].at[0], refs[-1].at[0], refs[-2].at[1], refs[-1].at[1],
    )


def sum_parts_kernel(spot, a0, a1, a2, b0, b1, b2, *refs):
    outs = refs[-PARTS:]
    half = a0.shape[1]
    for d in range(PARTS):
        f = spot[1] ^ d
        for rows, terms in ((slice(0, half), (a0, a1, a2)), (slice(half, 2 * half), (b0, b1, b2))):
            total = sum(term[f].astype(F32) for term in terms)
            outs[d][rows, :] = total.astype(B16)


def sum_parts(spot, split, got, last, *deps, pairs=False):
    keep_a, _, keep_b, _ = split
    shape = keep_a.shape[1:]
    first = pl.BlockSpec((None,) + shape, lambda i, spot: (0, 0, 0, 0))
    one = whole(shape)
    out = ((2,) if pairs else ()) + (2 * shape[1], LANES)
    count = 2 if pairs else PARTS
    return pl.pallas_call(
        sum_pairs_kernel if pairs else sum_parts_kernel,
        grid_spec=pltpu.PrefetchScalarGridSpec(
            num_scalar_prefetch=1,
            grid=(1,),
            in_specs=[first, first, one] * 2 + [pl.BlockSpec(memory_space=pl.ANY)] * len(deps),
            out_specs=[whole(out)] * count,
        ),
        out_shape=[sds(out, B16)] * count,
        compiler_params=params(),
        cost_estimate=cost(0, 10 * keep_a.size),
        name="sum_parts",
    )(spot, keep_a, got[0], last[0], keep_b, got[1], last[1], *deps)


def choose_ring_kernel(spot, *refs):
    firsts, seconds, out_ref = refs[:PARTS], refs[PARTS : 2 * PARTS], refs[-1]
    rows = out_ref.shape[1]
    for e in range(PARTS):

        @pl.when(spot[2] == 0)
        def _():
            out_ref[e] = seconds[e][...]

        @pl.when(spot[2] == 1)
        def _():
            out_ref[e] = firsts[e][:rows, :]


def choose_ring(spot, firsts, seconds):
    shape = (PARTS,) + seconds[0].shape
    return pl.pallas_call(
        choose_ring_kernel,
        grid_spec=pltpu.PrefetchScalarGridSpec(
            num_scalar_prefetch=1,
            grid=(1,),
            in_specs=[whole(p.shape) for p in (*firsts, *seconds)],
            out_specs=whole(shape),
        ),
        out_shape=sds(shape, B16),
        compiler_params=params(),
        cost_estimate=cost(0, 4e6),
        name="choose_ring",
    )(spot, *firsts, *seconds)


def finish_kernel(spot, *refs):
    firsts, seconds, got_ref = refs[:PARTS], refs[PARTS : 2 * PARTS], refs[2 * PARTS]
    gate_ref, up_ref, down_ref, out_ref, q_ref, k_ref, v_ref, gain_ref, mine_ref = refs[
        2 * PARTS + 1 :
    ]
    places = [(ref, t) for ref in (q_ref, k_ref, v_ref) for t in range(ref.shape[1] // LANES)]
    n = len(places) // PARTS
    half = got_ref.shape[1]
    part = gate_ref.shape[0]
    for e in range(PARTS):

        @pl.when(pl.program_id(0) == e)
        def _():
            mine_ref[1 - spot[2]] = got_ref[e]
            for c_part in range(PARTS):

                @pl.when(spot[0] ^ e == c_part)
                def _():
                    for t in range(n):
                        ref, tile = places[c_part * n + t]
                        block = firsts[e][half + t * part : half + (t + 1) * part, :]
                        ref[:, tile * LANES : (tile + 1) * LANES] = block.astype(F32)

            gain_ref[...] = firsts[e][half + n * part :, :].astype(F32)

            @pl.when(spot[2] == 0)
            def _():
                mine_ref[0] = firsts[e][:half, :]

            @pl.when(spot[2] == 1)
            def _():
                mine_ref[1] = seconds[e][...]

    at = 0
    for ref in (gate_ref, up_ref, down_ref, out_ref):
        rows = ref.shape[0]
        for t in range(ref.shape[1] // LANES):
            block = mine_ref[at // half, at % half : at % half + rows, :]
            ref[:, t * LANES : (t + 1) * LANES] = block.astype(F32)
            at += rows


def finish(spot, firsts, seconds, got, width, ff, q_width):
    part, cols = width // PARTS, ff // PARTS

    def by_cols(n):
        return pl.BlockSpec((None, part, n), lambda i, spot: (0, 0, spot[0] ^ i))

    def by_rows(n):
        return pl.BlockSpec((None, n, width), lambda i, spot: (0, spot[0] ^ i, 0))

    return pl.pallas_call(
        finish_kernel,
        grid_spec=pltpu.PrefetchScalarGridSpec(
            num_scalar_prefetch=1,
            grid=(PARTS,),
            in_specs=[whole(p.shape) for p in (*firsts, *seconds, got)],
            out_specs=[
                by_cols(cols),
                by_cols(cols),
                by_rows(ff // PARTS**2),
                by_rows(q_width // PARTS**2),
                *[
                    pl.BlockSpec((None, part, n), lambda i, spot: (0, 0, 0))
                    for n in (q_width, HD, HD)
                ],
                pl.BlockSpec((None, GAIN_ROWS, LANES), lambda i, spot: (spot[0] ^ i, 0, 0)),
            ],
            scratch_shapes=[pltpu.VMEM((2,) + seconds[0].shape, B16)],
        ),
        out_shape=[
            sds((1, part, ff), F32),
            sds((1, part, ff), F32),
            sds((1, ff // PARTS, width), F32),
            sds((1, q_width // PARTS, width), F32),
            *[sds((1, part, n), F32) for n in (q_width, HD, HD)],
            sds((PARTS, GAIN_ROWS, LANES), F32),
        ],
        compiler_params=params(),
        cost_estimate=cost(0, 12e6),
        name="finish",
    )(spot, *firsts, *seconds, got)


def split_pack(pack, width, ff, q_width):
    gate, down, out = pack_rows(width, ff, q_width)
    part = width // PARTS

    def cols(p):
        tiles = p.shape[2] // part
        return (
            p.reshape(PARTS, PARTS, tiles, part, LANES)
            .transpose(1, 3, 0, 2, 4)
            .reshape(width, PARTS * tiles * LANES)
        )

    def rows(p):
        n = p.shape[2] // (width // LANES)
        return (
            p.reshape(PARTS, PARTS, width // LANES, n, LANES)
            .transpose(1, 0, 3, 2, 4)
            .reshape(PARTS * PARTS * n, width)
        )

    return (
        cols(pack[:, :, :gate]),
        cols(pack[:, :, gate : 2 * gate]),
        rows(pack[:, :, 2 * gate : 2 * gate + down]),
        rows(pack[:, :, 2 * gate + down :]),
    )


def moved(array, axis, far, layer=None):
    sizes = [lax.axis_size(name) for name in AXES]
    pairs = []
    for s in range(sizes[0]) if layer is None else [layer]:
        for f in range(sizes[1]):
            for c in range(sizes[2]):
                f2 = f ^ far if axis == "fsdp" else f
                c2 = c ^ far if axis == "ctx" else c
                pairs.append(
                    ((s * sizes[1] + f) * sizes[2] + c, (s * sizes[1] + f2) * sizes[2] + c2)
                )
    return lax.ppermute(array, AXES, pairs)


def swapped(array):
    return lax.ppermute(array, "section", [(0, 1), (1, 0)])


def passed_along(array, by):
    devices = lax.axis_size("ctx")
    pairs = [(i, i + by) for i in range(devices) if 0 <= i + by < devices]
    return lax.ppermute(array, "ctx", pairs)


FAR = range(1, PARTS)


def other_shards(quarter, layer=None):
    return [moved(quarter, "fsdp", d, layer) for d in FAR]


def at(array, index):
    return lax.dynamic_index_in_dim(array, index, 0, keepdims=False)


def near_quarters(shards, layer=None):
    return moved(shards, "ctx", 1, layer), moved(shards, "ctx", 2, layer)


def near_halves(near, *deps):
    one, two = near
    rows = one.shape[1]
    return joined([(one, 0, rows // 2)], *deps), joined([(two, rows // 2, rows)], *deps)


def far_quarter(halves):
    by_one = moved(halves[0], "ctx", 2)
    by_two = moved(halves[1], "ctx", 1)
    return jnp.concatenate([by_one, by_two], axis=1)


def ctx_near(split):
    return moved(split[1], "ctx", 1), moved(split[3], "ctx", 2)


def far_sends(split, got, *deps):
    keep_a, _, keep_b, _ = split
    return add_pairs(keep_a, got[0], keep_b, got[1], *deps)


def ctx_far(sends):
    send_a, send_b = sends
    return moved(send_a, "ctx", 2), moved(send_b, "ctx", 1)


def fsdp_summed(parts, layer=None):
    total = parts[0].astype(F32)
    for d in FAR:
        total += moved(parts[d], "fsdp", d, layer).astype(F32)
    return total.astype(B16)


def fsdp_summed_in_two(keep, send):
    got = moved(send, "fsdp", 1)

    def both(n):
        return keep[n].astype(F32) + got[n].astype(F32)

    last = moved(both(1).astype(B16), "fsdp", 2)
    return (both(0) + last.astype(F32)).astype(B16)


def ctx_ring(piece):
    return [piece] + [moved(piece, "ctx", e) for e in FAR]


def per_device(
    inputs,
    grad_out,
    lengths,
    in_gain,
    query_weight,
    key_weight,
    value_weight,
    query_gain,
    key_gain,
    out_weight,
    attn_gain,
    ffn_gain,
    gate_weight,
    up_weight,
    down_weight,
    post_gain,
):
    section = lax.axis_index("section")
    fsdp_index = lax.axis_index("fsdp")
    ctx_index = lax.axis_index("ctx")
    shards = lax.axis_size("fsdp")
    in_pieces = shards == PARTS and lax.axis_size("ctx") == PARTS
    tok = inputs.shape[2]
    width = inputs.shape[3]
    q_width = query_weight.shape[2]
    ff = gate_weight.shape[2]
    first_layer = section == 0

    qkv_own = jnp.concatenate([query_weight[0], key_weight[0], value_weight[0]], axis=1)
    gain_own = jnp.concatenate(
        [in_gain[0], attn_gain[0], ffn_gain[0], post_gain[0], query_gain[0], key_gain[0]]
    )

    def as_gains(raw):
        n, m = width // shards, HD // shards
        gd = [raw[:, i * n : (i + 1) * n].reshape(1, width) for i in range(4)]
        gh = [raw[:, 4 * n + i * m : 4 * n + (i + 1) * m].reshape(1, HD) for i in range(2)]
        gd = jnp.concatenate(gd + [jnp.zeros((4, width), raw.dtype)]).astype(F32)
        gh = jnp.concatenate(gh + [jnp.zeros((6, HD), raw.dtype)]).astype(F32)
        return gd, gh

    def own_row(array):
        return lax.dynamic_index_in_dim(array[:, 0], section, 0, keepdims=False)

    offset, low = layout_for(own_row(lengths), ctx_index * tok, tok)
    cos, sin = rope_tables(offset)
    low_col, low_row = low[:, None], low[None, :]

    spot = jnp.stack([ctx_index, fsdp_index, section]).astype(jnp.int32)
    if in_pieces:
        gain_rows = jnp.pad(gain_own, (0, GAIN_ROWS * LANES - gain_own.shape[0]))
        gain_rows = gain_rows.reshape(GAIN_ROWS, LANES)
        ffn_parts = pack_ffn(gate_weight, up_weight, down_weight, out_weight)
        ffn_other = swapped(ffn_parts)
        qkv_parts, quarter = pack_qkv(
            spot, query_weight, key_weight, value_weight, gain_rows, ffn_parts
        )

        def arriving(layer, *deps):
            own = half_quarter(layer, spot, ffn_parts, ffn_other, *deps)
            return own, other_shards(own)

        first_own, first_arriving = arriving(0)
        shards_in = joined(other_shards(quarter), first_own, *first_arriving[:2])
        near = near_quarters(shards_in)
        far = far_quarter(near_halves(near, first_arriving[2]))
        pieces = joined(
            [qkv_parts, shards_in, *near, far], *first_arriving, cos, sin, low_col
        )
        w_qkv, raw = place_qkv(spot, pieces, swapped(pieces), width, q_width + 2 * HD)
        raw = raw.reshape(2, PARTS, GAIN_ROWS * LANES)
        first_shards = joined(first_arriving, pieces)
        first_near = near_quarters(first_shards)
        _, second_arriving = arriving(1, first_shards)

        def other_half(shards, near, far):
            near = joined([shards, *near])
            return near, far, swapped(near), swapped(far)

        state = {}

        def before_attend(layer, q):
            if layer == 0:
                far = far_quarter(near_halves(first_near, q, *second_arriving))
                state["pieces"] = other_half(first_shards, first_near, far)
                return second_arriving
            far = far_quarter(state["halves"])
            state["pieces"] = other_half(*state["shards"], far)
            return (far,)

        def before_ffn(layer, o, gate):
            if layer == 1:
                return ()
            shards = joined(second_arriving, o)
            near = near_quarters(shards)
            state["shards"] = (shards, near)
            state["halves"] = near_halves(near, gate)
            return ()

        def place(layer):
            gate, up, down, out = place_ffn(
                layer, spot, ffn_parts, ffn_other, state["pieces"], width, ff, q_width
            )
            return out, gate, up, down

    else:

        def whole_weight(own):
            full = lax.all_gather(own, "fsdp", axis=0, tiled=True)
            return lax.all_gather(full, "section", axis=0)

        full = [
            whole_weight(w)
            for w in (qkv_own, out_weight[0], gate_weight[0], up_weight[0], down_weight[0])
        ]
        w_qkv = full[0]
        raw = whole_weight(gain_own[None])

        def place(layer):
            return tuple(w[layer] for w in full[1:])

        def before_attend(layer, q):
            return ()

        def before_ffn(layer, o, gate):
            return ()


    x = own_row(inputs)
    kept = []
    for layer in range(2):
        gd, gh = as_gains(raw[layer])
        a, kpre, near = kv_call(layer, x, gd, gh, cos, sin, w_qkv)
        far = passed_along(near, 1)
        qpre, q = q_call(layer, a, gh, cos, sin, w_qkv)
        o = attn_call(q, far, near, low_col, *before_attend(layer, q))
        weights = place(layer)
        y, h, g, u, z, result = ffn_call(o, x, gd, *weights, *before_ffn(layer, o, weights[1]))
        kept.append((x, a, kpre, near, far, qpre, q, o, y, h, g, u, z, result, gd, gh, weights))
        x = result

    spot_back = spot if in_pieces else jnp.zeros_like(spot)

    def layer_back(layer, cot, attn_deps, q_deps, kv_deps):
        x, a, kpre, near, far, qpre, q, o, y, h, g, u, z, result, gd, gh, weights = kept[layer]
        keep, send, dh, do, gd_part = ffn_back_call(spot_back, cot, z, h, y, o, gd, g, u, *weights)
        dq, dfar, dnear, gh_part = attn_back_call(
            q, do, qpre, far, near, low_row, gh, cos, sin, *attn_deps(keep, send)
        )
        dback = passed_along(dfar, -1)
        if tok > WINDOW:
            dback = jnp.pad(dback, ((tok - WINDOW, 0), (0, 0)))
        wq_grad, da = q_back_call(layer, a, dq, w_qkv, *q_deps(keep, send, dq))
        qkv_pack, dx = kv_back_call(
            layer, a, x, dh, da, dnear, dback, kpre, gd, gh, cos, sin, w_qkv, wq_grad,
            gd_part, gh_part, *kv_deps(),
        )
        return (keep, send), qkv_pack, dx

    cot = own_row(grad_out)
    if in_pieces:
        def split_second(keep, send, dq):
            state["split1"] = add_split(spot, keep, swapped(send))
            state["near1"] = ctx_near(state["split1"])
            return (state["split1"][0],)

        ffn_pack, qkv_pack, mid = layer_back(1, cot, lambda *_: (), split_second, lambda: ())

        def far_second(keep, send):
            sends = far_sends(state["split1"], state["near1"], keep)
            state["far1"] = ctx_far(sends)
            return (sends[0],)

        def split_first(keep, send, dq):
            state["split0"] = add_split(spot, keep, swapped(send), dq)
            state["near0"] = ctx_near(state["split0"])
            parts = sum_parts(
                spot, state["split1"], state["near1"], state["far1"], state["split0"][0], pairs=True
            )
            state["ffn1"] = fsdp_summed_in_two(*parts)
            return (parts[0],)

        def far_first():
            state["sends0"] = far_sends(state["split0"], state["near0"])
            return (state["sends0"][0],)

        first_ffn_pack, first_qkv_pack, grad_in = layer_back(
            0, mid, far_second, split_first, far_first
        )
    else:
        ffn_pack, qkv_pack, mid = layer_back(1, cot, *[lambda *_: ()] * 3)
        first_ffn_pack, first_qkv_pack, grad_in = layer_back(0, mid, *[lambda *_: ()] * 3)
    packs = [(first_ffn_pack, first_qkv_pack), (ffn_pack, qkv_pack)]
    in_grads = [grad_in, mid]

    mine = jnp.stack([kept[0][13], in_grads[0]])
    others = jnp.stack([kept[1][13], in_grads[1]])
    got = swapped(jnp.where(first_layer, others, mine))
    mine = jnp.where(first_layer, mine, others)
    activations, input_grads = [
        jnp.stack([jnp.where(first_layer, mine[n], got[n]), jnp.where(first_layer, got[n], mine[n])])
        for n in range(2)
    ]

    if in_pieces:
        keep = jnp.where(first_layer, first_qkv_pack, qkv_pack)
        qkv_split = add_split(spot, keep, swapped(jnp.where(first_layer, qkv_pack, first_qkv_pack)))
        seconds = ctx_ring(state["ffn1"])
        far0 = ctx_far(state["sends0"])
        ffn0 = fsdp_summed(sum_parts(spot, state["split0"], state["near0"], far0))
        qkv_near = ctx_near(qkv_split)
        qkv_far = ctx_far(far_sends(qkv_split, qkv_near))
        qkv_own = fsdp_summed(sum_parts(spot, qkv_split, qkv_near, qkv_far))
        firsts = ctx_ring(jnp.concatenate([ffn0, qkv_own]))
        got = swapped(choose_ring(spot, firsts, seconds))
        gate_g, up_g, down_g, out_g, q_g, k_g, v_g, gain_sums = finish(
            spot, firsts, seconds, got, width, ff, q_width
        )
        gain_sums = gain_sums[:, : (4 * width + 2 * HD) // LANES // PARTS].reshape(-1)
    else:
        sums = []
        gain_sums = []
        for halves, qkv_pack in packs:
            ffn_pack = jnp.concatenate(halves, axis=2)
            gate, up, down, out = split_pack(ffn_pack, width, ff, q_width)
            part = width // PARTS
            n = (4 * width + 2 * HD) // LANES // PARTS
            gain_sums.append(qkv_pack[:, 0, -GAIN_ROWS:][:, :n].reshape(-1))
            qkv_pack = qkv_pack[:, :, :-GAIN_ROWS]
            tiles = qkv_pack.shape[2] // part
            qkv = (
                qkv_pack.reshape(PARTS, PARTS, tiles, part, LANES)
                .transpose(1, 3, 0, 2, 4)
                .reshape(width, -1)
            )
            sums.append((gate, up, down, out, qkv))
        shard = [
            lax.psum_scatter(
                lax.psum_scatter(jnp.stack(pair), "section", scatter_dimension=0, tiled=True)[0],
                "fsdp",
                scatter_dimension=0,
                tiled=True,
            )
            for pair in zip(*sums)
        ]
        gate_g, up_g, down_g, out_g, qkv_g = (
            w.astype(F32)[None] for w in lax.psum(tuple(shard), "ctx")
        )
        q_g, k_g, v_g = jnp.split(qkv_g, [q_width, q_width + HD], axis=2)
        gain_sums = at(lax.psum(jnp.stack(gain_sums), AXES), section).astype(F32)

    def gain_shard(first, n):
        return lax.dynamic_slice_in_dim(gain_sums, first + fsdp_index * n, n, 0)[None]

    dn, hn = width // shards, HD // shards
    d_gains = [gain_shard(i * width, dn) for i in range(4)]
    h_gains = [gain_shard(4 * width + i * HD, hn) for i in range(2)]

    return (
        activations[None, :, None],
        input_grads[None, :, None],
        d_gains[0],
        q_g,
        k_g,
        v_g,
        h_gains[0],
        h_gains[1],
        out_g,
        d_gains[1],
        d_gains[2],
        gate_g,
        up_g,
        down_g,
        d_gains[3],
    )


def solution(mesh):
    return jax.shard_map(
        per_device,
        mesh=mesh,
        in_specs=(
            P(None, "fsdp", "ctx", None),
            P(None, "fsdp", "ctx", None),
            P(None, "fsdp", None),
            P("section", "fsdp"),
            P("section", "fsdp", None),
            P("section", "fsdp", None),
            P("section", "fsdp", None),
            P("section", "fsdp"),
            P("section", "fsdp"),
            P("section", "fsdp", None),
            P("section", "fsdp"),
            P("section", "fsdp"),
            P("section", "fsdp", None),
            P("section", "fsdp", None),
            P("section", "fsdp", None),
            P("section", "fsdp"),
        ),
        out_specs=(
            P("section", None, "fsdp", "ctx", None),
            P("section", None, "fsdp", "ctx", None),
            P("section", "fsdp"),
            P("section", "fsdp", None),
            P("section", "fsdp", None),
            P("section", "fsdp", None),
            P("section", "fsdp"),
            P("section", "fsdp"),
            P("section", "fsdp", None),
            P("section", "fsdp"),
            P("section", "fsdp"),
            P("section", "fsdp", None),
            P("section", "fsdp", None),
            P("section", "fsdp", None),
            P("section", "fsdp"),
        ),
        check_vma=False,
    )
```

```python
from functools import partial

import jax
import jax.numpy as jnp
from jax import lax
from jax.experimental import pallas as pl
from jax.experimental.pallas import tpu as pltpu
from jax.sharding import PartitionSpec as P

HD = 256
WINDOW = 512
EPS = 1e-06
LANES = 128
PARTS = 4
GAIN_ROWS = 32
QB = 128
F32 = jnp.float32
B16 = jnp.bfloat16
VMEM_LIMIT = 56 * 1024 * 1024
AXES = ("section", "fsdp", "ctx")


def rope_tables(offset):
    half_dim = HD // 2
    inv_freq = 10000.0 ** (-(jnp.arange(half_dim).astype(F32) * 2.0 / HD))
    angles = offset.astype(F32)[:, None] * inv_freq[None, :]
    return (jnp.cos(angles), jnp.sin(angles))


def layout_for(seq_lens, first_place, tok_count):
    seq_ends = jnp.cumsum(seq_lens)
    seq_starts = seq_ends - seq_lens
    places = first_place + jnp.arange(tok_count)
    segment = jnp.sum((places[:, None] >= seq_ends[None, :]).astype(jnp.int32), axis=1)
    labels = jnp.arange(seq_lens.shape[0])
    seg_hit = segment[:, None] == labels[None, :]
    start = jnp.sum(jnp.where(seg_hit, seq_starts[None, :], 0), axis=1)
    offset = places - start
    low = jnp.maximum(start, places - (WINDOW - 1)) - first_place + WINDOW
    return offset, low.astype(jnp.int32)


def dot(a, b):
    return lax.dot_general(a, b, (((1,), (0,)), ((), ())), preferred_element_type=F32)


def dot_nt(a, b):
    return lax.dot_general(a, b, (((1,), (1,)), ((), ())), preferred_element_type=F32)


def dot_tn(a, b):
    return lax.dot_general(a, b, (((0,), (0,)), ((), ())), preferred_element_type=F32)


def inv_rms(v):
    return lax.rsqrt(jnp.mean(v * v, axis=-1, keepdims=True) + EPS)


def rms_back(v, gain, grad):
    r = inv_rms(v)
    gg = grad * gain
    normed = v * r
    back = r * (gg - normed * jnp.mean(normed * gg, axis=-1, keepdims=True))
    return back, jnp.sum(grad * normed, axis=0, keepdims=True)


def rope(v, cos, sin):
    u, w = v[:, : HD // 2], v[:, HD // 2 :]
    return jnp.concatenate([u * cos - w * sin, w * cos + u * sin], axis=-1)


def rope_back(g, cos, sin):
    a, b = g[:, : HD // 2], g[:, HD // 2 :]
    return jnp.concatenate([a * cos + b * sin, b * cos - a * sin], axis=-1)


GELU_C = 0.7978845608028654
GELU_A = 0.044715


def gelu_parts(g):
    g2 = g * g
    t = jnp.tanh(GELU_C * g * (1.0 + GELU_A * g2))
    half = 0.5 * (1.0 + t)
    value = g * half
    slope = half + 0.5 * g * (1.0 - t * t) * (GELU_C * (1.0 + 3.0 * GELU_A * g2))
    return value, slope


def params(**kw):
    return pltpu.CompilerParams(vmem_limit_bytes=VMEM_LIMIT, **kw)


def cost(flops, nbytes):
    return pl.CostEstimate(flops=int(flops) * 400, bytes_accessed=int(nbytes), transcendentals=0)


def whole(shape):
    n = len(shape)
    return pl.BlockSpec(shape, lambda *i: (0,) * n)


def held_back(kernel, first, n):
    def body(*refs):
        kernel(*refs[:first], *refs[first + n :])

    return body


def sds(shape, dtype):
    return jax.ShapeDtypeStruct(shape, dtype)


def kv_kernel(x_ref, gd_ref, gh_ref, cos_ref, sin_ref, w_ref, a_ref, pre_ref, kv_ref):
    x = x_ref[...].astype(F32)
    a = (x * inv_rms(x) * gd_ref[0:1, :]).astype(B16)
    a_ref[...] = a
    both = dot(a, w_ref[...])
    pre = both[:, :HD]
    pre_ref[...] = pre.astype(B16)
    keys = rope(pre * inv_rms(pre) * gh_ref[1:2, :], cos_ref[...], sin_ref[...])
    kv_ref[:, :HD] = keys.astype(B16)
    kv_ref[:, HD:] = both[:, HD:].astype(B16)


def kv_call(layer, x, gd, gh, cos, sin, w_qkv):
    tok, width = x.shape
    q_width = w_qkv.shape[2] - 2 * HD
    return pl.pallas_call(
        kv_kernel,
        grid=(1,),
        in_specs=[
            whole(x.shape),
            whole(gd.shape),
            whole(gh.shape),
            whole(cos.shape),
            whole(sin.shape),
            pl.BlockSpec((None, width, 2 * HD), lambda j: (layer, 0, q_width // (2 * HD))),
        ],
        out_specs=[whole((tok, width)), whole((tok, HD)), whole((tok, 2 * HD))],
        out_shape=[sds((tok, width), B16), sds((tok, HD), B16), sds((tok, 2 * HD), B16)],
        compiler_params=params(),
        cost_estimate=cost(4 * tok * width * HD, 4e6),
        name="keys_values",
    )(x, gd, gh, cos, sin, w_qkv)


def q_kernel(a_ref, gh_ref, cos_ref, sin_ref, w_ref, pre_ref, q_ref):
    pre = dot(a_ref[...], w_ref[...])
    pre_ref[...] = pre.astype(B16)
    q_ref[...] = rope(pre * inv_rms(pre) * gh_ref[0:1, :], cos_ref[...], sin_ref[...]).astype(B16)


def q_call(layer, a, gh, cos, sin, w_qkv):
    tok, width = a.shape
    q_width = w_qkv.shape[2] - 2 * HD
    block = pl.BlockSpec((tok, HD), lambda j: (0, j))
    return pl.pallas_call(
        q_kernel,
        grid=(q_width // HD,),
        in_specs=[
            whole(a.shape),
            whole(gh.shape),
            whole(cos.shape),
            whole(sin.shape),
            pl.BlockSpec((None, width, HD), lambda j: (layer, 0, j)),
        ],
        out_specs=[block, block],
        out_shape=[sds((tok, q_width), B16), sds((tok, q_width), B16)],
        compiler_params=params(),
        cost_estimate=cost(2 * tok * width * q_width, 5e6),
        name="queries",
    )(a, gh, cos, sin, w_qkv)


SCORE_SCALE = HD ** (-0.5)


def attn_kernel(q_ref, far_ref, near_ref, low_ref, o_ref, kv_scr):
    b = pl.program_id(0)

    @pl.when(b == 0)
    def _():
        kv_scr[:WINDOW, :] = far_ref[...]
        kv_scr[WINDOW:, :] = near_ref[...]

    span = WINDOW + QB
    first = pl.multiple_of(b * QB, QB)
    keys = kv_scr[pl.ds(first, span), :HD]
    vals = kv_scr[pl.ds(first, span), HD:]
    col = lax.broadcasted_iota(jnp.int32, (QB, span), 1)
    row = lax.broadcasted_iota(jnp.int32, (QB, span), 0)
    allowed = (col >= low_ref[...] - b * QB) & (col <= row + WINDOW)
    for h in range(q_ref.shape[1] // HD):
        scores = dot_nt(q_ref[:, h * HD : (h + 1) * HD], keys) * SCORE_SCALE
        e = jnp.where(allowed, jnp.exp(scores), 0.0)
        total = jnp.sum(e, axis=1, keepdims=True)
        o_ref[:, h * HD : (h + 1) * HD] = (dot(e.astype(B16), vals) / total).astype(B16)


def attn_call(q, far, near, low, *deps):
    tok, q_width = q.shape
    return pl.pallas_call(
        held_back(attn_kernel, 4, len(deps)),
        grid=(tok // QB,),
        in_specs=[
            pl.BlockSpec((QB, q_width), lambda b: (b, 0)),
            whole(far.shape),
            whole(near.shape),
            pl.BlockSpec((QB, 1), lambda b: (b, 0)),
        ]
        + [pl.BlockSpec(memory_space=pl.ANY)] * len(deps),
        out_specs=pl.BlockSpec((QB, q_width), lambda b: (b, 0)),
        out_shape=sds((tok, q_width), B16),
        scratch_shapes=[pltpu.VMEM((WINDOW + tok, 2 * HD), B16)],
        compiler_params=params(),
        cost_estimate=cost(4 * tok * q_width * (WINDOW + QB), 3e6),
        name="attend",
    )(q, far, near, low, *deps)


FC = 512


def ffn_kernel(
    o_ref, x_ref, gd_ref, wo_ref, wg_ref, wu_ref, wd_ref,
    y_ref, h_ref, g_ref, u_ref, z_ref, out_ref, b_scr,
):
    j = pl.program_id(0)

    @pl.when(j == 0)
    def _():
        y = dot(o_ref[...], wo_ref[...])
        y_ref[...] = y
        h = x_ref[...].astype(F32) + y * inv_rms(y) * gd_ref[1:2, :]
        h_ref[...] = h
        b_scr[...] = (h * inv_rms(h) * gd_ref[2:3, :]).astype(B16)

    b = b_scr[...]
    g = dot(b, wg_ref[...])
    u = dot(b, wu_ref[...])
    g_ref[...] = g.astype(B16)
    u_ref[...] = u.astype(B16)
    value = g * 0.5 * (1.0 + jnp.tanh(GELU_C * g * (1.0 + GELU_A * g * g)))
    z = dot((value * u).astype(B16), wd_ref[...])

    @pl.when(j == 0)
    def _():
        z_ref[...] = z

    @pl.when(j > 0)
    def _():
        z_ref[...] += z

    @pl.when(j == pl.num_programs(0) - 1)
    def _():
        zz = z_ref[...]
        out_ref[...] = (h_ref[...] + zz * inv_rms(zz) * gd_ref[3:4, :]).astype(B16)


def ffn_call(o, x, gd, w_out, w_gate, w_up, w_down, *deps):
    tok, width = x.shape
    ff = w_gate.shape[1]
    cols = pl.BlockSpec((tok, FC), lambda j: (0, j))
    tw = whole((tok, width))
    return pl.pallas_call(
        held_back(ffn_kernel, 7, len(deps)),
        grid=(ff // FC,),
        in_specs=[
            whole(o.shape),
            tw,
            whole(gd.shape),
            whole(w_out.shape),
            pl.BlockSpec((width, FC), lambda j: (0, j)),
            pl.BlockSpec((width, FC), lambda j: (0, j)),
            pl.BlockSpec((FC, width), lambda j: (j, 0)),
        ]
        + [pl.BlockSpec(memory_space=pl.ANY)] * len(deps),
        out_specs=[tw, tw, cols, cols, tw, tw],
        out_shape=[
            sds((tok, width), F32),
            sds((tok, width), F32),
            sds((tok, ff), B16),
            sds((tok, ff), B16),
            sds((tok, width), F32),
            sds((tok, width), B16),
        ],
        scratch_shapes=[pltpu.VMEM((tok, width), B16)],
        compiler_params=params(),
        cost_estimate=cost(2 * tok * width * (o.shape[1] + 3 * ff), 22e6),
        name="feed_forward",
    )(o, x, gd, w_out, w_gate, w_up, w_down, *deps)


def ffn_back_kernel(
    spot, c_ref, z_ref, h_ref, y_ref, o_ref, gd_ref, g_ref, u_ref, wo_ref, wg_ref, wu_ref, wd_ref,
    keep_ref, send_ref, dh_ref, do_ref, gg_ref, dz_scr, bt_scr, db_scr,
):
    j = pl.program_id(0)
    half = keep_ref.shape[2]

    def put(blocks):
        for section in range(2):

            @pl.when(spot[2] == section)
            def _():
                for c_part, p, row, block in blocks:
                    ref = keep_ref if row // half == section else send_ref
                    ref[c_part, p, pl.ds(row % half, block.shape[0]), :] = block

    tok, width = c_ref.shape
    part = width // PARTS
    n_gate = PARTS * part
    n_down = (width // LANES) * (FC // PARTS)
    out_rows = o_ref.shape[1] // (PARTS * PARTS)

    @pl.when(j == 0)
    def _():
        dz, post_grad = rms_back(z_ref[...], gd_ref[3:4, :], c_ref[...].astype(F32))
        dz_scr[...] = dz.astype(B16)
        gg_ref[...] = jnp.zeros(gg_ref.shape, F32)
        gg_ref[3:4, :] = post_grad
        h = h_ref[...]
        bt_scr[...] = (h * inv_rms(h) * gd_ref[2:3, :]).T.astype(B16)
        db_scr[...] = jnp.zeros(db_scr.shape, F32)

    dz = dz_scr[...]
    df = dot_nt(dz, wd_ref[...])
    value, slope = gelu_parts(g_ref[...].astype(F32))
    u = u_ref[...].astype(F32)
    f = (value * u).astype(B16)
    du = (df * value).astype(B16)
    dg = (df * u * slope).astype(B16)
    db_scr[...] += dot_nt(dg, wg_ref[...]) + dot_nt(du, wu_ref[...])
    bt = bt_scr[...]
    blocks = []
    for first, term in ((0, dg), (n_gate, du)):
        grad = dot(bt, term).astype(B16)
        for p in range(PARTS):
            for t in range(FC // LANES):
                block = grad[p * part : (p + 1) * part, t * LANES : (t + 1) * LANES]
                blocks.append((j, p, first + t * part, block))
    grad = dot_tn(f, dz).astype(B16)
    rows = FC // PARTS
    for p in range(PARTS):
        for t in range(width // LANES):
            block = grad[p * rows : (p + 1) * rows, t * LANES : (t + 1) * LANES]
            blocks.append((p, j, 2 * n_gate + t * rows, block))
    put(blocks)

    @pl.when(j == pl.num_programs(0) - 1)
    def _():
        add, ffn_grad = rms_back(h_ref[...], gd_ref[2:3, :], db_scr[...])
        dh = c_ref[...].astype(F32) + add
        dh_ref[...] = dh
        dy32, attn_grad = rms_back(y_ref[...], gd_ref[1:2, :], dh)
        dy = dy32.astype(B16)
        gg_ref[1:2, :] = attn_grad
        gg_ref[2:3, :] = ffn_grad
        do_ref[...] = dot_nt(dy, wo_ref[...]).astype(B16)
        og = dot_tn(o_ref[...], dy).astype(B16)
        out_blocks = []
        for f_part in range(PARTS):
            for p in range(PARTS):
                at = (f_part * PARTS + p) * out_rows
                for t in range(width // LANES):
                    block = og[at : at + out_rows, t * LANES : (t + 1) * LANES]
                    out_blocks.append((p, f_part, 2 * n_gate + n_down + t * out_rows, block))
        put(out_blocks)


def pack_rows(width, ff, q_width):
    gate = width // PARTS * (ff // PARTS // LANES)
    down = ff // (PARTS * PARTS) * (width // LANES)
    out = q_width // (PARTS * PARTS) * (width // LANES)
    return gate, down, out


def ffn_back_call(spot, c, z, h, y, o, gd, g, u, w_out, w_gate, w_up, w_down):
    tok, width = c.shape
    ff = w_gate.shape[1]
    q_width = o.shape[1]
    gate, down, out = pack_rows(width, ff, q_width)
    pack_shape = (PARTS, PARTS, (2 * gate + down + out) // 2, LANES)
    cols = pl.BlockSpec((tok, FC), lambda j, *_: (0, j))
    tw = whole((tok, width))
    return pl.pallas_call(
        ffn_back_kernel,
        grid_spec=pltpu.PrefetchScalarGridSpec(
            num_scalar_prefetch=1,
            grid=(ff // FC,),
            in_specs=[
                tw,
                tw,
                tw,
                tw,
                whole(o.shape),
                whole(gd.shape),
                cols,
                cols,
                whole(w_out.shape),
                pl.BlockSpec((width, FC), lambda j, *_: (0, j)),
                pl.BlockSpec((width, FC), lambda j, *_: (0, j)),
                pl.BlockSpec((FC, width), lambda j, *_: (j, 0)),
            ],
            out_specs=[whole(pack_shape), whole(pack_shape), tw, whole(o.shape), whole(gd.shape)],
            scratch_shapes=[
                pltpu.VMEM((tok, width), B16),
                pltpu.VMEM((width, tok), B16),
                pltpu.VMEM((tok, width), F32),
            ],
        ),
        out_shape=[
            sds(pack_shape, B16),
            sds(pack_shape, B16),
            sds((tok, width), F32),
            sds(o.shape, B16),
            sds(gd.shape, F32),
        ],
        compiler_params=params(),
        cost_estimate=cost(4 * tok * width * (q_width + 3 * ff), 35e6),
        name="feed_forward_back",
    )(spot, c, z, h, y, o, gd, g, u, w_out, w_gate, w_up, w_down)


def attn_back_kernel(
    q_ref, do_ref, qpre_ref, far_ref, near_ref, low_ref, gh_ref, cos_ref, sin_ref,
    dq_ref, dfar_ref, dnear_ref, gg_ref, kv_scr, dkv_scr,
):
    b = pl.program_id(0)

    @pl.when(b == 0)
    def _():
        kv_scr[:WINDOW, :] = far_ref[...]
        kv_scr[WINDOW:, :] = near_ref[...]
        dkv_scr[...] = jnp.zeros(dkv_scr.shape, F32)
        gg_ref[...] = jnp.zeros(gg_ref.shape, F32)

    span = WINDOW + QB
    first = pl.multiple_of(b * QB, QB)
    keys = kv_scr[pl.ds(first, span), :HD]
    vals = kv_scr[pl.ds(first, span), HD:]
    col = lax.broadcasted_iota(jnp.int32, (span, QB), 0)
    row = lax.broadcasted_iota(jnp.int32, (span, QB), 1)
    allowed = (col >= low_ref[...] - b * QB) & (col <= row + WINDOW)
    cos, sin = cos_ref[...], sin_ref[...]
    dkeys = jnp.zeros((span, HD), F32)
    dvals = jnp.zeros((span, HD), F32)
    gain_grad = jnp.zeros((1, HD), F32)
    for h in range(q_ref.shape[1] // HD):
        at = slice(h * HD, (h + 1) * HD)
        q = q_ref[:, at]
        do = do_ref[:, at]
        scores = dot_nt(keys, q) * SCORE_SCALE
        e = jnp.where(allowed, jnp.exp(scores), 0.0)
        p = e * (1.0 / jnp.sum(e, axis=0, keepdims=True))
        dp = dot_nt(vals, do)
        inner = jnp.sum(p * dp, axis=0, keepdims=True)
        ds = (p * (dp - inner)).astype(B16)
        dvals += dot(p.astype(B16), do)
        dkeys += dot(ds, q)
        dq = dot_tn(ds, keys) * SCORE_SCALE
        dq0, gain = rms_back(qpre_ref[:, at].astype(F32), gh_ref[0:1, :], rope_back(dq, cos, sin))
        gain_grad += gain
        dq_ref[:, at] = dq0.astype(B16)
    dkv_scr[pl.ds(first, span), :HD] += dkeys * SCORE_SCALE
    dkv_scr[pl.ds(first, span), HD:] += dvals
    gg_ref[0:1, :] += gain_grad

    @pl.when(b == pl.num_programs(0) - 1)
    def _():
        dfar_ref[...] = dkv_scr[:WINDOW, :].astype(B16)
        dnear_ref[...] = dkv_scr[WINDOW:, :]


def attn_back_call(q, do, qpre, far, near, low_row, gh, cos, sin, *deps):
    tok, q_width = q.shape
    block = pl.BlockSpec((QB, q_width), lambda b: (b, 0))
    table = pl.BlockSpec((QB, HD // 2), lambda b: (b, 0))
    return pl.pallas_call(
        held_back(attn_back_kernel, 9, len(deps)),
        grid=(tok // QB,),
        in_specs=[
            block,
            block,
            block,
            whole(far.shape),
            whole(near.shape),
            pl.BlockSpec((1, QB), lambda b: (0, b)),
            whole(gh.shape),
            table,
            table,
        ]
        + [pl.BlockSpec(memory_space=pl.ANY)] * len(deps),
        out_specs=[block, whole(far.shape), whole(near.shape), whole(gh.shape)],
        out_shape=[
            sds(q.shape, B16),
            sds(far.shape, B16),
            sds(near.shape, F32),
            sds(gh.shape, F32),
        ],
        scratch_shapes=[
            pltpu.VMEM((WINDOW + tok, 2 * HD), B16),
            pltpu.VMEM((WINDOW + tok, 2 * HD), F32),
        ],
        compiler_params=params(),
        cost_estimate=cost(10 * tok * q_width * (WINDOW + QB), 8e6),
        name="attend_back",
    )(q, do, qpre, far, near, low_row, gh, cos, sin, *deps)


def q_back_kernel(a_ref, dq_ref, w_ref, wq_grad_ref, da_ref):
    dq = dq_ref[...]
    wq_grad_ref[...] = dot_tn(a_ref[...], dq).astype(B16)
    da_ref[...] = dot_nt(dq, w_ref[...])


def q_back_call(layer, a, dq, w_qkv, *deps):
    tok, width = a.shape
    q_width = dq.shape[1]
    return pl.pallas_call(
        held_back(q_back_kernel, 3, len(deps)),
        grid=(1,),
        in_specs=[
            whole(a.shape),
            whole(dq.shape),
            pl.BlockSpec((None, width, q_width), lambda j: (layer, 0, 0)),
        ]
        + [pl.BlockSpec(memory_space=pl.ANY)] * len(deps),
        out_specs=[whole((width, q_width)), whole((tok, width))],
        out_shape=[sds((width, q_width), B16), sds((tok, width), F32)],
        compiler_params=params(),
        cost_estimate=cost(4 * tok * width * q_width, 6e6),
        name="queries_back",
    )(a, dq, w_qkv, *deps)


def kv_back_kernel(
    a_ref, x_ref, dh_ref, da_ref, dnear_ref, dback_ref, kpre_ref, gd_ref, gh_ref,
    cos_ref, sin_ref, w_ref, wq_ref, gd_part_ref, gh_part_ref, pack_ref, dx_ref,
):
    width = x_ref.shape[1]
    part = width // PARTS
    dkv = dnear_ref[...]
    tail = dback_ref[...].astype(F32)
    dkv = dkv + tail
    dk0, k_grad = rms_back(
        kpre_ref[...].astype(F32),
        gh_ref[1:2, :],
        rope_back(dkv[:, :HD], cos_ref[...], sin_ref[...]),
    )
    both = jnp.concatenate([dk0.astype(B16), dkv[:, HD:].astype(B16)], axis=1)
    kv_grad = dot_tn(a_ref[...], both).astype(B16)
    da = da_ref[...] + dot_nt(both, w_ref[...])
    add, in_grad = rms_back(x_ref[...].astype(F32), gd_ref[0:1, :], da)
    dx_ref[...] = (dh_ref[...] + add).astype(B16)
    gains = [in_grad] + [gd_part_ref[i : i + 1, :] for i in range(1, 4)]
    gains += [gh_part_ref[0:1, :], k_grad]
    lines = [g[:, t : t + LANES] for g in gains for t in range(0, g.shape[1], LANES)]
    n = len(lines) // PARTS
    blank = jnp.zeros((GAIN_ROWS - n, LANES), F32)
    for c_part in range(PARTS):
        block = jnp.concatenate(lines[c_part * n : (c_part + 1) * n] + [blank]).astype(B16)
        for p in range(PARTS):
            pack_ref[c_part, p, pack_ref.shape[2] - GAIN_ROWS :, :] = block
    q_tiles = wq_ref.shape[1] // LANES
    tiles = q_tiles + 2 * HD // LANES
    each = tiles // PARTS
    for t in range(tiles):
        c_part, slot = t // each, t % each
        for p in range(PARTS):
            rows = slice(p * part, (p + 1) * part)
            if t < q_tiles:
                piece = wq_ref[rows, t * LANES : (t + 1) * LANES]
            else:
                piece = kv_grad[rows, (t - q_tiles) * LANES : (t - q_tiles + 1) * LANES]
            pack_ref[c_part, p, slot * part : (slot + 1) * part, :] = piece


def kv_back_call(
    layer, a, x, dh, da, dnear, dback, kpre, gd, gh, cos, sin, w_qkv, wq_grad, gd_part, gh_part,
    *deps,
):
    tok, width = a.shape
    q_width = wq_grad.shape[1]
    part = width // PARTS
    rows = part * ((q_width + 2 * HD) // LANES // PARTS) + GAIN_ROWS
    pack_shape = (PARTS, PARTS, rows, LANES)
    tw = whole((tok, width))
    return pl.pallas_call(
        held_back(kv_back_kernel, 15, len(deps)),
        grid=(1,),
        in_specs=[
            tw,
            tw,
            tw,
            tw,
            whole(dnear.shape),
            whole(dback.shape),
            whole(kpre.shape),
            whole(gd.shape),
            whole(gh.shape),
            whole(cos.shape),
            whole(sin.shape),
            pl.BlockSpec((None, width, 2 * HD), lambda j: (layer, 0, q_width // (2 * HD))),
            whole(wq_grad.shape),
            whole(gd.shape),
            whole(gh.shape),
        ]
        + [pl.BlockSpec(memory_space=pl.ANY)] * len(deps),
        out_specs=[whole(pack_shape), tw],
        out_shape=[sds(pack_shape, B16), sds((tok, width), B16)],
        compiler_params=params(),
        cost_estimate=cost(8 * tok * width * HD, 10e6),
        name="keys_values_back",
    )(a, x, dh, da, dnear, dback, kpre, gd, gh, cos, sin, w_qkv, wq_grad, gd_part, gh_part, *deps)


def pack_qkv_kernel(spot, q_ref, k_ref, v_ref, gain_ref, dep_ref, all_ref, own_ref):
    part = q_ref.shape[0]
    refs = [(r, t) for r in (q_ref, k_ref, v_ref) for t in range(r.shape[1] // LANES)]
    each = len(refs) // PARTS
    for n, (ref, t) in enumerate(refs):
        rows = slice(n % each * part, (n % each + 1) * part)
        all_ref[n // each, rows, :] = ref[:, t * LANES : (t + 1) * LANES]
    for c_part in range(PARTS):
        all_ref[c_part, each * part :, :] = gain_ref[...]
    own_ref[0] = all_ref[spot[0]]


def pack_qkv(spot, query, key, value, gains, dep):
    weights = (query, key, value)
    rows = sum(w.shape[2] for w in weights) // PARTS // LANES * query.shape[1] + GAIN_ROWS
    return pl.pallas_call(
        pack_qkv_kernel,
        grid_spec=pltpu.PrefetchScalarGridSpec(
            num_scalar_prefetch=1,
            grid=(1,),
            in_specs=[
                pl.BlockSpec((None,) + w.shape[1:], lambda i, spot: (0, 0, 0)) for w in weights
            ]
            + [whole(gains.shape), pl.BlockSpec(memory_space=pl.ANY)],
            out_specs=[whole((PARTS, rows, LANES)), whole((1, rows, LANES))],
        ),
        out_shape=[sds((PARTS, rows, LANES), B16), sds((1, rows, LANES), B16)],
        compiler_params=params(),
        cost_estimate=cost(0, 2e6),
        name="pack_qkv",
    )(spot, *weights, gains, dep)


def pack_ffn_kernel(gate_ref, up_ref, down_ref, out_ref, all_ref):
    at = 0
    for ref in (gate_ref, up_ref, down_ref, out_ref):
        rows = ref.shape[0]
        for t in range(ref.shape[1] // LANES):
            all_ref[at : at + rows, :] = ref[:, t * LANES : (t + 1) * LANES]
            at += rows


def pack_ffn(gate, up, down, out):
    by_cols = pl.BlockSpec(
        (None, gate.shape[1], gate.shape[2] // PARTS), lambda i: (0, 0, i)
    )

    def by_rows(w):
        return pl.BlockSpec((None, w.shape[1] // PARTS, w.shape[2]), lambda i: (0, i, 0))

    rows = sum(w.size for w in (gate, up, down, out)) // PARTS // LANES
    return pl.pallas_call(
        pack_ffn_kernel,
        grid=(PARTS,),
        in_specs=[by_cols, by_cols, by_rows(down), by_rows(out)],
        out_specs=pl.BlockSpec((None, rows, LANES), lambda i: (i, 0, 0)),
        out_shape=sds((PARTS, rows, LANES), B16),
        compiler_params=params(),
        cost_estimate=cost(0, 5e6),
        name="pack_ffn",
    )(gate, up, down, out)


def half_quarter_kernel(layer, spot, own_ref, other_ref, *refs):
    mine = spot[2] == layer

    @pl.when(mine)
    def _():
        refs[-1][...] = own_ref[...]

    @pl.when(jnp.logical_not(mine))
    def _():
        refs[-1][...] = other_ref[...]


def half_quarter(layer, spot, own, other, *deps):
    shape = (1, own.shape[1] // 2, LANES)
    block = pl.BlockSpec(shape, lambda i, spot: (spot[0], spot[2], 0))
    return pl.pallas_call(
        partial(half_quarter_kernel, layer),
        grid_spec=pltpu.PrefetchScalarGridSpec(
            num_scalar_prefetch=1,
            grid=(1,),
            in_specs=[block, block] + [pl.BlockSpec(memory_space=pl.ANY)] * len(deps),
            out_specs=pl.BlockSpec(shape, lambda i, spot: (0, 0, 0)),
        ),
        out_shape=sds(shape, B16),
        compiler_params=params(),
        cost_estimate=cost(0, 1e6),
        name="half_quarter",
    )(spot, own, other, *deps)


def joined(parts, *deps):
    parts = [p if isinstance(p, tuple) else (p, 0, p.shape[1]) for p in parts]
    counts = [p[0].shape[0] for p in parts]

    def body(*refs):
        at = 0
        for (array, low, high), ref in zip(parts, refs):
            refs[-1][at : at + array.shape[0]] = ref[:, low:high, :]
            at += array.shape[0]

    shape = (sum(counts), parts[0][2] - parts[0][1], LANES)
    return pl.pallas_call(
        body,
        in_specs=[pl.BlockSpec(memory_space=pltpu.VMEM)] * len(parts)
        + [pl.BlockSpec(memory_space=pl.ANY)] * len(deps),
        out_specs=pl.BlockSpec(memory_space=pltpu.VMEM),
        out_shape=sds(shape, B16),
        compiler_params=params(),
        cost_estimate=cost(0, 4 * shape[0] * shape[1] * LANES),
        name="joined",
    )(*[p[0] for p in parts], *deps)


def place_qkv_kernel(spot, own_ref, other_ref, w_ref, gain_ref):
    part = w_ref.shape[0] // PARTS
    each = w_ref.shape[1] // LANES // PARTS

    def take(ref):
        for c_part in range(PARTS):
            e = spot[0] ^ c_part
            for p in range(PARTS):
                d = spot[1] ^ p
                at = jnp.where(d == 0, c_part, PARTS + (PARTS - 1) * e + d - 1)
                for t in range(each):
                    lane = (c_part * each + t) * LANES
                    w_ref[p * part : (p + 1) * part, lane : lane + LANES] = ref[
                        at, t * part : (t + 1) * part, :
                    ]
                if c_part == 0:
                    gain_ref[p] = ref[at, ref.shape[1] - GAIN_ROWS :, :]

    pl.when(pl.program_id(0) == 0)(lambda: take(own_ref))
    pl.when(pl.program_id(0) == 1)(lambda: take(other_ref))


def place_qkv(spot, own, other, width, cols):
    everything = pl.BlockSpec(own.shape, lambda i, spot: (0, 0, 0))
    return pl.pallas_call(
        place_qkv_kernel,
        grid_spec=pltpu.PrefetchScalarGridSpec(
            num_scalar_prefetch=1,
            grid=(2,),
            in_specs=[everything, everything],
            out_specs=[
                pl.BlockSpec((None, width, cols), lambda i, spot: (spot[2] ^ i, 0, 0)),
                pl.BlockSpec(
                    (None, PARTS, GAIN_ROWS, LANES), lambda i, spot: (spot[2] ^ i, 0, 0, 0)
                ),
            ],
        ),
        out_shape=[sds((2, width, cols), B16), sds((2, PARTS, GAIN_ROWS, LANES), B16)],
        compiler_params=params(),
        cost_estimate=cost(0, 8e6),
        name="place_qkv",
    )(spot, own, other)


def place_ffn_kernel(
    layer, spot, own_ref, other_ref, near_ref, far_ref, got_near_ref, got_far_ref,
    gate_ref, up_ref, down_ref, out_ref, pieces, sems,
):
    step = pl.program_id(0)
    section = spot[2]
    last = PARTS * PARTS - PARTS + 1
    shard = pieces.at[:PARTS]
    copies = [
        pltpu.make_async_copy(near_ref, pieces.at[PARTS:last, section], sems.at[1]),
        pltpu.make_async_copy(got_near_ref, pieces.at[PARTS:last, 1 - section], sems.at[2]),
        pltpu.make_async_copy(far_ref, pieces.at[last:, section], sems.at[3]),
        pltpu.make_async_copy(got_far_ref, pieces.at[last:, 1 - section], sems.at[4]),
    ]

    def shard_copy(do):
        pl.when(section == layer)(lambda: do(pltpu.make_async_copy(own_ref, shard, sems.at[0])))
        pl.when(section != layer)(lambda: do(pltpu.make_async_copy(other_ref, shard, sems.at[0])))

    @pl.when(step == 0)
    def _():
        shard_copy(lambda copy: copy.start())
        for copy in copies:
            copy.start()
        shard_copy(lambda copy: copy.wait())
        copies[0].wait()
        copies[1].wait()

    @pl.when(step == PARTS - 1)
    def _():
        copies[2].wait()
        copies[3].wait()

    width, cols = gate_ref.shape
    part = width // PARTS
    half = pieces.shape[2]
    c_part = spot[0] ^ step
    for p in range(PARTS):
        d = spot[1] ^ p
        index = jnp.where(d == 0, c_part, PARTS + (PARTS - 1) * step + d - 1)

        def piece(at, n):
            return pieces[index, at // half, at % half : at % half + n, :]

        at = 0
        for w_ref in (gate_ref, up_ref):
            for t in range(cols // LANES):
                w_ref[p * part : (p + 1) * part, t * LANES : (t + 1) * LANES] = piece(at, part)
                at += part
        for w_ref in (down_ref, out_ref):
            rows = w_ref.shape[2]
            for t in range(width // LANES):
                w_ref[p, 0, :, t * LANES : (t + 1) * LANES] = piece(at, rows)
                at += rows


def place_ffn(layer, spot, own, other, pieces, width, ff, q_width):
    cols = pl.BlockSpec((width, ff // PARTS), lambda i, spot: (0, spot[0] ^ i))

    def rows(n):
        return pl.BlockSpec(
            (PARTS, 1, n // PARTS**2, width), lambda i, spot: (0, spot[0] ^ i, 0, 0)
        )

    half = own.shape[1] // 2
    shard = (PARTS, 2, half, LANES)
    gate, up, down, out = pl.pallas_call(
        partial(place_ffn_kernel, layer),
        grid_spec=pltpu.PrefetchScalarGridSpec(
            num_scalar_prefetch=1,
            grid=(PARTS,),
            in_specs=[pl.BlockSpec(memory_space=pl.ANY)] * 6,
            out_specs=[cols, cols, rows(ff), rows(q_width)],
            scratch_shapes=[
                pltpu.VMEM((PARTS * PARTS, 2, half, LANES), B16),
                pltpu.SemaphoreType.DMA((5,)),
            ],
        ),
        out_shape=[
            sds((width, ff), B16),
            sds((width, ff), B16),
            sds((PARTS, PARTS, ff // PARTS**2, width), B16),
            sds((PARTS, PARTS, q_width // PARTS**2, width), B16),
        ],
        compiler_params=params(),
        cost_estimate=cost(0, 18e6),
        name="place_ffn",
    )(spot, own.reshape(shard), other.reshape(shard), *pieces)
    return gate, up, down.reshape(ff, width), out.reshape(q_width, width)


def add_split_kernel(spot, first_ref, second_ref, *refs):
    keep_a, send_a, keep_b, send_b = refs[-PARTS:]
    half = first_ref.shape[1] // 2
    a, b = slice(0, half), slice(half, 2 * half)
    for rows, far, out, n in (
        (a, 0, keep_a, 0), (a, 2, keep_a, 1), (a, 1, send_a, 0), (a, 3, send_a, 1),
        (b, 0, keep_b, 0), (b, 1, keep_b, 1), (b, 2, send_b, 0), (b, 3, send_b, 1),
    ):
        c_part = spot[0] ^ far
        total = first_ref[c_part, rows, :].astype(F32) + second_ref[c_part, rows, :].astype(F32)
        out[n] = total.astype(B16)


def add_split(spot, first, second, *deps):
    n = first.shape[2]
    block = pl.BlockSpec((PARTS, None, n, LANES), lambda i, spot: (0, i, 0, 0))
    out = pl.BlockSpec((2, None, n // 2, LANES), lambda i, spot: (0, i, 0, 0))
    return pl.pallas_call(
        add_split_kernel,
        grid_spec=pltpu.PrefetchScalarGridSpec(
            num_scalar_prefetch=1,
            grid=(PARTS,),
            in_specs=[block, block] + [pl.BlockSpec(memory_space=pl.ANY)] * len(deps),
            out_specs=[out] * PARTS,
        ),
        out_shape=[sds((2, PARTS, n // 2, LANES), B16)] * PARTS,
        compiler_params=params(),
        cost_estimate=cost(0, 3 * 2 * first.size),
        name="add_split",
    )(spot, first, second, *deps)


def add_pairs_kernel(a_ref, b_ref, c_ref, d_ref, *refs):
    refs[-2][...] = (a_ref[...].astype(F32) + b_ref[...].astype(F32)).astype(B16)
    refs[-1][...] = (c_ref[...].astype(F32) + d_ref[...].astype(F32)).astype(B16)


def add_pairs(a, b, c, d, *deps):
    shape = a.shape[1:]
    return pl.pallas_call(
        add_pairs_kernel,
        grid=(1,),
        in_specs=[pl.BlockSpec((None,) + shape, lambda i: (1, 0, 0, 0))] * 4
        + [pl.BlockSpec(memory_space=pl.ANY)] * len(deps),
        out_specs=[whole(shape)] * 2,
        out_shape=[sds(shape, B16)] * 2,
        compiler_params=params(),
        cost_estimate=cost(0, 6 * a.size),
        name="add_pairs",
    )(a, b, c, d, *deps)


def sum_pairs_kernel(spot, a0, a1, a2, b0, b1, b2, *refs):
    sum_parts_kernel(
        spot, a0, a1, a2, b0, b1, b2,
        refs[-2].at[0], refs[-1].at[0], refs[-2].at[1], refs[-1].at[1],
    )


def sum_parts_kernel(spot, a0, a1, a2, b0, b1, b2, *refs):
    outs = refs[-PARTS:]
    half = a0.shape[1]
    for d in range(PARTS):
        f = spot[1] ^ d
        for rows, terms in ((slice(0, half), (a0, a1, a2)), (slice(half, 2 * half), (b0, b1, b2))):
            total = sum(term[f].astype(F32) for term in terms)
            outs[d][rows, :] = total.astype(B16)


def sum_parts(spot, split, got, last, *deps, pairs=False):
    keep_a, _, keep_b, _ = split
    shape = keep_a.shape[1:]
    first = pl.BlockSpec((None,) + shape, lambda i, spot: (0, 0, 0, 0))
    one = whole(shape)
    out = ((2,) if pairs else ()) + (2 * shape[1], LANES)
    count = 2 if pairs else PARTS
    return pl.pallas_call(
        sum_pairs_kernel if pairs else sum_parts_kernel,
        grid_spec=pltpu.PrefetchScalarGridSpec(
            num_scalar_prefetch=1,
            grid=(1,),
            in_specs=[first, first, one] * 2 + [pl.BlockSpec(memory_space=pl.ANY)] * len(deps),
            out_specs=[whole(out)] * count,
        ),
        out_shape=[sds(out, B16)] * count,
        compiler_params=params(),
        cost_estimate=cost(0, 10 * keep_a.size),
        name="sum_parts",
    )(spot, keep_a, got[0], last[0], keep_b, got[1], last[1], *deps)


def choose_ring_kernel(spot, *refs):
    firsts, seconds, out_ref = refs[:PARTS], refs[PARTS : 2 * PARTS], refs[-1]
    rows = out_ref.shape[1]
    for e in range(PARTS):

        @pl.when(spot[2] == 0)
        def _():
            out_ref[e] = seconds[e][...]

        @pl.when(spot[2] == 1)
        def _():
            out_ref[e] = firsts[e][:rows, :]


def choose_ring(spot, firsts, seconds):
    shape = (PARTS,) + seconds[0].shape
    return pl.pallas_call(
        choose_ring_kernel,
        grid_spec=pltpu.PrefetchScalarGridSpec(
            num_scalar_prefetch=1,
            grid=(1,),
            in_specs=[whole(p.shape) for p in (*firsts, *seconds)],
            out_specs=whole(shape),
        ),
        out_shape=sds(shape, B16),
        compiler_params=params(),
        cost_estimate=cost(0, 4e6),
        name="choose_ring",
    )(spot, *firsts, *seconds)


def finish_kernel(spot, *refs):
    firsts, seconds, got_ref = refs[:PARTS], refs[PARTS : 2 * PARTS], refs[2 * PARTS]
    gate_ref, up_ref, down_ref, out_ref, q_ref, k_ref, v_ref, gain_ref, mine_ref = refs[
        2 * PARTS + 1 :
    ]
    places = [(ref, t) for ref in (q_ref, k_ref, v_ref) for t in range(ref.shape[1] // LANES)]
    n = len(places) // PARTS
    half = got_ref.shape[1]
    part = gate_ref.shape[0]
    for e in range(PARTS):

        @pl.when(pl.program_id(0) == e)
        def _():
            mine_ref[1 - spot[2]] = got_ref[e]
            for c_part in range(PARTS):

                @pl.when(spot[0] ^ e == c_part)
                def _():
                    for t in range(n):
                        ref, tile = places[c_part * n + t]
                        block = firsts[e][half + t * part : half + (t + 1) * part, :]
                        ref[:, tile * LANES : (tile + 1) * LANES] = block.astype(F32)

            gain_ref[...] = firsts[e][half + n * part :, :].astype(F32)

            @pl.when(spot[2] == 0)
            def _():
                mine_ref[0] = firsts[e][:half, :]

            @pl.when(spot[2] == 1)
            def _():
                mine_ref[1] = seconds[e][...]

    at = 0
    for ref in (gate_ref, up_ref, down_ref, out_ref):
        rows = ref.shape[0]
        for t in range(ref.shape[1] // LANES):
            block = mine_ref[at // half, at % half : at % half + rows, :]
            ref[:, t * LANES : (t + 1) * LANES] = block.astype(F32)
            at += rows


def finish(spot, firsts, seconds, got, width, ff, q_width):
    part, cols = width // PARTS, ff // PARTS

    def by_cols(n):
        return pl.BlockSpec((None, part, n), lambda i, spot: (0, 0, spot[0] ^ i))

    def by_rows(n):
        return pl.BlockSpec((None, n, width), lambda i, spot: (0, spot[0] ^ i, 0))

    return pl.pallas_call(
        finish_kernel,
        grid_spec=pltpu.PrefetchScalarGridSpec(
            num_scalar_prefetch=1,
            grid=(PARTS,),
            in_specs=[whole(p.shape) for p in (*firsts, *seconds, got)],
            out_specs=[
                by_cols(cols),
                by_cols(cols),
                by_rows(ff // PARTS**2),
                by_rows(q_width // PARTS**2),
                *[
                    pl.BlockSpec((None, part, n), lambda i, spot: (0, 0, 0))
                    for n in (q_width, HD, HD)
                ],
                pl.BlockSpec((None, GAIN_ROWS, LANES), lambda i, spot: (spot[0] ^ i, 0, 0)),
            ],
            scratch_shapes=[pltpu.VMEM((2,) + seconds[0].shape, B16)],
        ),
        out_shape=[
            sds((1, part, ff), F32),
            sds((1, part, ff), F32),
            sds((1, ff // PARTS, width), F32),
            sds((1, q_width // PARTS, width), F32),
            *[sds((1, part, n), F32) for n in (q_width, HD, HD)],
            sds((PARTS, GAIN_ROWS, LANES), F32),
        ],
        compiler_params=params(),
        cost_estimate=cost(0, 12e6),
        name="finish",
    )(spot, *firsts, *seconds, got)


def split_pack(pack, width, ff, q_width):
    gate, down, out = pack_rows(width, ff, q_width)
    part = width // PARTS

    def cols(p):
        tiles = p.shape[2] // part
        return (
            p.reshape(PARTS, PARTS, tiles, part, LANES)
            .transpose(1, 3, 0, 2, 4)
            .reshape(width, PARTS * tiles * LANES)
        )

    def rows(p):
        n = p.shape[2] // (width // LANES)
        return (
            p.reshape(PARTS, PARTS, width // LANES, n, LANES)
            .transpose(1, 0, 3, 2, 4)
            .reshape(PARTS * PARTS * n, width)
        )

    return (
        cols(pack[:, :, :gate]),
        cols(pack[:, :, gate : 2 * gate]),
        rows(pack[:, :, 2 * gate : 2 * gate + down]),
        rows(pack[:, :, 2 * gate + down :]),
    )


def moved(array, axis, far, layer=None):
    sizes = [lax.axis_size(name) for name in AXES]
    pairs = []
    for s in range(sizes[0]) if layer is None else [layer]:
        for f in range(sizes[1]):
            for c in range(sizes[2]):
                f2 = f ^ far if axis == "fsdp" else f
                c2 = c ^ far if axis == "ctx" else c
                pairs.append(
                    ((s * sizes[1] + f) * sizes[2] + c, (s * sizes[1] + f2) * sizes[2] + c2)
                )
    return lax.ppermute(array, AXES, pairs)


def swapped(array):
    return lax.ppermute(array, "section", [(0, 1), (1, 0)])


def passed_along(array, by):
    devices = lax.axis_size("ctx")
    pairs = [(i, i + by) for i in range(devices) if 0 <= i + by < devices]
    return lax.ppermute(array, "ctx", pairs)


FAR = range(1, PARTS)


def other_shards(quarter, layer=None):
    return [moved(quarter, "fsdp", d, layer) for d in FAR]


def at(array, index):
    return lax.dynamic_index_in_dim(array, index, 0, keepdims=False)


def near_quarters(shards, layer=None):
    return moved(shards, "ctx", 1, layer), moved(shards, "ctx", 2, layer)


def near_halves(near, *deps):
    one, two = near
    rows = one.shape[1]
    return joined([(one, 0, rows // 2)], *deps), joined([(two, rows // 2, rows)], *deps)


def far_quarter(halves):
    by_one = moved(halves[0], "ctx", 2)
    by_two = moved(halves[1], "ctx", 1)
    return jnp.concatenate([by_one, by_two], axis=1)


def ctx_near(split):
    return moved(split[1], "ctx", 1), moved(split[3], "ctx", 2)


def far_sends(split, got, *deps):
    keep_a, _, keep_b, _ = split
    return add_pairs(keep_a, got[0], keep_b, got[1], *deps)


def ctx_far(sends):
    send_a, send_b = sends
    return moved(send_a, "ctx", 2), moved(send_b, "ctx", 1)


def fsdp_summed(parts, layer=None):
    total = parts[0].astype(F32)
    for d in FAR:
        total += moved(parts[d], "fsdp", d, layer).astype(F32)
    return total.astype(B16)


def fsdp_summed_in_two(keep, send):
    got = moved(send, "fsdp", 1)

    def both(n):
        return keep[n].astype(F32) + got[n].astype(F32)

    last = moved(both(1).astype(B16), "fsdp", 2)
    return (both(0) + last.astype(F32)).astype(B16)


def ctx_ring(piece):
    return [piece] + [moved(piece, "ctx", e) for e in FAR]


def per_device(
    inputs,
    grad_out,
    lengths,
    in_gain,
    query_weight,
    key_weight,
    value_weight,
    query_gain,
    key_gain,
    out_weight,
    attn_gain,
    ffn_gain,
    gate_weight,
    up_weight,
    down_weight,
    post_gain,
):
    section = lax.axis_index("section")
    fsdp_index = lax.axis_index("fsdp")
    ctx_index = lax.axis_index("ctx")
    shards = lax.axis_size("fsdp")
    in_pieces = shards == PARTS and lax.axis_size("ctx") == PARTS
    tok = inputs.shape[2]
    width = inputs.shape[3]
    q_width = query_weight.shape[2]
    ff = gate_weight.shape[2]
    first_layer = section == 0

    qkv_own = jnp.concatenate([query_weight[0], key_weight[0], value_weight[0]], axis=1)
    gain_own = jnp.concatenate(
        [in_gain[0], attn_gain[0], ffn_gain[0], post_gain[0], query_gain[0], key_gain[0]]
    )

    def as_gains(raw):
        n, m = width // shards, HD // shards
        gd = [raw[:, i * n : (i + 1) * n].reshape(1, width) for i in range(4)]
        gh = [raw[:, 4 * n + i * m : 4 * n + (i + 1) * m].reshape(1, HD) for i in range(2)]
        gd = jnp.concatenate(gd + [jnp.zeros((4, width), raw.dtype)]).astype(F32)
        gh = jnp.concatenate(gh + [jnp.zeros((6, HD), raw.dtype)]).astype(F32)
        return gd, gh

    def own_row(array):
        return lax.dynamic_index_in_dim(array[:, 0], section, 0, keepdims=False)

    offset, low = layout_for(own_row(lengths), ctx_index * tok, tok)
    cos, sin = rope_tables(offset)
    low_col, low_row = low[:, None], low[None, :]

    spot = jnp.stack([ctx_index, fsdp_index, section]).astype(jnp.int32)
    if in_pieces:
        gain_rows = jnp.pad(gain_own, (0, GAIN_ROWS * LANES - gain_own.shape[0]))
        gain_rows = gain_rows.reshape(GAIN_ROWS, LANES)
        ffn_parts = pack_ffn(gate_weight, up_weight, down_weight, out_weight)
        ffn_other = swapped(ffn_parts)
        qkv_parts, quarter = pack_qkv(
            spot, query_weight, key_weight, value_weight, gain_rows, ffn_parts
        )

        def arriving(layer, *deps):
            own = half_quarter(layer, spot, ffn_parts, ffn_other, *deps)
            return own, other_shards(own)

        first_own, first_arriving = arriving(0)
        shards_in = joined(other_shards(quarter), first_own, *first_arriving[:2])
        near = near_quarters(shards_in)
        far = far_quarter(near_halves(near, first_arriving[2]))
        pieces = joined(
            [qkv_parts, shards_in, *near, far], *first_arriving, cos, sin, low_col
        )
        w_qkv, raw = place_qkv(spot, pieces, swapped(pieces), width, q_width + 2 * HD)
        raw = raw.reshape(2, PARTS, GAIN_ROWS * LANES)
        first_shards = joined(first_arriving, pieces)
        first_near = near_quarters(first_shards)
        _, second_arriving = arriving(1, first_shards)

        def other_half(shards, near, far):
            near = joined([shards, *near])
            return near, far, swapped(near), swapped(far)

        state = {}

        def before_attend(layer, q):
            if layer == 0:
                far = far_quarter(near_halves(first_near, q, *second_arriving))
                state["pieces"] = other_half(first_shards, first_near, far)
                return second_arriving
            far = far_quarter(state["halves"])
            state["pieces"] = other_half(*state["shards"], far)
            return (far,)

        def before_ffn(layer, o, gate):
            if layer == 1:
                return ()
            shards = joined(second_arriving, o)
            near = near_quarters(shards)
            state["shards"] = (shards, near)
            state["halves"] = near_halves(near, gate)
            return ()

        def place(layer):
            gate, up, down, out = place_ffn(
                layer, spot, ffn_parts, ffn_other, state["pieces"], width, ff, q_width
            )
            return out, gate, up, down

    else:

        def whole_weight(own):
            full = lax.all_gather(own, "fsdp", axis=0, tiled=True)
            return lax.all_gather(full, "section", axis=0)

        full = [
            whole_weight(w)
            for w in (qkv_own, out_weight[0], gate_weight[0], up_weight[0], down_weight[0])
        ]
        w_qkv = full[0]
        raw = whole_weight(gain_own[None])

        def place(layer):
            return tuple(w[layer] for w in full[1:])

        def before_attend(layer, q):
            return ()

        def before_ffn(layer, o, gate):
            return ()


    x = own_row(inputs)
    kept = []
    for layer in range(2):
        gd, gh = as_gains(raw[layer])
        a, kpre, near = kv_call(layer, x, gd, gh, cos, sin, w_qkv)
        far = passed_along(near, 1)
        qpre, q = q_call(layer, a, gh, cos, sin, w_qkv)
        o = attn_call(q, far, near, low_col, *before_attend(layer, q))
        weights = place(layer)
        y, h, g, u, z, result = ffn_call(o, x, gd, *weights, *before_ffn(layer, o, weights[1]))
        kept.append((x, a, kpre, near, far, qpre, q, o, y, h, g, u, z, result, gd, gh, weights))
        x = result

    spot_back = spot if in_pieces else jnp.zeros_like(spot)

    def layer_back(layer, cot, attn_deps, q_deps, kv_deps):
        x, a, kpre, near, far, qpre, q, o, y, h, g, u, z, result, gd, gh, weights = kept[layer]
        keep, send, dh, do, gd_part = ffn_back_call(spot_back, cot, z, h, y, o, gd, g, u, *weights)
        dq, dfar, dnear, gh_part = attn_back_call(
            q, do, qpre, far, near, low_row, gh, cos, sin, *attn_deps(keep, send)
        )
        dback = passed_along(dfar, -1)
        if tok > WINDOW:
            dback = jnp.pad(dback, ((tok - WINDOW, 0), (0, 0)))
        wq_grad, da = q_back_call(layer, a, dq, w_qkv, *q_deps(keep, send, dq))
        qkv_pack, dx = kv_back_call(
            layer, a, x, dh, da, dnear, dback, kpre, gd, gh, cos, sin, w_qkv, wq_grad,
            gd_part, gh_part, *kv_deps(),
        )
        return (keep, send), qkv_pack, dx

    cot = own_row(grad_out)
    if in_pieces:
        def split_second(keep, send, dq):
            state["split1"] = add_split(spot, keep, swapped(send))
            state["near1"] = ctx_near(state["split1"])
            return (state["split1"][0],)

        ffn_pack, qkv_pack, mid = layer_back(1, cot, lambda *_: (), split_second, lambda: ())

        def far_second(keep, send):
            sends = far_sends(state["split1"], state["near1"], keep)
            state["far1"] = ctx_far(sends)
            return (sends[0],)

        def split_first(keep, send, dq):
            state["split0"] = add_split(spot, keep, swapped(send), dq)
            state["near0"] = ctx_near(state["split0"])
            parts = sum_parts(
                spot, state["split1"], state["near1"], state["far1"], state["split0"][0], pairs=True
            )
            state["ffn1"] = fsdp_summed_in_two(*parts)
            return (parts[0],)

        def far_first():
            state["sends0"] = far_sends(state["split0"], state["near0"])
            return (state["sends0"][0],)

        first_ffn_pack, first_qkv_pack, grad_in = layer_back(
            0, mid, far_second, split_first, far_first
        )
    else:
        ffn_pack, qkv_pack, mid = layer_back(1, cot, *[lambda *_: ()] * 3)
        first_ffn_pack, first_qkv_pack, grad_in = layer_back(0, mid, *[lambda *_: ()] * 3)
    packs = [(first_ffn_pack, first_qkv_pack), (ffn_pack, qkv_pack)]
    in_grads = [grad_in, mid]

    mine = jnp.stack([kept[0][13], in_grads[0]])
    others = jnp.stack([kept[1][13], in_grads[1]])
    got = swapped(jnp.where(first_layer, others, mine))
    mine = jnp.where(first_layer, mine, others)
    activations, input_grads = [
        jnp.stack([jnp.where(first_layer, mine[n], got[n]), jnp.where(first_layer, got[n], mine[n])])
        for n in range(2)
    ]

    if in_pieces:
        keep = jnp.where(first_layer, first_qkv_pack, qkv_pack)
        qkv_split = add_split(spot, keep, swapped(jnp.where(first_layer, qkv_pack, first_qkv_pack)))
        seconds = ctx_ring(state["ffn1"])
        far0 = ctx_far(state["sends0"])
        ffn0 = fsdp_summed(sum_parts(spot, state["split0"], state["near0"], far0))
        qkv_near = ctx_near(qkv_split)
        qkv_far = ctx_far(far_sends(qkv_split, qkv_near))
        qkv_own = fsdp_summed(sum_parts(spot, qkv_split, qkv_near, qkv_far))
        firsts = ctx_ring(jnp.concatenate([ffn0, qkv_own]))
        got = swapped(choose_ring(spot, firsts, seconds))
        gate_g, up_g, down_g, out_g, q_g, k_g, v_g, gain_sums = finish(
            spot, firsts, seconds, got, width, ff, q_width
        )
        gain_sums = gain_sums[:, : (4 * width + 2 * HD) // LANES // PARTS].reshape(-1)
    else:
        sums = []
        gain_sums = []
        for halves, qkv_pack in packs:
            ffn_pack = jnp.concatenate(halves, axis=2)
            gate, up, down, out = split_pack(ffn_pack, width, ff, q_width)
            part = width // PARTS
            n = (4 * width + 2 * HD) // LANES // PARTS
            gain_sums.append(qkv_pack[:, 0, -GAIN_ROWS:][:, :n].reshape(-1))
            qkv_pack = qkv_pack[:, :, :-GAIN_ROWS]
            tiles = qkv_pack.shape[2] // part
            qkv = (
                qkv_pack.reshape(PARTS, PARTS, tiles, part, LANES)
                .transpose(1, 3, 0, 2, 4)
                .reshape(width, -1)
            )
            sums.append((gate, up, down, out, qkv))
        shard = [
            lax.psum_scatter(
                lax.psum_scatter(jnp.stack(pair), "section", scatter_dimension=0, tiled=True)[0],
                "fsdp",
                scatter_dimension=0,
                tiled=True,
            )
            for pair in zip(*sums)
        ]
        gate_g, up_g, down_g, out_g, qkv_g = (
            w.astype(F32)[None] for w in lax.psum(tuple(shard), "ctx")
        )
        q_g, k_g, v_g = jnp.split(qkv_g, [q_width, q_width + HD], axis=2)
        gain_sums = at(lax.psum(jnp.stack(gain_sums), AXES), section).astype(F32)

    def gain_shard(first, n):
        return lax.dynamic_slice_in_dim(gain_sums, first + fsdp_index * n, n, 0)[None]

    dn, hn = width // shards, HD // shards
    d_gains = [gain_shard(i * width, dn) for i in range(4)]
    h_gains = [gain_shard(4 * width + i * HD, hn) for i in range(2)]

    return (
        activations[None, :, None],
        input_grads[None, :, None],
        d_gains[0],
        q_g,
        k_g,
        v_g,
        h_gains[0],
        h_gains[1],
        out_g,
        d_gains[1],
        d_gains[2],
        gate_g,
        up_g,
        down_g,
        d_gains[3],
    )


def solution(mesh):
    return jax.shard_map(
        per_device,
        mesh=mesh,
        in_specs=(
            P(None, "fsdp", "ctx", None),
            P(None, "fsdp", "ctx", None),
            P(None, "fsdp", None),
            P("section", "fsdp"),
            P("section", "fsdp", None),
            P("section", "fsdp", None),
            P("section", "fsdp", None),
            P("section", "fsdp"),
            P("section", "fsdp"),
            P("section", "fsdp", None),
            P("section", "fsdp"),
            P("section", "fsdp"),
            P("section", "fsdp", None),
            P("section", "fsdp", None),
            P("section", "fsdp", None),
            P("section", "fsdp"),
        ),
        out_specs=(
            P("section", None, "fsdp", "ctx", None),
            P("section", None, "fsdp", "ctx", None),
            P("section", "fsdp"),
            P("section", "fsdp", None),
            P("section", "fsdp", None),
            P("section", "fsdp", None),
            P("section", "fsdp"),
            P("section", "fsdp"),
            P("section", "fsdp", None),
            P("section", "fsdp"),
            P("section", "fsdp"),
            P("section", "fsdp", None),
            P("section", "fsdp", None),
            P("section", "fsdp", None),
            P("section", "fsdp"),
        ),
        check_vma=False,
    )
```
